32 devices in a mesh: groups: 2 (over y), pool: 4 (over z), tensor: 4 (over x, core).
Axes of the slice: x: 2, y: 2, z: 4, core: 2. Of those that a mesh axis runs over, the one named last changes fastest.
Arguments:
- hidden: bfloat16 [1024, 4096], P(('groups', 'pool')), parts along dimension 0, may hold values from -6 to 6
- w_x: bfloat16 [4096, 4096], P(None, 'tensor'), may hold values from -0.09375 to 0.09375
- w_bc: bfloat16 [4096, 2048], P(None, 'tensor'), may hold values from -0.09375 to 0.09375
- w_dt: bfloat16 [4096, 64], P(None, 'tensor'), may hold values from -0.09375 to 0.09375
- conv_x: float32 [4, 4096], P(None, 'tensor'), may hold values from -3 to 3
- conv_bc: float32 [4, 2048], P(None, 'tensor'), may hold values from -3 to 3
- dt_bias: float32 [64], P('tensor'), may hold values from -4 to -1
- a_log: float32 [64], P('tensor'), may hold values from 0 to 2.77
- d_skip: float32 [64], P('tensor'), may hold values from 0.5 to 1.5
- norm_gain: float32 [4096], P('tensor'), may hold values from 0.5 to 1.5
- w_out: bfloat16 [4096, 4096], P('tensor'), may hold values from -0.09375 to 0.09375
- ssm_pool: bfloat16 [144, 64, 64, 128], P(('groups', 'pool'), 'tensor'), parts along dimension 0, may hold values from -0.59765625 to 0.59765625
- conv_pool_x: bfloat16 [144, 3, 4096], P(('groups', 'pool'), None, 'tensor'), parts along dimension 0, may hold values from -6 to 6
- conv_pool_bc: bfloat16 [144, 3, 2048], P(('groups', 'pool'), None, 'tensor'), parts along dimension 0, may hold values from -6 to 6
- owners: int32 [128], P('groups'), parts along dimension 0, may hold values from 0 to 3, as said below
- slots: int32 [128], P('groups'), parts along dimension 0, may hold values from 0 to 17, as said below
- accepted: int32 [128], P('groups'), parts along dimension 0, may hold values from 1 to 8
Outputs:
- mixed: bfloat16 [1024, 4096], P(('groups', 'pool'), 'tensor'), parts along dimension 0
- new_ssm_pool: bfloat16 [144, 64, 64, 128], P(('groups', 'pool'), 'tensor'), parts along dimension 0
- new_conv_x: bfloat16 [144, 3, 4096], P(('groups', 'pool'), None, 'tensor'), parts along dimension 0
- new_conv_bc: bfloat16 [144, 3, 2048], P(('groups', 'pool'), None, 'tensor'), parts along dimension 0
The draws below stay inside these ranges and needn't reach their ends.
There are 2 independent parts, one for each index of `groups`. The reference program is written for one: setup_inputs(seed, part) draws one part's arguments, and reference() takes and returns one part's arrays. A program takes and returns all parts, laid end to end along the dimension named above; an argument that names none is the same for every part. Nothing has to cross between parts.
Inputs may be any that keep to these rules, and one draw needn't show every extreme that they name: `owners`: of the requests of one pool index (aligned blocks of 16), at most 6 have their states on one pool index, and exactly 6 do for some pool index; every pool index holds the states of exactly 16 requests. `slots`: no two requests share an owner and a slot.
All inputs are finite; a program needn't handle non-finite values.
Results may differ from the reference program's by a relative error of at most 0.0071.
Values may be sent and summed in bfloat16 or wider, within the bound.
No kernel may reach another device: no remote copies, remote signals or barrier semaphores. Data moves between devices by JAX's collectives and lax.ppermute only.
A program may use at most 128 MiB of HBM per device.

```python
import jax
import jax.numpy as jnp
from jax import lax

D = 4096
HEADS = 64
HEAD_DIM = 64
STATE = 128
GROUPS = 8
KERNEL = 4
DRAFT = 8
REQ_DEV = 16
SLOT_DEV = 18
REQS = 64
TOKENS = 512
SLOTS = 72
N_POOL = 4


def assign_slots(key):
    share = REQ_DEV // N_POOL
    high_count = share + share // 2
    low_count = share - share // 2
    offsets = jnp.concatenate([jnp.zeros((high_count,), jnp.int32), jnp.ones((low_count,), jnp.int32), 2 + jnp.arange((N_POOL - 2) * share, dtype=jnp.int32) // share])
    shifts = jax.random.permutation(jax.random.fold_in(key, 11), N_POOL).astype(jnp.int32)
    order_key = jax.random.fold_in(key, 12)

    def per_requester(index):
        shuffled = jax.random.permutation(jax.random.fold_in(order_key, index), offsets)
        return (shuffled + shifts[index]) % N_POOL
    owner_ids = jax.vmap(per_requester)(jnp.arange(N_POOL, dtype=jnp.int32)).reshape(-1).astype(jnp.int32)
    onehot = (owner_ids[:, None] == jnp.arange(N_POOL, dtype=jnp.int32)[None, :]).astype(jnp.int32)
    rank_owner = jnp.sum((jnp.cumsum(onehot, axis=0) - onehot) * onehot, axis=1)
    slot_key = jax.random.fold_in(key, 13)
    orders = jax.vmap(lambda index: jax.random.permutation(jax.random.fold_in(slot_key, index), SLOT_DEV))(jnp.arange(N_POOL, dtype=jnp.int32))
    slot_ids = orders[owner_ids, rank_owner].astype(jnp.int32)
    return (owner_ids, slot_ids)


def draw_owners(key, part):
    return assign_slots(key)[0]


def draw_slots(key, part):
    return assign_slots(key)[1]


def with_ends(drawn, stream_key, least, largest):
    spot = [jax.random.randint(jax.random.fold_in(stream_key, axis), (), 0, length) for axis, length in enumerate(drawn.shape)]
    longest = drawn.shape.index(max(drawn.shape))
    neighbour = spot[:longest] + [(spot[longest] + 1) % drawn.shape[longest]] + spot[longest + 1:]
    return drawn.at[tuple(spot)].set(least).at[tuple(neighbour)].set(largest)


def shard_levels(key, shape, cuts, low, largest):
    loudness = 1.0
    for dim, shards_of in cuts:
        heights = jax.random.uniform(jax.random.fold_in(jax.random.fold_in(key, 6), dim), (shards_of,), jnp.float32, low / len(cuts), largest / len(cuts))
        loudness = loudness * jnp.repeat(jnp.exp(heights), shape[dim] // shards_of).reshape((-1,) + (1,) * (len(shape) - 1 - dim))
    return loudness


def normal_values(stream_key, dims, spread, reach, pieces=(), kind=jnp.bfloat16):
    drawn = jax.random.normal(stream_key, dims, jnp.float32) * spread
    if len(pieces) > 0:
        drawn = shard_levels(stream_key, dims, pieces, -0.22, 0.18) * drawn
    return jnp.clip(drawn, min=-reach, max=reach).astype(kind)


def setup_inputs(seed: int = 0, part: int = 0) -> dict:
    arg_keys = jax.random.split(jax.random.key(seed), 18)
    part_keys = jax.random.split(jax.random.fold_in(arg_keys[17], part), 18)
    hidden = normal_values(part_keys[0], (TOKENS, D), 1.0, 6.0, ((0, 4),))
    w_x = normal_values(arg_keys[1], (D, HEADS * HEAD_DIM), D ** -0.5, 0.09375, ((1, 4),))
    w_bc = normal_values(arg_keys[2], (D, 2 * GROUPS * STATE), D ** -0.5, 0.09375, ((1, 4),))
    w_dt = normal_values(arg_keys[3], (D, HEADS), D ** -0.5, 0.09375, ((1, 4),))
    conv_x = normal_values(arg_keys[4], (KERNEL, HEADS * HEAD_DIM), KERNEL ** -0.5, 3.0, ((1, 4),), jnp.float32)
    conv_bc = normal_values(arg_keys[5], (KERNEL, 2 * GROUPS * STATE), KERNEL ** -0.5, 3.0, ((1, 4),), jnp.float32)
    dt_bias = jnp.clip(-4.0 + 3.0 * jax.random.uniform(arg_keys[6], (HEADS,), jnp.float32) ** shard_levels(arg_keys[6], (HEADS,), ((0, 4),), -0.2, 0.2), -4.0, -1.0)
    a_log = jnp.clip(2.77 * jax.random.uniform(arg_keys[7], (HEADS,), jnp.float32) ** shard_levels(arg_keys[7], (HEADS,), ((0, 4),), -0.2, 0.2), 0.0, 2.77)
    d_skip = jnp.clip(0.5 + 1.0 * jax.random.uniform(arg_keys[8], (HEADS,), jnp.float32) ** shard_levels(arg_keys[8], (HEADS,), ((0, 4),), -0.2, 0.2), 0.5, 1.5)
    norm_gain = jnp.clip(1.0 + 0.1 * jax.random.normal(arg_keys[9], (HEADS * HEAD_DIM,), jnp.float32), 0.5, 1.5)
    w_out = normal_values(arg_keys[10], (HEADS * HEAD_DIM, D), (HEADS * HEAD_DIM) ** -0.5, 0.09375, ((0, 4),))
    ssm_pool = normal_values(part_keys[11], (SLOTS, HEADS, HEAD_DIM, STATE), 0.1, 0.59765625, ((0, 4), (1, 4)))
    conv_pool_x = normal_values(part_keys[12], (SLOTS, KERNEL - 1, HEADS * HEAD_DIM), 1.0, 6.0, ((0, 4), (2, 4)))
    conv_pool_bc = normal_values(part_keys[13], (SLOTS, KERNEL - 1, 2 * GROUPS * STATE), 1.0, 6.0, ((0, 4), (2, 4)))
    owners = draw_owners(jax.random.fold_in(jax.random.fold_in(arg_keys[17], part), 71), part)
    slots = draw_slots(jax.random.fold_in(jax.random.fold_in(arg_keys[17], part), 71), part)
    accepted = with_ends(jax.random.randint(part_keys[16], (REQS,), 1, DRAFT + 1), jax.random.fold_in(part_keys[16], 1), 1, DRAFT).astype(jnp.int32)
    return dict(hidden=hidden, w_x=w_x, w_bc=w_bc, w_dt=w_dt, conv_x=conv_x, conv_bc=conv_bc, dt_bias=dt_bias, a_log=a_log, d_skip=d_skip, norm_gain=norm_gain, w_out=w_out, ssm_pool=ssm_pool, conv_pool_x=conv_pool_x, conv_pool_bc=conv_pool_bc, owners=owners, slots=slots, accepted=accepted)


EPS = 1e-05

def conv_part(state_rows, raw_rows, weight, accepted):
    window = state_rows.shape[1]
    length_new = raw_rows.shape[1]
    joined = jnp.concatenate([state_rows, raw_rows], axis=1)
    summed = jnp.zeros(raw_rows.shape, jnp.float32)
    for offset in range(window + 1):
        summed = summed + weight[offset] * joined[:, offset:offset + length_new].astype(jnp.float32)
    picks = accepted[:, None] + jnp.arange(window, dtype=jnp.int32)[None, :]
    picks = jnp.broadcast_to(picks[:, :, None], (joined.shape[0], window, joined.shape[2]))
    kept_rows = jnp.take_along_axis(joined, picks, axis=1)
    return (jax.nn.silu(summed), kept_rows)

def reference(hidden, w_x, w_bc, w_dt, conv_x, conv_bc, dt_bias, a_log, d_skip, norm_gain, w_out, ssm_pool, conv_pool_x, conv_pool_bc, owners, slots, accepted):
    request_count = owners.shape[0]
    global_slot = (owners * SLOT_DEV + slots).astype(jnp.int32)
    raw_x = jnp.dot(hidden, w_x, preferred_element_type=jnp.float32).astype(jnp.bfloat16).reshape(request_count, DRAFT, -1)
    raw_bc = jnp.dot(hidden, w_bc, preferred_element_type=jnp.float32).astype(jnp.bfloat16).reshape(request_count, DRAFT, -1)
    dt_raw = jnp.dot(hidden, w_dt, preferred_element_type=jnp.float32).reshape(request_count, DRAFT, HEADS)
    conv_out_x, kept_x = conv_part(conv_pool_x[global_slot], raw_x, conv_x, accepted)
    conv_out_bc, kept_bc = conv_part(conv_pool_bc[global_slot], raw_bc, conv_bc, accepted)
    bc_act = lax.optimization_barrier(conv_out_bc.astype(jnp.bfloat16)).astype(jnp.float32)
    bc_groups = bc_act.reshape(request_count, DRAFT, 2, GROUPS, STATE)
    step_size = jax.nn.softplus(dt_raw + dt_bias)
    decay = jnp.exp(-step_size * jnp.exp(a_log))
    inputs = conv_out_x.reshape(request_count, DRAFT, HEADS, HEAD_DIM)
    per_group = HEADS // GROUPS

    def one_group(pool_now, group_id):
        head_start = group_id * per_group
        head_block = lax.dynamic_slice_in_dim(pool_now, head_start, per_group, 1)
        carried = head_block[global_slot].astype(jnp.float32)
        x_part = lax.dynamic_slice_in_dim(inputs, head_start, per_group, 2)
        step_part = lax.dynamic_slice_in_dim(step_size, head_start, per_group, 2)
        decay_part = lax.dynamic_slice_in_dim(decay, head_start, per_group, 2)
        skip_part = lax.dynamic_slice_in_dim(d_skip, head_start, per_group, 0)
        b_group = lax.dynamic_index_in_dim(bc_groups[:, :, 0], group_id, 2, keepdims=False)
        c_group = lax.dynamic_index_in_dim(bc_groups[:, :, 1], group_id, 2, keepdims=False)
        kept_state = jnp.zeros(carried.shape, jnp.float32)
        outputs = []
        for position in range(DRAFT):
            carried = carried * decay_part[:, position, :, None, None] + (step_part[:, position, :, None] * x_part[:, position])[..., None] * b_group[:, position, None, None, :]
            readout = jnp.einsum('rhpn,rn->rhp', carried, c_group[:, position], precision=lax.Precision.HIGHEST)
            outputs.append(readout + skip_part[None, :, None] * x_part[:, position])
            kept_state = jnp.where((accepted == position + 1)[:, None, None, None], carried, kept_state)
        head_block = head_block.at[global_slot].set(kept_state.astype(jnp.bfloat16))
        pool_now = lax.dynamic_update_slice_in_dim(pool_now, head_block, head_start, 1)
        return (pool_now, jnp.stack(outputs, axis=1))
    new_ssm_pool, group_y = lax.scan(one_group, ssm_pool, jnp.arange(GROUPS, dtype=jnp.int32))
    ssm_y = jnp.transpose(group_y, (1, 2, 0, 3, 4)).reshape(request_count, DRAFT, HEADS, HEAD_DIM)
    mean_sq = lax.optimization_barrier(jnp.mean(ssm_y * ssm_y, axis=3, keepdims=True))
    normed = (ssm_y * lax.rsqrt(mean_sq + EPS)).reshape(request_count * DRAFT, HEADS * HEAD_DIM) * norm_gain
    mixed = jnp.dot(normed.astype(jnp.bfloat16), w_out, preferred_element_type=jnp.float32).astype(jnp.bfloat16)
    new_conv_x = conv_pool_x.at[global_slot].set(kept_x)
    new_conv_bc = conv_pool_bc.at[global_slot].set(kept_bc)
    return (mixed, new_ssm_pool, new_conv_x, new_conv_bc)
```

```python
import functools

import jax
import jax.numpy as jnp
from jax import lax
from jax.experimental import pallas as pl
from jax.experimental.pallas import tpu as pltpu
from jax.sharding import PartitionSpec as P

HEADS = 64
HEAD_DIM = 64
STATE = 128
GROUPS = 8
DRAFT = 8
SHIFT = 3
EPS = 1e-05
FAR = 4096.0

F32 = jnp.float32
BF16 = jnp.bfloat16
ANY = pl.BlockSpec(memory_space=pl.ANY)
VMEM = pl.BlockSpec(memory_space=pltpu.VMEM)
SMEM = pl.BlockSpec(memory_space=pltpu.SMEM)


def params(mib, **more):
    return pltpu.CompilerParams(vmem_limit_bytes=mib * 2**20, **more)


def cost(flops, moved):
    return pl.CostEstimate(flops=int(flops), bytes_accessed=int(moved), transcendentals=0)


def iota(shape, dim):
    return lax.broadcasted_iota(jnp.int32, shape, dim)


def dot(a, b):
    return jnp.dot(a, b, preferred_element_type=F32)


def dot_t(a, b):
    return lax.dot_general(a, b, (((1,), (1,)), ((), ())), preferred_element_type=F32)


def as_col(row):
    n = row.shape[1]
    eye = iota((n, n), 0) == iota((n, n), 1)
    return jnp.sum(jnp.where(eye, jnp.broadcast_to(row, (n, n)), 0.0), axis=1, keepdims=True)


def wrap(value, n):
    return jnp.where(value < 0, value + n, value)


def block_shift(req):
    return req.bit_length() - 1


def ranks(orow, ocol, req):
    n = orow.shape[1]
    sub, lane = iota((n, n), 0), iota((n, n), 1)
    sh = block_shift(req)
    same = (ocol == orow) & ((sub >> sh) == (lane >> sh))
    row = jnp.sum(jnp.where(same & (sub < lane), 1.0, 0.0), axis=0, keepdims=True)
    col = jnp.sum(jnp.where(same & (lane < sub), 1.0, 0.0), axis=1, keepdims=True)
    return row, col


def hot(mask):
    return jnp.where(mask, 1.0, 0.0).astype(BF16)


def send_matrix(orow, me, n_pool, req, cr):
    ocol = as_col(orow)
    _, rank_col = ranks(orow, ocol, req)
    total, tokens = orow.shape[1], req * DRAFT
    place_col = wrap(ocol - me.astype(F32), n_pool) * cr + rank_col * DRAFT
    token = iota((total, tokens), 1)
    mine = (iota((total, tokens), 0) - me * req) == (token >> SHIFT)
    place = jnp.sum(jnp.where(mine, jnp.broadcast_to(place_col, (total, tokens)), 0.0), axis=0, keepdims=True)
    place = place + (iota((1, tokens), 1) & (DRAFT - 1)).astype(F32)
    return hot(iota((n_pool * cr, tokens), 0).astype(F32) == place)


def collect_matrix(orow, me, n_pool, req, cr):
    ocol = as_col(orow)
    rank_row, _ = ranks(orow, ocol, req)
    total, tokens = orow.shape[1], req * DRAFT
    place_row = wrap(orow - me.astype(F32), n_pool) * cr + rank_row * DRAFT
    token = iota((tokens, total), 0)
    mine = (iota((tokens, total), 1) - me * req) == (token >> SHIFT)
    place = jnp.sum(jnp.where(mine, jnp.broadcast_to(place_row, (tokens, total)), 0.0), axis=1, keepdims=True)
    place = place + (iota((tokens, 1), 0) & (DRAFT - 1)).astype(F32)
    return hot(iota((tokens, n_pool * cr), 1).astype(F32) == place)


def owner_matrix(orow, srow, me, n_pool, req, cr, slots):
    ocol = as_col(orow)
    rank_row, _ = ranks(orow, ocol, req)
    total, rows = orow.shape[1], slots * DRAFT
    block = (iota((1, total), 1) >> block_shift(req)).astype(F32)
    place_row = wrap(me.astype(F32) - block, n_pool) * cr + rank_row * DRAFT + FAR
    slot = (iota((rows, total), 0) >> SHIFT).astype(F32)
    match = (orow == me.astype(F32)) & (srow == slot)
    place = jnp.sum(jnp.where(match, jnp.broadcast_to(place_row, (rows, total)), 0.0), axis=1, keepdims=True)
    place = place - FAR + (iota((rows, 1), 0) & (DRAFT - 1)).astype(F32)
    return hot(iota((rows, n_pool * cr), 1).astype(F32) == place)


def return_matrix(orow, srow, me, n_pool, req, cr, slots):
    ocol, scol = as_col(orow), as_col(srow)
    _, rank_col = ranks(orow, ocol, req)
    total, rows = orow.shape[1], slots * DRAFT
    block = (iota((total, 1), 0) >> block_shift(req)).astype(F32)
    place_col = wrap(me.astype(F32) - block, n_pool) * cr + rank_col * DRAFT + FAR
    slot = (iota((total, rows), 1) >> SHIFT).astype(F32)
    match = (ocol == me.astype(F32)) & (scol == slot)
    place = jnp.sum(jnp.where(match, jnp.broadcast_to(place_col, (total, rows)), 0.0), axis=0, keepdims=True)
    place = place - FAR + (iota((1, rows), 1) & (DRAFT - 1)).astype(F32)
    return hot(iota((n_pool * cr, rows), 0).astype(F32) == place)


def slot_accepts(orow, srow, arow, me, slots):
    total, rows = orow.shape[1], slots * DRAFT
    slot = (iota((rows, total), 0) >> SHIFT).astype(F32)
    match = (orow == me.astype(F32)) & (srow == slot)
    return jnp.sum(jnp.where(match, jnp.broadcast_to(arow, (rows, total)), 0.0), axis=1, keepdims=True)


def conv_slots(raw, pool, weight, accepts):
    rows, width = raw.shape
    slots = rows // DRAFT
    window = pool.shape[1]
    old = jnp.concatenate(
        [pool.astype(F32), jnp.zeros((slots, DRAFT - window, width), F32)], axis=1
    ).reshape(rows, width)
    position = iota((rows, width), 0) & (DRAFT - 1)
    summed = weight[window] * raw
    for back in range(1, window + 1):
        new_part = pltpu.roll(raw, back, 0)
        old_part = pltpu.roll(old, (back - window) % rows, 0)
        summed = summed + weight[window - back] * jnp.where(position < back, old_part, new_part)
    sub, lane = iota((rows, rows), 0), iota((rows, rows), 1)
    here = (sub >> SHIFT) == (lane >> SHIFT)
    at = (sub & (DRAFT - 1)).astype(F32) + accepts
    source = (lane & (DRAFT - 1)).astype(F32)
    from_old = hot(here & (source == at) & (source < window))
    from_new = hot(here & (source + window == at))
    kept = dot(from_old, old.astype(BF16)) + dot(from_new, raw.astype(BF16))
    return summed, kept.astype(BF16).reshape(slots, DRAFT, width)[:, :window]


def silu(v):
    return v / (1.0 + jnp.exp(-v))


def spread_matrix(heads):
    shape = (heads, heads * HEAD_DIM)
    return hot(iota(shape, 0) == (iota(shape, 1) >> 6))


def spread(values, matrix):
    high = values.astype(BF16)
    low = (values - high.astype(F32)).astype(BF16)
    return dot(high, matrix) + dot(low, matrix)


def project_kernel(n_pool, req, cr, chunk, with_dt, *refs):
    me_ref, orow_ref, hidden, w = refs[:4]
    refs = refs[4:]
    if with_dt:
        w_dt, refs = refs[0], refs[1:]
    outs, refs = refs[:n_pool], refs[n_pool:]
    hbuf, wbuf, sems = refs[:3]
    steps = hidden.shape[1] // chunk
    copies = []
    for k in range(steps):
        part = pl.ds(k * chunk, chunk)
        copies.append(
            [
                pltpu.make_async_copy(hidden.at[:, part], hbuf.at[:, part], sems.at[0, k]),
                pltpu.make_async_copy(w.at[part], wbuf.at[part], sems.at[1, k]),
            ]
        )
        if with_dt:
            copies[-1].append(pltpu.make_async_copy(w_dt.at[part], refs[3].at[part], sems.at[2, k]))
        for copy in copies[-1]:
            copy.start()
    order = send_matrix(orow_ref[...].astype(F32), me_ref[0], n_pool, req, cr)
    total = jnp.zeros((hidden.shape[0], w.shape[1]), F32)
    if with_dt:
        total_dt = jnp.zeros((hidden.shape[0], w_dt.shape[1]), F32)
    for k in range(steps):
        for copy in copies[k]:
            copy.wait()
        rows = hbuf[:, k * chunk : (k + 1) * chunk]
        total = total + dot(rows, wbuf[k * chunk : (k + 1) * chunk])
        if with_dt:
            total_dt = total_dt + dot(rows, refs[3][k * chunk : (k + 1) * chunk])
    width = w.shape[1]
    placed = dot(order, total.astype(BF16)).astype(BF16)
    for s in range(n_pool):
        outs[s][:, :width] = placed[s * cr : (s + 1) * cr]
    if with_dt:
        heads = w_dt.shape[1]
        high = total_dt.astype(BF16)
        low = (total_dt - high.astype(F32)).astype(BF16)
        shape = (heads, 128)
        to_high = hot(iota(shape, 0) == iota(shape, 1))
        to_low = hot(iota(shape, 0) + heads == iota(shape, 1))
        pair = (dot(high, to_high) + dot(low, to_low)).astype(BF16)
        placed = dot(order, pair).astype(BF16)
        for s in range(n_pool):
            outs[s][:, width:] = placed[s * cr : (s + 1) * cr]


def project(me, orow, hidden, w, w_dt, n_pool, req, cr):
    tokens, depth = hidden.shape
    width = w.shape[1]
    chunk = min(512, depth)
    with_dt = w_dt is not None
    extra = 128 if with_dt else 0
    scratch = [
        pltpu.VMEM((tokens, depth), BF16),
        pltpu.VMEM((depth, width), BF16),
        pltpu.SemaphoreType.DMA((3, depth // chunk)),
    ]
    if with_dt:
        scratch.append(pltpu.VMEM((depth, w_dt.shape[1]), BF16))
    operands = [me, orow, hidden, w] + ([w_dt] if with_dt else [])
    return pl.pallas_call(
        functools.partial(project_kernel, n_pool, req, cr, chunk, with_dt),
        out_shape=[jax.ShapeDtypeStruct((cr, width + extra), BF16)] * n_pool,
        in_specs=[SMEM, VMEM, ANY, ANY] + ([ANY] if with_dt else []),
        out_specs=[VMEM] * n_pool,
        scratch_shapes=scratch,
        compiler_params=params(32),
        cost_estimate=cost(2 * tokens * depth * width, depth * (width + extra) * 2 + tokens * depth * 2),
    )(*operands)


def bc_kernel(n_pool, req, cr, me_ref, orow_ref, srow_ref, arow_ref, *refs):
    got, refs = refs[:n_pool], refs[n_pool:]
    pool_ref, weight_ref, act_ref, dt_ref, kept_ref = refs
    slots, _, width = pool_ref.shape
    me = me_ref[0]
    orow, srow, arow = (r[...].astype(F32) for r in (orow_ref, srow_ref, arow_ref))
    order = owner_matrix(orow, srow, me, n_pool, req, cr, slots)
    accepts = slot_accepts(orow, srow, arow, me, slots)
    raw = dot(order, jnp.concatenate([g[...] for g in got], axis=0))
    heads = dt_ref.shape[1]
    shape = (128, heads)
    lane = iota(shape, 0)
    head = iota(shape, 1)
    both = hot((lane == head) | (lane == head + heads))
    dt_ref[...] = dot(raw[:, width:].astype(BF16), both)
    summed, kept = conv_slots(raw[:, :width], pool_ref[...], weight_ref[...], accepts)
    kept_ref[...] = kept
    act_ref[...] = silu(summed).astype(BF16)


def bc_stage(me, orow, srow, arow, got, pool, weight, heads, n_pool, req, cr):
    slots, _, width = pool.shape
    rows = slots * DRAFT
    return pl.pallas_call(
        functools.partial(bc_kernel, n_pool, req, cr),
        out_shape=[
            jax.ShapeDtypeStruct((rows, width), BF16),
            jax.ShapeDtypeStruct((rows, heads), F32),
            jax.ShapeDtypeStruct(pool.shape, BF16),
        ],
        in_specs=[SMEM] + [VMEM] * (n_pool + 5),
        out_specs=[VMEM] * 3,
        compiler_params=params(24),
        cost_estimate=cost(2e6, 1e6),
    )(me, orow, srow, arow, *got, pool, weight)


def exchange_plan(n_tensor, width, span):
    piece = span * STATE
    per_group = HEADS // GROUPS
    head_local = HEADS // n_tensor
    edges, own = [], []
    for target in range(n_tensor):
        first = target * head_local // per_group
        for kind in range(2):
            column = (kind * GROUPS + first) * STATE
            source, part = column // width, column % width // piece
            (own if source == target else edges).append((source, target, kind, part))
    rounds = []
    for edge in edges:
        for one in rounds:
            if all(edge[0] != e[0] and edge[1] != e[1] for e in one):
                one.append(edge)
                break
        else:
            rounds.append([edge])
    return rounds, own


def exchange(act, n_tensor, span, rank):
    width = act.shape[1]
    piece = span * STATE
    rounds, own = exchange_plan(n_tensor, width, span)
    sides = [jnp.zeros((act.shape[0], piece), act.dtype)] * 2

    def part_of(table):
        offset = jnp.asarray(table, jnp.int32)[rank] * piece
        return lax.dynamic_slice_in_dim(act, offset, piece, axis=1)

    for kind in range(2):
        table, there = [0] * n_tensor, [False] * n_tensor
        for source, target, k, part in own:
            if k == kind:
                table[target], there[target] = part, True
        if any(there):
            sides[kind] = jnp.where(jnp.asarray(there)[rank], part_of(table), sides[kind])
    for one in rounds:
        table = [0] * n_tensor
        kinds = [-1] * n_tensor
        for source, target, kind, part in one:
            table[source], kinds[target] = part, kind
        moved = lax.ppermute(part_of(table), "tensor", [(e[0], e[1]) for e in one])
        got = jnp.asarray(kinds, jnp.int32)[rank]
        for kind in range(2):
            sides[kind] = jnp.where(got == kind, moved, sides[kind])
    return sides


def mix_kernel(
    me_ref, orow_ref, srow_ref, arow_ref, b_ref, c_ref, dt_ref, bias_ref, alog_ref, pool, y_ref, m_ref, w_ref, d_ref, buf, sems
):
    slots, heads = pool.shape[:2]
    rows = slots * DRAFT
    span = b_ref.shape[1] // STATE
    per = heads // span
    copies = [pltpu.make_async_copy(pool.at[j], buf.at[j], sems.at[j]) for j in range(slots)]
    for copy in copies:
        copy.start()
    orow, srow, arow = (r[...].astype(F32) for r in (orow_ref, srow_ref, arow_ref))
    accepts = slot_accepts(orow, srow, arow, me_ref[0], slots)
    x = dt_ref[...] + bias_ref[...]
    step = jnp.maximum(x, 0.0) + jnp.log1p(jnp.exp(-jnp.abs(x)))
    logs = -step * jnp.exp(alog_ref[...])
    position = iota((rows, heads), 0) & (DRAFT - 1)
    for back in (1, 2, 4):
        logs = logs + jnp.where(position >= back, pltpu.roll(logs, back, 0), 0.0)
    last = jnp.where(position.astype(F32) + 1 == accepts, logs, 0.0).reshape(slots, DRAFT, heads)
    last = jnp.broadcast_to(jnp.sum(last, axis=1, keepdims=True), (slots, DRAFT, heads))
    d_ref[...] = jnp.exp(last[:, 0, :])
    last = last.reshape(rows, heads)
    w_ref[...] = jnp.where(position.astype(F32) < accepts, jnp.exp(jnp.minimum(last - logs, 0.0)) * step, 0.0)
    eye = jnp.where(iota((rows, rows), 0) == iota((rows, rows), 1), 1.0, 0.0)

    def turned(v):
        return lax.dot_general(
            v, eye, (((0,), (0,)), ((), ())), preferred_element_type=F32, precision=lax.Precision.HIGHEST
        )

    logs_t, step_t = turned(logs), turned(step)
    sub, lane = iota((rows, rows), 0), iota((rows, rows), 1)
    causal = ((sub >> SHIFT) == (lane >> SHIFT)) & (lane <= sub)
    for g in range(span):
        part = slice(g * STATE, (g + 1) * STATE)
        pair = jnp.where(causal, dot_t(c_ref[:, part], b_ref[:, part]), 0.0)
        for h in range(g * per, (g + 1) * per):
            fade = jnp.exp(jnp.minimum(logs[:, h : h + 1] - logs_t[h : h + 1], 0.0))
            m_ref[h] = (pair * fade * step_t[h : h + 1]).astype(BF16)
    fade = spread(jnp.exp(logs), spread_matrix(heads))
    c = c_ref[...].astype(F32)
    for j in range(slots):
        copies[j].wait()
        here = slice(j * DRAFT, (j + 1) * DRAFT)
        for g in range(span):
            states = buf[j, g * per : (g + 1) * per].reshape(per * HEAD_DIM, STATE)
            columns = slice(g * per * HEAD_DIM, (g + 1) * per * HEAD_DIM)
            read = dot_t(c[here, g * STATE : (g + 1) * STATE].astype(BF16), states)
            y_ref[here, columns] = read * fade[here, columns]


def mix_stage(me, orow, srow, arow, b, c, dt, bias, a_log, pool):
    slots, heads = pool.shape[:2]
    rows = slots * DRAFT
    return pl.pallas_call(
        mix_kernel,
        out_shape=[
            jax.ShapeDtypeStruct((rows, heads * HEAD_DIM), F32),
            jax.ShapeDtypeStruct((heads, rows, rows), BF16),
            jax.ShapeDtypeStruct((rows, heads), F32),
            jax.ShapeDtypeStruct((slots, heads), F32),
        ],
        in_specs=[SMEM] + [VMEM] * 8 + [ANY],
        out_specs=[VMEM] * 4,
        scratch_shapes=[pltpu.VMEM(pool.shape, BF16), pltpu.SemaphoreType.DMA((slots,))],
        compiler_params=params(32),
        cost_estimate=cost(2 * rows * heads * HEAD_DIM * STATE, 2 * pool.size),
    )(me, orow, srow, arow, b, c, dt, bias, a_log, pool)


def x_kernel(n_pool, req, cr, me_ref, orow_ref, srow_ref, arow_ref, *refs):
    got, refs = refs[:n_pool], refs[n_pool:]
    pool_ref, weight_ref, y_ref, m_ref, skip_ref, gain_ref = refs[:6]
    outs, (x_ref, kept_ref) = refs[6 : 6 + n_pool], refs[6 + n_pool :]
    slots, _, width = pool_ref.shape
    heads = width // HEAD_DIM
    me = me_ref[0]
    orow, srow, arow = (r[...].astype(F32) for r in (orow_ref, srow_ref, arow_ref))
    order = owner_matrix(orow, srow, me, n_pool, req, cr, slots)
    accepts = slot_accepts(orow, srow, arow, me, slots)
    raw = dot(order, jnp.concatenate([g[...] for g in got], axis=0))
    summed, kept = conv_slots(raw, pool_ref[...], weight_ref[...], accepts)
    kept_ref[...] = kept
    x = silu(summed)
    x_ref[...] = x
    matrix = spread_matrix(heads)
    small = x.astype(BF16)
    parts = [dot(m_ref[h], small[:, h * HEAD_DIM : (h + 1) * HEAD_DIM]) for h in range(heads)]
    y = jnp.concatenate(parts, axis=1) + y_ref[...] + spread(skip_ref[...], matrix) * x
    square = (y * y).astype(BF16)
    scale = lax.rsqrt(dot_t(square, matrix) * (1.0 / HEAD_DIM) + EPS)
    normed = (y * spread(scale, matrix) * gain_ref[...]).astype(BF16)
    back = return_matrix(orow, srow, me, n_pool, req, cr, slots)
    placed = dot(back, normed).astype(BF16)
    for s in range(n_pool):
        outs[s][...] = placed[s * cr : (s + 1) * cr]


def x_stage(me, orow, srow, arow, got, pool, weight, y, m, skip, gain, n_pool, req, cr):
    slots, _, width = pool.shape
    rows = slots * DRAFT
    return pl.pallas_call(
        functools.partial(x_kernel, n_pool, req, cr),
        out_shape=[jax.ShapeDtypeStruct((cr, width), BF16)] * n_pool
        + [jax.ShapeDtypeStruct((rows, width), F32), jax.ShapeDtypeStruct(pool.shape, BF16)],
        in_specs=[SMEM] + [VMEM] * (n_pool + 9),
        out_specs=[VMEM] * (n_pool + 2),
        compiler_params=params(32),
        cost_estimate=cost(2 * rows * rows * width, 4e6),
    )(me, orow, srow, arow, *got, pool, weight, y, m, skip, gain)


def state_kernel(d_ref, x_ref, w_ref, b_ref, pool, new_pool, buf, sems, out_sems):
    slots, heads = pool.shape[:2]
    rows = slots * DRAFT
    span = b_ref.shape[1] // STATE
    per = heads // span
    copies = [pltpu.make_async_copy(pool.at[j], buf.at[j], sems.at[j]) for j in range(slots)]
    backs = [pltpu.make_async_copy(buf.at[j], new_pool.at[j], out_sems.at[j]) for j in range(slots)]
    for copy in copies:
        copy.start()
    weighted = x_ref[...] * spread(w_ref[...], spread_matrix(heads))
    turned = weighted.T
    high = turned.astype(BF16)
    b = b_ref[...]
    slot = iota((rows, STATE), 0) >> SHIFT
    for j in range(slots):
        copies[j].wait()
        for g in range(span):
            rhs = jnp.where(slot == j, b[:, g * STATE : (g + 1) * STATE].astype(F32), 0.0).astype(BF16)
            added = dot(high[g * per * HEAD_DIM : (g + 1) * per * HEAD_DIM], rhs)
            for i in range(per):
                h = g * per + i
                kept = buf[j, h].astype(F32) * d_ref[j, h] + added[i * HEAD_DIM : (i + 1) * HEAD_DIM]
                buf[j, h] = kept.astype(BF16)
        backs[j].start()
    for copy in backs:
        copy.wait()


def state_stage(d, x, w, b, pool):
    slots = pool.shape[0]
    return pl.pallas_call(
        state_kernel,
        out_shape=jax.ShapeDtypeStruct(pool.shape, BF16),
        in_specs=[SMEM] + [VMEM] * 3 + [ANY],
        out_specs=ANY,
        scratch_shapes=[
            pltpu.VMEM(pool.shape, BF16),
            pltpu.SemaphoreType.DMA((slots,)),
            pltpu.SemaphoreType.DMA((slots,)),
        ],
        compiler_params=params(32),
        cost_estimate=cost(4 * pool.size * DRAFT, 4 * pool.size),
    )(d, x, w, b, pool)


def out_kernel(n_line, other_core, n_pool, req, cr, me_ref, orow_ref, *refs):
    if other_core:
        got, refs = refs[:n_pool], refs[n_pool:]
    else:
        got, refs = refs[:1], refs[1:]
    w, outs = refs[0], refs[1 : 1 + n_line]
    refs = refs[1 + n_line :]
    if other_core:
        normed_ref, refs = refs[0], refs[1:]
    buf, sems = refs
    width = buf.shape[2]
    rank = me_ref[1]
    core, line = rank & 1, rank >> 1
    if other_core:
        core = 1 - core
    copies = []
    order = list(range(1, n_line)) + [0]
    for i in order:
        there = line + i
        there = jnp.where(there >= n_line, there - n_line, there)
        column = pl.multiple_of((2 * there + core) * width, 128)
        copies.append(pltpu.make_async_copy(w.at[:, pl.ds(column, width)], buf.at[i], sems.at[i]))
        copies[-1].start()
    if other_core:
        collect = collect_matrix(orow_ref[...].astype(F32), me_ref[0], n_pool, req, cr)
        rows = dot(collect, jnp.concatenate([g[...] for g in got], axis=0)).astype(BF16)
        normed_ref[...] = rows
    else:
        rows = got[0][...]
    for copy, i in zip(copies, order):
        copy.wait()
        outs[i][...] = dot(rows, buf[i]).astype(outs[i].dtype)


def out_stage(me, orow, got, w, n_line, other_core, n_pool, req, cr):
    depth, total = w.shape
    width = total // (2 * n_line)
    tokens = req * DRAFT
    kind = BF16 if other_core else F32
    shapes = [jax.ShapeDtypeStruct((tokens, width), kind)] * n_line
    if other_core:
        shapes = shapes + [jax.ShapeDtypeStruct((tokens, depth), BF16)]
    return pl.pallas_call(
        functools.partial(out_kernel, n_line, other_core, n_pool, req, cr),
        out_shape=shapes,
        in_specs=[SMEM, VMEM] + [VMEM] * len(got) + [ANY],
        out_specs=[VMEM] * len(shapes),
        scratch_shapes=[pltpu.VMEM((n_line, depth, width), BF16), pltpu.SemaphoreType.DMA((n_line,))],
        compiler_params=params(32),
        cost_estimate=cost(tokens * depth * total, depth * total),
    )(me, orow, *got, w)


def body(
    hidden,
    w_x,
    w_bc,
    w_dt,
    conv_x,
    conv_bc,
    dt_bias,
    a_log,
    d_skip,
    norm_gain,
    w_out,
    ssm_pool,
    conv_pool_x,
    conv_pool_bc,
    owners,
    slots,
    accepted,
):
    n_pool = lax.axis_size("pool")
    n_tensor = lax.axis_size("tensor")
    n_line = n_tensor // 2
    rank = lax.axis_index("tensor").astype(jnp.int32)
    me = jnp.stack([lax.axis_index("pool").astype(jnp.int32), rank])
    req = hidden.shape[0] // DRAFT
    share = req // n_pool
    capacity = share + share // 2
    cr = -(-capacity * DRAFT // 16) * 16
    head_local = w_dt.shape[1]
    span = max(1, head_local // (HEADS // GROUPS))
    orow, srow, arow = (v.reshape(1, -1) for v in (owners, slots, accepted))

    def row(v):
        return v.reshape(1, -1)

    def to_owner(parts):
        return [parts[0]] + [
            lax.ppermute(parts[s], "pool", [(i, (i + s) % n_pool) for i in range(n_pool)]) for s in range(1, n_pool)
        ]

    def to_requester(parts):
        return [parts[0]] + [
            lax.ppermute(parts[s], "pool", [((i + s) % n_pool, i) for i in range(n_pool)]) for s in range(1, n_pool)
        ]

    bc_sent = project(me, orow, hidden, w_bc, w_dt, n_pool, req, cr)
    bc_got = to_owner(bc_sent)
    x_sent = project(me, orow, hidden, w_x, None, n_pool, req, cr)
    x_got = to_owner(x_sent)
    act, dt, new_conv_bc = bc_stage(
        me, orow, srow, arow, bc_got, conv_pool_bc, conv_bc, head_local, n_pool, req, cr
    )
    b, c = exchange(act, n_tensor, span, rank)
    y, m, w, d = mix_stage(me, orow, srow, arow, b, c, dt, row(dt_bias), row(a_log), ssm_pool)
    stage = x_stage(
        me, orow, srow, arow, x_got, conv_pool_x, conv_x, y, m, row(d_skip), row(norm_gain), n_pool, req, cr
    )
    normed_sent, (x, new_conv_x) = stage[:n_pool], stage[n_pool:]
    normed_got = to_requester(normed_sent)
    new_pool = state_stage(d, x, w, b, ssm_pool)
    sends = out_stage(me, orow, normed_got, w_out, n_line, True, n_pool, req, cr)
    sends, normed = sends[:n_line], sends[n_line]
    swap = [(i, i ^ 1) for i in range(n_tensor)]
    order = list(range(1, n_line)) + [0]
    core_got = {i: lax.ppermute(sends[i], "tensor", swap) for i in order}
    keeps = out_stage(me, orow, [normed], w_out, n_line, False, n_pool, req, cr)
    mixed = None
    arrived = []
    for i in range(1, n_line):
        ahead = (keeps[i] + core_got[i].astype(F32)).astype(BF16)
        pairs = [(r, ((r // 2 + i) % n_line) * 2 + r % 2) for r in range(n_tensor)]
        arrived.append(lax.ppermute(ahead, "tensor", pairs))
    mixed = keeps[0] + core_got[0].astype(F32)
    for one in arrived:
        mixed = mixed + one.astype(F32)
    return (mixed.astype(BF16), new_pool, new_conv_x, new_conv_bc)


def solution(mesh):
    in_specs = (
        P(("groups", "pool"), None),
        P(None, "tensor"),
        P(None, "tensor"),
        P(None, "tensor"),
        P(None, "tensor"),
        P(None, "tensor"),
        P("tensor"),
        P("tensor"),
        P("tensor"),
        P("tensor"),
        P("tensor", None),
        P(("groups", "pool"), "tensor", None, None),
        P(("groups", "pool"), None, "tensor"),
        P(("groups", "pool"), None, "tensor"),
        P("groups"),
        P("groups"),
        P("groups"),
    )
    out_specs = (
        P(("groups", "pool"), "tensor"),
        P(("groups", "pool"), "tensor", None, None),
        P(("groups", "pool"), None, "tensor"),
        P(("groups", "pool"), None, "tensor"),
    )
    return jax.shard_map(body, mesh=mesh, in_specs=in_specs, out_specs=out_specs, check_vma=False)
```

```python
import functools

import jax
import jax.numpy as jnp
from jax import lax
from jax.experimental import pallas as pl
from jax.experimental.pallas import tpu as pltpu
from jax.sharding import PartitionSpec as P

HEADS = 64
HEAD_DIM = 64
STATE = 128
GROUPS = 8
DRAFT = 8
SHIFT = 3
EPS = 1e-05
FAR = 4096.0

F32 = jnp.float32
BF16 = jnp.bfloat16
ANY = pl.BlockSpec(memory_space=pl.ANY)
HBM = pl.BlockSpec(memory_space=pltpu.HBM)
VMEM = pl.BlockSpec(memory_space=pltpu.VMEM)
SMEM = pl.BlockSpec(memory_space=pltpu.SMEM)


def params(mib, **more):
    return pltpu.CompilerParams(vmem_limit_bytes=mib * 2**20, **more)


def cost(flops, moved):
    return pl.CostEstimate(flops=int(flops), bytes_accessed=int(moved), transcendentals=0)


def iota(shape, dim):
    return lax.broadcasted_iota(jnp.int32, shape, dim)


def dot(a, b):
    return jnp.dot(a, b, preferred_element_type=F32)


def dot_t(a, b):
    return lax.dot_general(a, b, (((1,), (1,)), ((), ())), preferred_element_type=F32)


def as_col(row):
    n = row.shape[1]
    eye = iota((n, n), 0) == iota((n, n), 1)
    return jnp.sum(jnp.where(eye, jnp.broadcast_to(row, (n, n)), 0.0), axis=1, keepdims=True)


def wrap(value, n):
    return jnp.where(value < 0, value + n, value)


def block_shift(req):
    return req.bit_length() - 1


def ranks(orow, ocol, req):
    n = orow.shape[1]
    sub, lane = iota((n, n), 0), iota((n, n), 1)
    sh = block_shift(req)
    same = (ocol == orow) & ((sub >> sh) == (lane >> sh))
    row = jnp.sum(jnp.where(same & (sub < lane), 1.0, 0.0), axis=0, keepdims=True)
    col = jnp.sum(jnp.where(same & (lane < sub), 1.0, 0.0), axis=1, keepdims=True)
    return row, col


def hot(mask):
    return jnp.where(mask, 1.0, 0.0).astype(BF16)


def send_matrix(orow, me, n_pool, req, cr):
    ocol = as_col(orow)
    _, rank_col = ranks(orow, ocol, req)
    total, tokens = orow.shape[1], req * DRAFT
    place_col = wrap(ocol - me.astype(F32), n_pool) * cr + rank_col * DRAFT
    token = iota((total, tokens), 1)
    mine = (iota((total, tokens), 0) - me * req) == (token >> SHIFT)
    place = jnp.sum(jnp.where(mine, jnp.broadcast_to(place_col, (total, tokens)), 0.0), axis=0, keepdims=True)
    place = place + (iota((1, tokens), 1) & (DRAFT - 1)).astype(F32)
    return hot(iota((n_pool * cr, tokens), 0).astype(F32) == place)


def collect_matrix(orow, me, n_pool, req, cr):
    ocol = as_col(orow)
    rank_row, _ = ranks(orow, ocol, req)
    total, tokens = orow.shape[1], req * DRAFT
    place_row = wrap(orow - me.astype(F32), n_pool) * cr + rank_row * DRAFT
    token = iota((tokens, total), 0)
    mine = (iota((tokens, total), 1) - me * req) == (token >> SHIFT)
    place = jnp.sum(jnp.where(mine, jnp.broadcast_to(place_row, (tokens, total)), 0.0), axis=1, keepdims=True)
    place = place + (iota((tokens, 1), 0) & (DRAFT - 1)).astype(F32)
    return hot(iota((tokens, n_pool * cr), 1).astype(F32) == place)


def owner_matrix(orow, srow, me, n_pool, req, cr, slots):
    ocol = as_col(orow)
    rank_row, _ = ranks(orow, ocol, req)
    total, rows = orow.shape[1], slots * DRAFT
    block = (iota((1, total), 1) >> block_shift(req)).astype(F32)
    place_row = wrap(me.astype(F32) - block, n_pool) * cr + rank_row * DRAFT + FAR
    slot = (iota((rows, total), 0) >> SHIFT).astype(F32)
    match = (orow == me.astype(F32)) & (srow == slot)
    place = jnp.sum(jnp.where(match, jnp.broadcast_to(place_row, (rows, total)), 0.0), axis=1, keepdims=True)
    place = place - FAR + (iota((rows, 1), 0) & (DRAFT - 1)).astype(F32)
    return hot(iota((rows, n_pool * cr), 1).astype(F32) == place)


def return_matrix(orow, srow, me, n_pool, req, cr, slots):
    ocol, scol = as_col(orow), as_col(srow)
    _, rank_col = ranks(orow, ocol, req)
    total, rows = orow.shape[1], slots * DRAFT
    block = (iota((total, 1), 0) >> block_shift(req)).astype(F32)
    place_col = wrap(me.astype(F32) - block, n_pool) * cr + rank_col * DRAFT + FAR
    slot = (iota((total, rows), 1) >> SHIFT).astype(F32)
    match = (ocol == me.astype(F32)) & (scol == slot)
    place = jnp.sum(jnp.where(match, jnp.broadcast_to(place_col, (total, rows)), 0.0), axis=0, keepdims=True)
    place = place - FAR + (iota((1, rows), 1) & (DRAFT - 1)).astype(F32)
    return hot(iota((n_pool * cr, rows), 0).astype(F32) == place)


def slot_accepts(orow, srow, arow, me, slots):
    total, rows = orow.shape[1], slots * DRAFT
    slot = (iota((rows, total), 0) >> SHIFT).astype(F32)
    match = (orow == me.astype(F32)) & (srow == slot)
    return jnp.sum(jnp.where(match, jnp.broadcast_to(arow, (rows, total)), 0.0), axis=1, keepdims=True)


def conv_slots(raw, pool, weight, accepts):
    rows, width = raw.shape
    slots = rows // DRAFT
    window = pool.shape[1]
    old = jnp.concatenate(
        [pool.astype(F32), jnp.zeros((slots, DRAFT - window, width), F32)], axis=1
    ).reshape(rows, width)
    position = iota((rows, width), 0) & (DRAFT - 1)
    summed = weight[window] * raw
    for back in range(1, window + 1):
        new_part = pltpu.roll(raw, back, 0)
        old_part = pltpu.roll(old, (back - window) % rows, 0)
        summed = summed + weight[window - back] * jnp.where(position < back, old_part, new_part)
    sub, lane = iota((rows, rows), 0), iota((rows, rows), 1)
    here = (sub >> SHIFT) == (lane >> SHIFT)
    at = (sub & (DRAFT - 1)).astype(F32) + accepts
    source = (lane & (DRAFT - 1)).astype(F32)
    from_old = hot(here & (source == at) & (source < window))
    from_new = hot(here & (source + window == at))
    kept = dot(from_old, old.astype(BF16)) + dot(from_new, raw.astype(BF16))
    return summed, kept.astype(BF16).reshape(slots, DRAFT, width)[:, :window]


def silu(v):
    return v / (1.0 + jnp.exp(-v))


def spread_matrix(heads):
    shape = (heads, heads * HEAD_DIM)
    return hot(iota(shape, 0) == (iota(shape, 1) >> 6))


def spread(values, matrix):
    high = values.astype(BF16)
    low = (values - high.astype(F32)).astype(BF16)
    return dot(high, matrix) + dot(low, matrix)


def project_kernel(n_pool, req, cr, chunk, with_dt, *refs):
    me_ref, orow_ref, hidden, w = refs[:4]
    refs = refs[4:]
    if with_dt:
        w_dt, refs = refs[0], refs[1:]
    outs, refs = refs[:n_pool], refs[n_pool:]
    hbuf, wbuf, sems = refs[:3]
    steps = hidden.shape[1] // chunk
    copies = []
    for k in range(steps):
        part = pl.ds(k * chunk, chunk)
        copies.append(
            [
                pltpu.make_async_copy(hidden.at[:, part], hbuf.at[:, part], sems.at[0, k]),
                pltpu.make_async_copy(w.at[part], wbuf.at[part], sems.at[1, k]),
            ]
        )
        if with_dt:
            copies[-1].append(pltpu.make_async_copy(w_dt.at[:, part], refs[3].at[:, part], sems.at[2, k]))
        for copy in copies[-1]:
            copy.start()
    order = send_matrix(orow_ref[...].astype(F32), me_ref[0], n_pool, req, cr)
    total = jnp.zeros((hidden.shape[0], w.shape[1]), F32)
    if with_dt:
        total_dt = jnp.zeros((hidden.shape[0], w_dt.shape[0]), F32)
    for k in range(steps):
        for copy in copies[k]:
            copy.wait()
        rows = hbuf[:, k * chunk : (k + 1) * chunk]
        total = total + dot(rows, wbuf[k * chunk : (k + 1) * chunk])
        if with_dt:
            total_dt = total_dt + dot_t(rows, refs[3][:, k * chunk : (k + 1) * chunk])
    width = w.shape[1]
    placed = dot(order, total.astype(BF16)).astype(BF16)
    for s in range(n_pool):
        outs[s][:, :width] = placed[s * cr : (s + 1) * cr]
    if with_dt:
        heads = w_dt.shape[0]
        high = total_dt.astype(BF16)
        low = (total_dt - high.astype(F32)).astype(BF16)
        shape = (heads, 128)
        to_high = hot(iota(shape, 0) == iota(shape, 1))
        to_low = hot(iota(shape, 0) + heads == iota(shape, 1))
        pair = (dot(high, to_high) + dot(low, to_low)).astype(BF16)
        placed = dot(order, pair).astype(BF16)
        for s in range(n_pool):
            outs[s][:, width:] = placed[s * cr : (s + 1) * cr]


def project(me, orow, hidden, w, w_dt, n_pool, req, cr):
    tokens, depth = hidden.shape
    width = w.shape[1]
    chunk = min(512, depth)
    with_dt = w_dt is not None
    extra = 128 if with_dt else 0
    scratch = [
        pltpu.VMEM((tokens, depth), BF16),
        pltpu.VMEM((depth, width), BF16),
        pltpu.SemaphoreType.DMA((3, depth // chunk)),
    ]
    if with_dt:
        scratch.append(pltpu.VMEM((w_dt.shape[0], depth), BF16))
    streamed = [hidden, w] + ([w_dt] if with_dt else [])
    streamed = [pltpu.with_memory_space_constraint(v, pltpu.HBM) for v in streamed]
    return pl.pallas_call(
        functools.partial(project_kernel, n_pool, req, cr, chunk, with_dt),
        out_shape=[jax.ShapeDtypeStruct((cr, width + extra), BF16)] * n_pool,
        in_specs=[SMEM, VMEM] + [HBM] * len(streamed),
        out_specs=[VMEM] * n_pool,
        scratch_shapes=scratch,
        compiler_params=params(16),
        cost_estimate=cost(2 * tokens * depth * width, depth * (width + extra) * 2 + tokens * depth * 2),
    )(me, orow, *streamed)


def pick(rank, table):
    value = jnp.int32(table[0])
    for i in range(1, len(table)):
        value = jnp.where(rank == i, jnp.int32(table[i]), value)
    return value


def exchange_plan(n_tensor, width, span):
    piece = span * STATE
    per_group = HEADS // GROUPS
    head_local = HEADS // n_tensor
    edges, own = [], []
    for target in range(n_tensor):
        first = target * head_local // per_group
        for kind in range(2):
            column = (kind * GROUPS + first) * STATE
            source, part = column // width, column % width // piece
            (own if source == target else edges).append((source, target, kind, part))
    rounds = []
    for edge in edges:
        for one in rounds:
            if all(edge[0] != e[0] and edge[1] != e[1] for e in one):
                one.append(edge)
                break
        else:
            rounds.append([edge])
    return [own] + rounds


def bc_kernel(n_pool, req, cr, parts, me_ref, orow_ref, srow_ref, arow_ref, *refs):
    got, refs = refs[:n_pool], refs[n_pool:]
    pool_ref, weight_ref, dt_ref, kept_ref = refs[:4]
    outs, act_ref = refs[4:-1], refs[-1]
    slots, _, width = pool_ref.shape
    me, rank = me_ref[0], me_ref[1]
    orow, srow, arow = (r[...].astype(F32) for r in (orow_ref, srow_ref, arow_ref))
    order = owner_matrix(orow, srow, me, n_pool, req, cr, slots)
    accepts = slot_accepts(orow, srow, arow, me, slots)
    raw = dot(order, jnp.concatenate([g[...] for g in got], axis=0))
    summed, kept = conv_slots(raw[:, :width], pool_ref[...], weight_ref[...], accepts)
    act_ref[...] = silu(summed).astype(BF16)
    for table, out in zip(parts, outs):
        piece = out.shape[1]
        out[...] = act_ref[:, pl.ds(pl.multiple_of(pick(rank, table) * piece, 128), piece)]
    heads = dt_ref.shape[1]
    shape = (128, heads)
    lane = iota(shape, 0)
    head = iota(shape, 1)
    both = hot((lane == head) | (lane == head + heads))
    dt_ref[...] = dot(raw[:, width:].astype(BF16), both)
    kept_ref[...] = kept


def bc_stage(me, orow, srow, arow, got, pool, weight, heads, plan, span, n_pool, req, cr):
    slots, _, width = pool.shape
    rows = slots * DRAFT
    piece = span * STATE
    n_tensor = HEADS // heads
    parts = []
    for one in plan:
        table = [0] * n_tensor
        for source, _, _, part in one:
            table[source] = part
        parts.append(table)
    return pl.pallas_call(
        functools.partial(bc_kernel, n_pool, req, cr, parts),
        out_shape=[
            jax.ShapeDtypeStruct((rows, heads), F32),
            jax.ShapeDtypeStruct(pool.shape, BF16),
        ]
        + [jax.ShapeDtypeStruct((rows, piece), BF16)] * len(plan),
        in_specs=[SMEM] + [VMEM] * (n_pool + 5),
        out_specs=[VMEM] * (2 + len(plan)),
        scratch_shapes=[pltpu.VMEM((rows, width), BF16)],
        compiler_params=params(16),
        cost_estimate=cost(2e6, 1e6),
    )(me, orow, srow, arow, *got, pool, weight)


def mix_kernel(kinds, me_ref, orow_ref, srow_ref, arow_ref, *refs):
    pieces, refs = refs[: len(kinds)], refs[len(kinds) :]
    dt_ref, bias_ref, alog_ref, pool, y_ref, m_ref, w_ref, d_ref, b_ref, c_ref = refs
    slots, heads = pool.shape[:2]
    rows = slots * DRAFT
    span = b_ref.shape[1] // STATE
    per = heads // span
    for side, ref in enumerate((b_ref, c_ref)):
        ref[...] = pieces[0][...]
        for table, piece in zip(kinds, pieces):
            mine = [int(kind == side) for kind in table]
            if any(mine):

                @pl.when(pick(me_ref[1], mine) == 1)
                def _(ref=ref, piece=piece):
                    ref[...] = piece[...]

    orow, srow, arow = (r[...].astype(F32) for r in (orow_ref, srow_ref, arow_ref))
    accepts = slot_accepts(orow, srow, arow, me_ref[0], slots)
    x = dt_ref[...] + bias_ref[...]
    step = jnp.maximum(x, 0.0) + jnp.log1p(jnp.exp(-jnp.abs(x)))
    logs = -step * jnp.exp(alog_ref[...])
    position = iota((rows, heads), 0) & (DRAFT - 1)
    for back in (1, 2, 4):
        logs = logs + jnp.where(position >= back, pltpu.roll(logs, back, 0), 0.0)
    last = jnp.where(position.astype(F32) + 1 == accepts, logs, 0.0).reshape(slots, DRAFT, heads)
    last = jnp.broadcast_to(jnp.sum(last, axis=1, keepdims=True), (slots, DRAFT, heads))
    d_ref[...] = jnp.exp(last[:, 0, :])
    last = last.reshape(rows, heads)
    w_ref[...] = jnp.where(position.astype(F32) < accepts, jnp.exp(jnp.minimum(last - logs, 0.0)) * step, 0.0)
    eye = jnp.where(iota((rows, rows), 0) == iota((rows, rows), 1), 1.0, 0.0)

    def turned(v):
        return lax.dot_general(
            v, eye, (((0,), (0,)), ((), ())), preferred_element_type=F32, precision=lax.Precision.HIGHEST
        )

    logs_t, step_t = turned(logs), turned(step)
    sub, lane = iota((rows, rows), 0), iota((rows, rows), 1)
    causal = ((sub >> SHIFT) == (lane >> SHIFT)) & (lane <= sub)
    for g in range(span):
        part = slice(g * STATE, (g + 1) * STATE)
        pair = jnp.where(causal, dot_t(c_ref[:, part], b_ref[:, part]), 0.0)
        for h in range(g * per, (g + 1) * per):
            fade = jnp.exp(jnp.minimum(logs[:, h : h + 1] - logs_t[h : h + 1], 0.0))
            m_ref[h] = (pair * fade * step_t[h : h + 1]).astype(BF16)
    fade = spread(jnp.exp(logs), spread_matrix(heads))
    c = c_ref[...].astype(F32)
    for j in range(slots):
        here = slice(j * DRAFT, (j + 1) * DRAFT)
        for g in range(span):
            states = pool[j, g * per : (g + 1) * per].reshape(per * HEAD_DIM, STATE)
            columns = slice(g * per * HEAD_DIM, (g + 1) * per * HEAD_DIM)
            read = dot_t(c[here, g * STATE : (g + 1) * STATE].astype(BF16), states)
            y_ref[here, columns] = read * fade[here, columns]


def mix_stage(me, orow, srow, arow, pieces, dt, bias, a_log, pool, plan):
    slots, heads = pool.shape[:2]
    rows = slots * DRAFT
    n_tensor = HEADS // heads
    kinds = []
    for one in plan:
        table = [-1] * n_tensor
        for _, target, kind, _ in one:
            table[target] = kind
        kinds.append(table)
    return pl.pallas_call(
        functools.partial(mix_kernel, kinds),
        out_shape=[
            jax.ShapeDtypeStruct((rows, heads * HEAD_DIM), F32),
            jax.ShapeDtypeStruct((heads, rows, rows), BF16),
            jax.ShapeDtypeStruct((rows, heads), F32),
            jax.ShapeDtypeStruct((slots, heads), F32),
            jax.ShapeDtypeStruct(pieces[0].shape, BF16),
        ],
        in_specs=[SMEM] + [VMEM] * (7 + len(plan)),
        out_specs=[VMEM] * 5,
        scratch_shapes=[pltpu.VMEM(pieces[0].shape, BF16)],
        compiler_params=params(16),
        cost_estimate=cost(2 * rows * heads * HEAD_DIM * STATE, 2 * pool.size),
    )(me, orow, srow, arow, *pieces, dt, bias, a_log, pool)


def x_kernel(n_pool, req, cr, me_ref, orow_ref, srow_ref, arow_ref, *refs):
    got, refs = refs[:n_pool], refs[n_pool:]
    pool_ref, weight_ref, y_ref, m_ref, skip_ref, gain_ref = refs[:6]
    outs, (x_ref, kept_ref) = refs[6 : 6 + n_pool], refs[6 + n_pool :]
    slots, _, width = pool_ref.shape
    heads = width // HEAD_DIM
    me = me_ref[0]
    orow, srow, arow = (r[...].astype(F32) for r in (orow_ref, srow_ref, arow_ref))
    order = owner_matrix(orow, srow, me, n_pool, req, cr, slots)
    accepts = slot_accepts(orow, srow, arow, me, slots)
    raw = dot(order, jnp.concatenate([g[...] for g in got], axis=0))
    summed, kept = conv_slots(raw, pool_ref[...], weight_ref[...], accepts)
    kept_ref[...] = kept
    x = silu(summed)
    x_ref[...] = x
    matrix = spread_matrix(heads)
    small = x.astype(BF16)
    parts = [dot(m_ref[h], small[:, h * HEAD_DIM : (h + 1) * HEAD_DIM]) for h in range(heads)]
    y = jnp.concatenate(parts, axis=1) + y_ref[...] + spread(skip_ref[...], matrix) * x
    square = (y * y).astype(BF16)
    scale = lax.rsqrt(dot_t(square, matrix) * (1.0 / HEAD_DIM) + EPS)
    normed = (y * spread(scale, matrix) * gain_ref[...]).astype(BF16)
    back = return_matrix(orow, srow, me, n_pool, req, cr, slots)
    placed = dot(back, normed).astype(BF16)
    for s in range(n_pool):
        outs[s][...] = placed[s * cr : (s + 1) * cr]


def x_stage(me, orow, srow, arow, got, pool, weight, y, m, skip, gain, n_pool, req, cr):
    slots, _, width = pool.shape
    rows = slots * DRAFT
    return pl.pallas_call(
        functools.partial(x_kernel, n_pool, req, cr),
        out_shape=[jax.ShapeDtypeStruct((cr, width), BF16)] * n_pool
        + [jax.ShapeDtypeStruct((rows, width), F32), jax.ShapeDtypeStruct(pool.shape, BF16)],
        in_specs=[SMEM] + [VMEM] * (n_pool + 9),
        out_specs=[VMEM] * (n_pool + 2),
        compiler_params=params(32),
        cost_estimate=cost(2 * rows * rows * width, 4e6),
    )(me, orow, srow, arow, *got, pool, weight, y, m, skip, gain)


def state_kernel(d_ref, x_ref, w_ref, b_ref, pool, new_pool, buf, out_sems):
    slots, heads = pool.shape[:2]
    rows = slots * DRAFT
    span = b_ref.shape[1] // STATE
    per = heads // span
    backs = [pltpu.make_async_copy(buf.at[j], new_pool.at[j], out_sems.at[j]) for j in range(slots)]
    weighted = x_ref[...] * spread(w_ref[...], spread_matrix(heads))
    turned = weighted.T
    high = turned.astype(BF16)
    b = b_ref[...]
    slot = iota((rows, STATE), 0) >> SHIFT
    for j in range(slots):
        for g in range(span):
            rhs = jnp.where(slot == j, b[:, g * STATE : (g + 1) * STATE].astype(F32), 0.0).astype(BF16)
            added = dot(high[g * per * HEAD_DIM : (g + 1) * per * HEAD_DIM], rhs)
            for i in range(per):
                h = g * per + i
                kept = pool[j, h].astype(F32) * d_ref[j, h] + added[i * HEAD_DIM : (i + 1) * HEAD_DIM]
                buf[j, h] = kept.astype(BF16)
        backs[j].start()
    for copy in backs:
        copy.wait()


def state_stage(d, x, w, b, pool):
    slots = pool.shape[0]
    return pl.pallas_call(
        state_kernel,
        out_shape=jax.ShapeDtypeStruct(pool.shape, BF16),
        in_specs=[SMEM] + [VMEM] * 4,
        out_specs=HBM,
        scratch_shapes=[
            pltpu.VMEM(pool.shape, BF16),
            pltpu.SemaphoreType.DMA((slots,)),
        ],
        compiler_params=params(16),
        cost_estimate=cost(4 * pool.size * DRAFT, 4 * pool.size),
    )(d, x, w, b, pool)


def out_kernel(n_line, other_core, n_pool, req, cr, me_ref, orow_ref, *refs):
    n_got = n_pool if other_core else 1
    got, w, refs = refs[:n_got], refs[n_got], refs[n_got + 1 :]
    outs = refs[:n_line]
    width = outs[0].shape[1]
    rank = me_ref[1]
    core, line = rank & 1, rank >> 1
    if other_core:
        core = 1 - core
        collect = collect_matrix(orow_ref[...].astype(F32), me_ref[0], n_pool, req, cr)
        rows = dot(collect, jnp.concatenate([g[...] for g in got], axis=0)).astype(BF16)
        refs[n_line][...] = rows
    else:
        rows = got[0][...]
    for i in list(range(1, n_line)) + [0]:
        there = line + i
        there = jnp.where(there >= n_line, there - n_line, there)
        column = pl.multiple_of((2 * there + core) * width, 128)
        outs[i][...] = dot(rows, w[:, pl.ds(column, width)]).astype(outs[i].dtype)


def out_stage(me, orow, got, w, n_line, other_core, n_pool, req, cr):
    depth, total = w.shape
    width = total // (2 * n_line)
    tokens = req * DRAFT
    kind = BF16 if other_core else F32
    shapes = [jax.ShapeDtypeStruct((tokens, width), kind)] * n_line
    if other_core:
        shapes = shapes + [jax.ShapeDtypeStruct((tokens, depth), BF16)]
    return pl.pallas_call(
        functools.partial(out_kernel, n_line, other_core, n_pool, req, cr),
        out_shape=shapes,
        in_specs=[SMEM] + [VMEM] * (len(got) + 2),
        out_specs=[VMEM] * len(shapes),
        compiler_params=params(16),
        cost_estimate=cost(tokens * depth * total, depth * total),
    )(me, orow, *got, w)


def body(
    hidden,
    w_x,
    w_bc,
    w_dt,
    conv_x,
    conv_bc,
    dt_bias,
    a_log,
    d_skip,
    norm_gain,
    w_out,
    ssm_pool,
    conv_pool_x,
    conv_pool_bc,
    owners,
    slots,
    accepted,
):
    n_pool = lax.axis_size("pool")
    n_tensor = lax.axis_size("tensor")
    n_line = n_tensor // 2
    me = jnp.stack([lax.axis_index(axis).astype(jnp.int32) for axis in ("pool", "tensor")])
    req = hidden.shape[0] // DRAFT
    share = req // n_pool
    capacity = share + share // 2
    cr = -(-capacity * DRAFT // 16) * 16
    head_local = w_dt.shape[1]
    span = max(1, head_local // (HEADS // GROUPS))
    orow, srow, arow = (v.reshape(1, -1) for v in (owners, slots, accepted))

    def row(v):
        return v.reshape(1, -1)

    def to_owner(parts):
        return [parts[0]] + [
            lax.ppermute(parts[s], "pool", [(i, (i + s) % n_pool) for i in range(n_pool)]) for s in range(1, n_pool)
        ]

    def to_requester(parts):
        return [parts[0]] + [
            lax.ppermute(parts[s], "pool", [((i + s) % n_pool, i) for i in range(n_pool)]) for s in range(1, n_pool)
        ]

    bc_sent = project(me, orow, hidden, w_bc, w_dt.T, n_pool, req, cr)
    bc_got = to_owner(bc_sent)
    x_sent = project(me, orow, hidden, w_x, None, n_pool, req, cr)
    x_got = to_owner(x_sent)
    bc_got, _ = lax.optimization_barrier((bc_got, x_sent))
    plan = exchange_plan(n_tensor, w_bc.shape[1], span)
    stage = bc_stage(
        me, orow, srow, arow, bc_got, conv_pool_bc, conv_bc, head_local, plan, span, n_pool, req, cr
    )
    dt, new_conv_bc, pieces = stage[0], stage[1], list(stage[2:])
    for i in range(1, len(plan)):
        pieces[i] = lax.ppermute(pieces[i], "tensor", [(e[0], e[1]) for e in plan[i]])
    y, m, w, d, b = mix_stage(me, orow, srow, arow, pieces, dt, row(dt_bias), row(a_log), ssm_pool, plan)
    stage = x_stage(
        me, orow, srow, arow, x_got, conv_pool_x, conv_x, y, m, row(d_skip), row(norm_gain), n_pool, req, cr
    )
    normed_sent, (x, new_conv_x) = stage[:n_pool], stage[n_pool:]
    normed_got = to_requester(normed_sent)
    new_pool = state_stage(d, x, w, b, ssm_pool)
    normed_got, _ = lax.optimization_barrier((normed_got, new_pool))
    sends = out_stage(me, orow, normed_got, w_out, n_line, True, n_pool, req, cr)
    sends, normed = sends[:n_line], sends[n_line]
    swap = [(i, i ^ 1) for i in range(n_tensor)]
    order = list(range(1, n_line)) + [0]
    core_got = {i: lax.ppermute(sends[i], "tensor", swap) for i in order}
    keeps = out_stage(me, orow, [normed], w_out, n_line, False, n_pool, req, cr)
    mixed = None
    arrived = []
    for i in range(1, n_line):
        ahead = (keeps[i] + core_got[i].astype(F32)).astype(BF16)
        pairs = [(r, ((r // 2 + i) % n_line) * 2 + r % 2) for r in range(n_tensor)]
        arrived.append(lax.ppermute(ahead, "tensor", pairs))
    mixed = keeps[0] + core_got[0].astype(F32)
    for one in arrived:
        mixed = mixed + one.astype(F32)
    return (mixed.astype(BF16), new_pool, new_conv_x, new_conv_bc)


def solution(mesh):
    in_specs = (
        P(("groups", "pool"), None),
        P(None, "tensor"),
        P(None, "tensor"),
        P(None, "tensor"),
        P(None, "tensor"),
        P(None, "tensor"),
        P("tensor"),
        P("tensor"),
        P("tensor"),
        P("tensor"),
        P("tensor", None),
        P(("groups", "pool"), "tensor", None, None),
        P(("groups", "pool"), None, "tensor"),
        P(("groups", "pool"), None, "tensor"),
        P("groups"),
        P("groups"),
        P("groups"),
    )
    out_specs = (
        P(("groups", "pool"), "tensor"),
        P(("groups", "pool"), "tensor", None, None),
        P(("groups", "pool"), None, "tensor"),
        P(("groups", "pool"), None, "tensor"),
    )
    return jax.shard_map(body, mesh=mesh, in_specs=in_specs, out_specs=out_specs, check_vma=False)
```

```python
import functools

import jax
import jax.numpy as jnp
from jax import lax
from jax.experimental import pallas as pl
from jax.experimental.pallas import tpu as pltpu
from jax.sharding import PartitionSpec as P

HEADS = 64
HEAD_DIM = 64
STATE = 128
GROUPS = 8
DRAFT = 8
SHIFT = 3
EPS = 1e-05
FAR = 4096.0

F32 = jnp.float32
BF16 = jnp.bfloat16
ANY = pl.BlockSpec(memory_space=pl.ANY)
HBM = pl.BlockSpec(memory_space=pltpu.HBM)
VMEM = pl.BlockSpec(memory_space=pltpu.VMEM)
SMEM = pl.BlockSpec(memory_space=pltpu.SMEM)


def params(mib, **more):
    return pltpu.CompilerParams(vmem_limit_bytes=mib * 2**20, **more)


def cost(flops, moved):
    return pl.CostEstimate(flops=int(flops), bytes_accessed=int(moved), transcendentals=0)


def iota(shape, dim):
    return lax.broadcasted_iota(jnp.int32, shape, dim)


def dot(a, b):
    return jnp.dot(a, b, preferred_element_type=F32)


def dot_t(a, b):
    return lax.dot_general(a, b, (((1,), (1,)), ((), ())), preferred_element_type=F32)


def as_col(row):
    n = row.shape[1]
    eye = iota((n, n), 0) == iota((n, n), 1)
    return jnp.sum(jnp.where(eye, jnp.broadcast_to(row, (n, n)), 0.0), axis=1, keepdims=True)


def wrap(value, n):
    return jnp.where(value < 0, value + n, value)


def block_shift(req):
    return req.bit_length() - 1


def ranks(orow, ocol, req):
    n = orow.shape[1]
    sub, lane = iota((n, n), 0), iota((n, n), 1)
    sh = block_shift(req)
    same = (ocol == orow) & ((sub >> sh) == (lane >> sh))
    row = jnp.sum(jnp.where(same & (sub < lane), 1.0, 0.0), axis=0, keepdims=True)
    col = jnp.sum(jnp.where(same & (lane < sub), 1.0, 0.0), axis=1, keepdims=True)
    return row, col


def hot(mask):
    return jnp.where(mask, 1.0, 0.0).astype(BF16)


def send_matrix(orow, me, n_pool, req, cr):
    ocol = as_col(orow)
    _, rank_col = ranks(orow, ocol, req)
    total, tokens = orow.shape[1], req * DRAFT
    place_col = wrap(ocol - me.astype(F32), n_pool) * cr + rank_col * DRAFT
    token = iota((total, tokens), 1)
    mine = (iota((total, tokens), 0) - me * req) == (token >> SHIFT)
    place = jnp.sum(jnp.where(mine, jnp.broadcast_to(place_col, (total, tokens)), 0.0), axis=0, keepdims=True)
    place = place + (iota((1, tokens), 1) & (DRAFT - 1)).astype(F32)
    return hot(iota((n_pool * cr, tokens), 0).astype(F32) == place)


def collect_matrix(orow, me, n_pool, req, cr):
    ocol = as_col(orow)
    rank_row, _ = ranks(orow, ocol, req)
    total, tokens = orow.shape[1], req * DRAFT
    place_row = wrap(orow - me.astype(F32), n_pool) * cr + rank_row * DRAFT
    token = iota((tokens, total), 0)
    mine = (iota((tokens, total), 1) - me * req) == (token >> SHIFT)
    place = jnp.sum(jnp.where(mine, jnp.broadcast_to(place_row, (tokens, total)), 0.0), axis=1, keepdims=True)
    place = place + (iota((tokens, 1), 0) & (DRAFT - 1)).astype(F32)
    return hot(iota((tokens, n_pool * cr), 1).astype(F32) == place)


def owner_matrix(orow, srow, me, n_pool, req, cr, slots):
    ocol = as_col(orow)
    rank_row, _ = ranks(orow, ocol, req)
    total, rows = orow.shape[1], slots * DRAFT
    block = (iota((1, total), 1) >> block_shift(req)).astype(F32)
    place_row = wrap(me.astype(F32) - block, n_pool) * cr + rank_row * DRAFT + FAR
    slot = (iota((rows, total), 0) >> SHIFT).astype(F32)
    match = (orow == me.astype(F32)) & (srow == slot)
    place = jnp.sum(jnp.where(match, jnp.broadcast_to(place_row, (rows, total)), 0.0), axis=1, keepdims=True)
    place = place - FAR + (iota((rows, 1), 0) & (DRAFT - 1)).astype(F32)
    return hot(iota((rows, n_pool * cr), 1).astype(F32) == place)


def pack_matrices(orow, srow, me, n_pool, req, cr, slots):
    ocol, scol = as_col(orow), as_col(srow)
    _, rank_col = ranks(orow, ocol, req)
    total, rows, tokens = orow.shape[1], slots * DRAFT, req * DRAFT
    mine = me.astype(F32)
    sub, lane = iota((total, total), 0), iota((total, total), 1)
    index = jnp.sum(jnp.where((orow == mine) & (lane < sub), 1.0, 0.0), axis=1, keepdims=True)
    slot = (iota((total, rows), 1) >> SHIFT).astype(F32)
    match = (ocol == mine) & (scol == slot)
    value = jnp.broadcast_to(index * DRAFT + FAR, (total, rows))
    at = jnp.sum(jnp.where(match, value, 0.0), axis=0, keepdims=True) - FAR
    at = at + (iota((1, rows), 1) & (DRAFT - 1)).astype(F32)
    pack = hot(iota((tokens, rows), 0).astype(F32) == at)
    block = (iota((total, 1), 0) >> block_shift(req)).astype(F32)
    place_col = wrap(mine - block, n_pool) * cr + rank_col * DRAFT + FAR
    match = (ocol == mine) & (index == (iota((total, tokens), 1) >> SHIFT).astype(F32))
    at = jnp.sum(jnp.where(match, jnp.broadcast_to(place_col, (total, tokens)), 0.0), axis=0, keepdims=True) - FAR
    at = at + (iota((1, tokens), 1) & (DRAFT - 1)).astype(F32)
    return pack, hot(iota((n_pool * cr, tokens), 0).astype(F32) == at)


def slot_accepts(orow, srow, arow, me, slots):
    total, rows = orow.shape[1], slots * DRAFT
    slot = (iota((rows, total), 0) >> SHIFT).astype(F32)
    match = (orow == me.astype(F32)) & (srow == slot)
    return jnp.sum(jnp.where(match, jnp.broadcast_to(arow, (rows, total)), 0.0), axis=1, keepdims=True)


def padded_pool(pool, width):
    slots, window, _ = pool.shape
    old = jnp.concatenate([pool.astype(F32), jnp.zeros((slots, DRAFT - window, width), F32)], axis=1)
    return old.reshape(slots * DRAFT, width)


def conv_slots(raw, pool, weight):
    rows, width = raw.shape
    window = pool.shape[1]
    old = padded_pool(pool, width)
    position = iota((rows, width), 0) & (DRAFT - 1)
    summed = weight[window] * raw
    for back in range(1, window + 1):
        new_part = pltpu.roll(raw, back, 0)
        old_part = pltpu.roll(old, (back - window) % rows, 0)
        summed = summed + weight[window - back] * jnp.where(position < back, old_part, new_part)
    return summed


def kept_rows(raw, pool, accepts):
    rows, width = raw.shape
    slots, window, _ = pool.shape
    old = padded_pool(pool, width)
    sub, lane = iota((rows, rows), 0), iota((rows, rows), 1)
    here = (sub >> SHIFT) == (lane >> SHIFT)
    at = (sub & (DRAFT - 1)).astype(F32) + accepts
    source = (lane & (DRAFT - 1)).astype(F32)
    from_old = hot(here & (source == at) & (source < window))
    from_new = hot(here & (source + window == at))
    kept = dot(from_old, old.astype(BF16)) + dot(from_new, raw.astype(BF16))
    return kept.astype(BF16).reshape(slots, DRAFT, width)[:, :window]


def silu(v):
    return v / (1.0 + jnp.exp(-v))


def spread_matrix(heads):
    shape = (heads, heads * HEAD_DIM)
    return hot(iota(shape, 0) == (iota(shape, 1) >> 6))


def spread(values, matrix):
    high = values.astype(BF16)
    low = (values - high.astype(F32)).astype(BF16)
    return dot(high, matrix) + dot(low, matrix)


def dma(pairs, sems, row):
    return [pltpu.make_async_copy(src, dst, sems.at[row, k]) for k, (src, dst) in enumerate(pairs)]


def project_bc_kernel(n_pool, req, cr, chunk, slots, owners, places, takes, hidden, w, w_dt, *refs):
    outs, refs = refs[:n_pool], refs[n_pool:]
    hbuf, send_ref, owner_ref, pack_ref, return_ref, collect_ref, accepts_ref = refs[:7]
    meta_buf, wbuf, dt_buf, sems = refs[7:]
    steps = hidden.shape[1] // chunk
    parts = [pl.ds(k * chunk, chunk) for k in range(steps)]
    copies = list(
        zip(
            dma([(hidden.at[:, p], hbuf.at[:, p]) for p in parts], sems, 0),
            dma([(w.at[p], wbuf.at[p]) for p in parts], sems, 1),
            dma([(w_dt.at[:, p], dt_buf.at[:, p]) for p in parts], sems, 2),
        )
    )
    tables = dma([(v, meta_buf.at[i]) for i, v in enumerate((owners, places, takes))], sems, 3)
    for copy in tables:
        copy.start()
    for group in copies:
        for copy in group:
            copy.start()
    for copy in tables:
        copy.wait()
    me = lax.axis_index("pool").astype(jnp.int32)
    orow, srow, arow = (meta_buf[i].astype(F32) for i in range(3))
    order = send_matrix(orow, me, n_pool, req, cr)
    send_ref[...] = order
    owner_ref[...] = owner_matrix(orow, srow, me, n_pool, req, cr, slots)
    pack_ref[...], return_ref[...] = pack_matrices(orow, srow, me, n_pool, req, cr, slots)
    collect_ref[...] = collect_matrix(orow, me, n_pool, req, cr)
    accepts_ref[...] = slot_accepts(orow, srow, arow, me, slots)
    heads = w_dt.shape[0]
    total, total_dt = None, None
    for k in range(steps):
        for copy in copies[k]:
            copy.wait()
        here = slice(k * chunk, (k + 1) * chunk)
        added, added_dt = dot(hbuf[:, here], wbuf[here]), dot_t(hbuf[:, here], dt_buf[:, here])
        total = added if total is None else total + added
        total_dt = added_dt if total_dt is None else total_dt + added_dt
    width = w.shape[1]
    placed = dot(order, total.astype(BF16)).astype(BF16)
    high = total_dt.astype(BF16)
    low = (total_dt - high.astype(F32)).astype(BF16)
    shape = (heads, 128)
    to_high = hot(iota(shape, 0) == iota(shape, 1))
    to_low = hot(iota(shape, 0) + heads == iota(shape, 1))
    pair = (dot(high, to_high) + dot(low, to_low)).astype(BF16)
    placed_dt = dot(order, pair).astype(BF16)
    for s in range(n_pool):
        outs[s][:, :width] = placed[s * cr : (s + 1) * cr]
        outs[s][:, width:] = placed_dt[s * cr : (s + 1) * cr]


def in_hbm(*arrays):
    return [pltpu.with_memory_space_constraint(v, pltpu.HBM) for v in arrays]


def project_bc(tables, hidden, w, w_dt, slots, n_pool, req, cr):
    tokens, depth = hidden.shape
    chunk = min(512, depth)
    width, rows = w.shape[1], slots * DRAFT
    outs = pl.pallas_call(
        functools.partial(project_bc_kernel, n_pool, req, cr, chunk, slots),
        out_shape=[jax.ShapeDtypeStruct((cr, width + 128), BF16)] * n_pool
        + [
            jax.ShapeDtypeStruct((tokens, depth), BF16),
            jax.ShapeDtypeStruct((n_pool * cr, tokens), BF16),
            jax.ShapeDtypeStruct((rows, n_pool * cr), BF16),
            jax.ShapeDtypeStruct((tokens, rows), BF16),
            jax.ShapeDtypeStruct((n_pool * cr, tokens), BF16),
            jax.ShapeDtypeStruct((tokens, n_pool * cr), BF16),
            jax.ShapeDtypeStruct((rows, 1), F32),
        ],
        in_specs=[HBM] * 6,
        out_specs=[VMEM] * (n_pool + 7),
        scratch_shapes=[
            pltpu.VMEM((3,) + tables[0].shape, jnp.int32),
            pltpu.VMEM((depth, width), BF16),
            pltpu.VMEM(w_dt.shape, BF16),
            pltpu.SemaphoreType.DMA((4, max(3, depth // chunk))),
        ],
        compiler_params=params(12),
        cost_estimate=cost(2 * tokens * depth * width, depth * (width + 128 + tokens) * 2),
    )(*in_hbm(*tables, hidden, w, w_dt))
    return outs[:n_pool], outs[n_pool:]


def project_x_kernel(n_pool, cr, chunk, hbuf, w, send_ref, *refs):
    outs, (wbuf, sems) = refs[:n_pool], refs[n_pool:]
    steps = w.shape[0] // chunk
    parts = [pl.ds(k * chunk, chunk) for k in range(steps)]
    copies = dma([(w.at[p], wbuf.at[p]) for p in parts], sems, 0)
    for copy in copies:
        copy.start()
    total = None
    for k in range(steps):
        copies[k].wait()
        here = slice(k * chunk, (k + 1) * chunk)
        added = dot(hbuf[:, here], wbuf[here])
        total = added if total is None else total + added
    placed = dot(send_ref[...], total.astype(BF16)).astype(BF16)
    for s in range(n_pool):
        outs[s][...] = placed[s * cr : (s + 1) * cr]


def project_x(hidden, w, send, n_pool, cr):
    tokens, depth = hidden.shape
    chunk = min(512, depth)
    width = w.shape[1]
    return pl.pallas_call(
        functools.partial(project_x_kernel, n_pool, cr, chunk),
        out_shape=[jax.ShapeDtypeStruct((cr, width), BF16)] * n_pool,
        in_specs=[VMEM, HBM, VMEM],
        out_specs=[VMEM] * n_pool,
        scratch_shapes=[
            pltpu.VMEM((depth, width), BF16),
            pltpu.SemaphoreType.DMA((1, depth // chunk)),
        ],
        compiler_params=params(14),
        cost_estimate=cost(2 * tokens * depth * width, depth * (width + tokens) * 2),
    )(hidden, *in_hbm(w), send)


def pick(rank, table):
    value = jnp.int32(table[0])
    for i in range(1, len(table)):
        value = jnp.where(rank == i, jnp.int32(table[i]), value)
    return value


def exchange_plan(n_tensor, width, span):
    piece = span * STATE
    per_group = HEADS // GROUPS
    head_local = HEADS // n_tensor
    edges, own = [], []
    for target in range(n_tensor):
        first = target * head_local // per_group
        for kind in range(2):
            column = (kind * GROUPS + first) * STATE
            source, part = column // width, column % width // piece
            (own if source == target else edges).append((source, target, kind, part))
    rounds = []
    while edges:
        best = matching(edges, n_tensor)
        rounds.append(best)
        edges = [e for e in edges if e not in best]
    return [own] + rounds


def completed(edges, n):
    pairs = [(e[0], e[1]) for e in edges]
    sources = [i for i in range(n) if i not in [p[0] for p in pairs]]
    targets = [i for i in reversed(range(n)) if i not in [p[1] for p in pairs]]
    return pairs + list(zip(sources, targets))


def matching(edges, n):
    held = {}

    def place(source, seen):
        for edge in edges:
            if edge[0] == source and edge[1] not in seen:
                seen.add(edge[1])
                if edge[1] not in held or place(held[edge[1]][0], seen):
                    held[edge[1]] = edge
                    return True
        return False

    for source in range(n):
        place(source, set())
    return [held[target] for target in sorted(held)]


def bc_kernel(n_pool, parts, owner_ref, *refs):
    got, refs = refs[:n_pool], refs[n_pool:]
    pool_ref, weight_ref, raw_ref = refs[:3]
    outs, act_ref = refs[3:-1], refs[-1]
    width = pool_ref.shape[2]
    rank = lax.axis_index("tensor").astype(jnp.int32)
    raw = dot(owner_ref[...], jnp.concatenate([g[...] for g in got], axis=0))
    raw_ref[...] = raw
    act_ref[...] = silu(conv_slots(raw[:, :width], pool_ref[...], weight_ref[...])).astype(BF16)
    for table, out in zip(parts, outs):
        piece = out.shape[1]
        out[...] = act_ref[:, pl.ds(pl.multiple_of(pick(rank, table) * piece, 128), piece)]


def bc_stage(owner, got, pool, weight, plan, span, n_pool, n_tensor):
    slots, _, width = pool.shape
    rows = slots * DRAFT
    piece = span * STATE
    parts = []
    for one in plan:
        table = [0] * n_tensor
        for source, _, _, part in one:
            table[source] = part
        parts.append(table)
    return pl.pallas_call(
        functools.partial(bc_kernel, n_pool, parts),
        out_shape=[jax.ShapeDtypeStruct((rows, width + 128), F32)]
        + [jax.ShapeDtypeStruct((rows, piece), BF16)] * len(plan),
        in_specs=[VMEM] * (n_pool + 3),
        out_specs=[VMEM] * (1 + len(plan)),
        scratch_shapes=[pltpu.VMEM((rows, width), BF16)],
        compiler_params=params(8),
        cost_estimate=cost(2e6, 1e6),
    )(owner, *got, pool, weight)


def pre_kernel(accepts_ref, raw_ref, bias_ref, alog_ref, pool, m_ref, fade_ref, w_ref, d_ref, states, sems):
    slots, heads = pool.shape[:2]
    rows = slots * DRAFT
    copies = [pltpu.make_async_copy(pool.at[j], states.at[j], sems.at[j]) for j in range(slots)]
    for copy in copies:
        copy.start()
    accepts = accepts_ref[...]
    width = raw_ref.shape[1] - 128
    shape = (128, heads)
    lane, head = iota(shape, 0), iota(shape, 1)
    both = hot((lane == head) | (lane == head + heads))
    x = dot(raw_ref[:, width:].astype(BF16), both) + bias_ref[...]
    step = jnp.maximum(x, 0.0) + jnp.log1p(jnp.exp(-jnp.abs(x)))
    logs = -step * jnp.exp(alog_ref[...])
    position = iota((rows, heads), 0) & (DRAFT - 1)
    for back in (1, 2, 4):
        logs = logs + jnp.where(position >= back, pltpu.roll(logs, back, 0), 0.0)
    last = jnp.where(position.astype(F32) + 1 == accepts, logs, 0.0).reshape(slots, DRAFT, heads)
    last = jnp.broadcast_to(jnp.sum(last, axis=1, keepdims=True), (slots, DRAFT, heads))
    d_ref[...] = jnp.exp(last[:, 0, :])
    last = last.reshape(rows, heads)
    w_ref[...] = jnp.where(position.astype(F32) < accepts, jnp.exp(jnp.minimum(last - logs, 0.0)) * step, 0.0)
    lanes = heads * DRAFT
    shape = (heads, lanes)
    repeat = jnp.where(iota(shape, 0) == (iota(shape, 1) >> SHIFT), 1.0, 0.0)

    def wide(v):
        return jnp.dot(v, repeat, preferred_element_type=F32, precision=lax.Precision.HIGHEST)

    t, u = iota((rows, lanes), 0) & (DRAFT - 1), iota((rows, lanes), 1) & (DRAFT - 1)

    def at_u(v):
        v = jnp.where(t == u, v, 0.0).reshape(slots, DRAFT, lanes)
        return jnp.broadcast_to(jnp.sum(v, axis=1, keepdims=True), (slots, DRAFT, lanes)).reshape(rows, lanes)

    wide_logs = wide(logs)
    fade = jnp.where(u <= t, jnp.exp(jnp.minimum(wide_logs - at_u(wide_logs), 0.0)) * at_u(wide(step)), 0.0)
    fade = fade.astype(BF16)
    shape = (lanes, rows)
    same = (iota(shape, 0) & (DRAFT - 1)) == (iota(shape, 1) & (DRAFT - 1))
    head = iota(shape, 0) >> SHIFT
    for h in range(heads):
        m_ref[h] = dot(fade, hot(same & (head == h))).astype(BF16)
    fade_ref[...] = spread(jnp.exp(logs), spread_matrix(heads))
    for copy in copies:
        copy.wait()


def pre_stage(accepts, raw, bias, a_log, pool):
    slots, heads = pool.shape[:2]
    rows = slots * DRAFT
    return pl.pallas_call(
        pre_kernel,
        out_shape=[
            jax.ShapeDtypeStruct((heads, rows, rows), BF16),
            jax.ShapeDtypeStruct((rows, heads * HEAD_DIM), F32),
            jax.ShapeDtypeStruct((rows, heads), F32),
            jax.ShapeDtypeStruct((slots, heads), F32),
            jax.ShapeDtypeStruct(pool.shape, BF16),
        ],
        in_specs=[VMEM] * 4 + [HBM],
        out_specs=[VMEM] * 5,
        scratch_shapes=[pltpu.SemaphoreType.DMA((slots,))],
        compiler_params=params(20),
        cost_estimate=cost(1e6, 2 * pool.size),
    )(accepts, raw, bias, a_log, *in_hbm(pool))


def mix_kernel(kinds, fade_m_ref, fade_ref, states, *refs):
    pieces, (y_ref, m_ref, b_ref, c_ref) = refs[: len(kinds)], refs[len(kinds) :]
    slots, heads = states.shape[:2]
    span = b_ref.shape[1] // STATE
    per = heads // span
    rank = lax.axis_index("tensor").astype(jnp.int32)
    for side, ref in enumerate((b_ref, c_ref)):
        ref[...] = pieces[0][...]
        for table, piece in zip(kinds, pieces):
            mine = [int(kind == side) for kind in table]
            if any(mine):

                @pl.when(pick(rank, mine) == 1)
                def _(ref=ref, piece=piece):
                    ref[...] = piece[...]

    rows = slots * DRAFT
    here = (iota((rows, rows), 0) >> SHIFT) == (iota((rows, rows), 1) >> SHIFT)
    for g in range(span):
        part = slice(g * STATE, (g + 1) * STATE)
        pair = jnp.where(here, dot_t(c_ref[:, part], b_ref[:, part]), 0.0)
        for h in range(g * per, (g + 1) * per):
            m_ref[h] = (pair * fade_m_ref[h].astype(F32)).astype(BF16)
    c = c_ref[...].astype(F32)
    for j in range(slots):
        here = slice(j * DRAFT, (j + 1) * DRAFT)
        for g in range(span):
            old = states[j, g * per : (g + 1) * per].reshape(per * HEAD_DIM, STATE)
            columns = slice(g * per * HEAD_DIM, (g + 1) * per * HEAD_DIM)
            read = dot_t(c[here, g * STATE : (g + 1) * STATE].astype(BF16), old)
            y_ref[here, columns] = read * fade_ref[here, columns]


def mix_stage(fade_m, fade, states, pieces, plan, n_tensor):
    slots, heads = states.shape[:2]
    rows = slots * DRAFT
    kinds = []
    for one in plan:
        table = [-1] * n_tensor
        for _, target, kind, _ in one:
            table[target] = kind
        kinds.append(table)
    return pl.pallas_call(
        functools.partial(mix_kernel, kinds),
        out_shape=[
            jax.ShapeDtypeStruct((rows, heads * HEAD_DIM), F32),
            jax.ShapeDtypeStruct((heads, rows, rows), BF16),
            jax.ShapeDtypeStruct(pieces[0].shape, BF16),
        ],
        in_specs=[VMEM] * (3 + len(plan)),
        out_specs=[VMEM] * 3,
        scratch_shapes=[pltpu.VMEM(pieces[0].shape, BF16)],
        compiler_params=params(8),
        cost_estimate=cost(2 * rows * heads * HEAD_DIM * STATE, 2 * states.size),
    )(fade_m, fade, states, *pieces)


def x_kernel(n_pool, owner_ref, pack_ref, *refs):
    got, refs = refs[:n_pool], refs[n_pool:]
    pool_ref, weight_ref, y_ref, m_ref, skip_ref, gain_ref = refs[:6]
    normed_ref, x_ref, raw_ref = refs[6:]
    heads = pool_ref.shape[2] // HEAD_DIM
    raw = dot(owner_ref[...], jnp.concatenate([g[...] for g in got], axis=0))
    raw_ref[...] = raw
    x = silu(conv_slots(raw, pool_ref[...], weight_ref[...]))
    x_ref[...] = x
    matrix = spread_matrix(heads)
    small = x.astype(BF16)
    parts = [dot(m_ref[h], small[:, h * HEAD_DIM : (h + 1) * HEAD_DIM]) for h in range(heads)]
    y = jnp.concatenate(parts, axis=1) + y_ref[...] + spread(skip_ref[...], matrix) * x
    square = (y * y).astype(BF16)
    scale = lax.rsqrt(dot_t(square, matrix) * (1.0 / HEAD_DIM) + EPS)
    normed = (y * spread(scale, matrix) * gain_ref[...]).astype(BF16)
    normed_ref[...] = dot(pack_ref[...], normed).astype(BF16)


def x_stage(owner, pack, got, pool, weight, y, m, skip, gain, n_pool):
    slots, _, width = pool.shape
    rows = slots * DRAFT
    return pl.pallas_call(
        functools.partial(x_kernel, n_pool),
        out_shape=[jax.ShapeDtypeStruct((pack.shape[0], width), BF16)] + [jax.ShapeDtypeStruct((rows, width), F32)] * 2,
        in_specs=[VMEM] * (n_pool + 8),
        out_specs=[VMEM] * 3,
        compiler_params=params(16),
        cost_estimate=cost(2 * rows * rows * width, 4e6),
    )(owner, pack, *got, pool, weight, y, m, skip, gain)


def state_kernel(span_of, again, d_ref, x_ref, w_ref, b_ref, pool, accepts_ref, raws, convs, *refs):
    new_pool, kepts, buf, out_sems = refs[1:] if again else refs
    slots, heads = pool.shape[:2]
    rows = slots * DRAFT
    span = b_ref.shape[1] // STATE
    per = heads // span
    backs = {j: pltpu.make_async_copy(buf.at[j], new_pool.at[j], out_sems.at[j]) for j in span_of}
    weighted = x_ref[...] * spread(w_ref[...], spread_matrix(heads))
    high = weighted.T.astype(BF16)
    b = b_ref[...]
    slot = iota((rows, STATE), 0) >> SHIFT
    for j in span_of:
        for g in range(span):
            rhs = jnp.where(slot == j, b[:, g * STATE : (g + 1) * STATE].astype(F32), 0.0).astype(BF16)
            added = dot(high[g * per * HEAD_DIM : (g + 1) * per * HEAD_DIM], rhs)
            for i in range(per):
                h = g * per + i
                kept = pool[j, h].astype(F32) * d_ref[j, h] + added[i * HEAD_DIM : (i + 1) * HEAD_DIM]
                buf[j, h] = kept.astype(BF16)
        backs[j].start()
    for raw, conv, kept in zip(raws, convs, kepts):
        kept[...] = kept_rows(raw[:, : conv.shape[2]], conv[...], accepts_ref[...])
    for copy in backs.values():
        copy.wait()


def state_stage(span_of, d, x, w, b, pool, accepts, raws, convs, begun):
    slots = pool.shape[0]
    again = begun is not None
    operands = [d, x, w, b, pool, accepts, raws, convs] + ([begun] if again else [])
    at = 6 + len(raws) + len(convs)
    return pl.pallas_call(
        functools.partial(state_kernel, span_of, again),
        out_shape=[jax.ShapeDtypeStruct(pool.shape, BF16), [jax.ShapeDtypeStruct(v.shape, BF16) for v in convs]],
        in_specs=[SMEM] + [VMEM] * 5 + [[VMEM] * len(raws), [VMEM] * len(convs)] + ([HBM] if again else []),
        out_specs=[HBM, [VMEM] * len(convs)],
        scratch_shapes=[
            pltpu.VMEM(pool.shape, BF16),
            pltpu.SemaphoreType.DMA((slots,)),
        ],
        input_output_aliases={at: 0} if again else {},
        compiler_params=params(16),
        cost_estimate=cost(2 * pool.size * DRAFT, 2 * pool.size),
    )(*operands)


def out_kernel(chunks, n_line, other_core, rows, w, *outs):
    width = outs[0].shape[1]
    rank = lax.axis_index("tensor").astype(jnp.int32)
    core, line = rank & 1, rank >> 1
    if other_core:
        core = 1 - core
    for i, out in zip(chunks, outs):
        there = line + i
        there = jnp.where(there >= n_line, there - n_line, there)
        column = pl.multiple_of((2 * there + core) * width, 128)
        out[...] = dot(rows[...], w[:, pl.ds(column, width)]).astype(out.dtype)


def out_stage(rows, w, chunks, n_line, other_core):
    depth, total = w.shape
    width = total // (2 * n_line)
    tokens = rows.shape[0]
    return pl.pallas_call(
        functools.partial(out_kernel, chunks, n_line, other_core),
        out_shape=[jax.ShapeDtypeStruct((tokens, width), BF16 if other_core else F32)] * len(chunks),
        in_specs=[VMEM] * 2,
        out_specs=[VMEM] * len(chunks),
        compiler_params=params(8),
        cost_estimate=cost(2 * tokens * depth * width * len(chunks), 2 * depth * width * len(chunks)),
    )(rows, w)


def place_kernel(part, n_pool, cr, keep, core, return_ref, *refs):
    arrived, outs = refs[:-n_pool], refs[-n_pool:]
    total = keep[:, part] + core[:, part].astype(F32)
    for one in arrived:
        total = total + one[...].astype(F32)
    placed = dot(return_ref[...], total.astype(BF16)).astype(BF16)
    for s in range(n_pool):
        outs[s][...] = placed[s * cr : (s + 1) * cr]


def place_stage(part, keep, core, back, arrived, n_pool, cr):
    width = part.stop - part.start
    return pl.pallas_call(
        functools.partial(place_kernel, part, n_pool, cr),
        out_shape=[jax.ShapeDtypeStruct((cr, width), BF16)] * n_pool,
        in_specs=[VMEM] * (3 + len(arrived)),
        out_specs=[VMEM] * n_pool,
        compiler_params=params(8),
        cost_estimate=cost(1e6, 1e6),
    )(keep, core, back, *arrived)


def collect_kernel(collect_ref, parts, out):
    at = 0
    for got in parts:
        width = got[0].shape[1]
        rows = jnp.concatenate([g[...] for g in got], axis=0)
        out[:, at : at + width] = dot(collect_ref[...], rows).astype(BF16)
        at += width


def collect_stage(collect, parts):
    width = sum(got[0].shape[1] for got in parts)
    return pl.pallas_call(
        collect_kernel,
        out_shape=jax.ShapeDtypeStruct((collect.shape[0], width), BF16),
        in_specs=[VMEM, [[VMEM] * len(got) for got in parts]],
        out_specs=VMEM,
        compiler_params=params(8),
        cost_estimate=cost(1e6, 1e6),
    )(collect, parts)


def body(
    hidden,
    w_x,
    w_bc,
    w_dt,
    conv_x,
    conv_bc,
    dt_bias,
    a_log,
    d_skip,
    norm_gain,
    w_out,
    ssm_pool,
    conv_pool_x,
    conv_pool_bc,
    owners,
    slots,
    accepted,
):
    n_pool = lax.axis_size("pool")
    n_tensor = lax.axis_size("tensor")
    n_line = n_tensor // 2
    req = hidden.shape[0] // DRAFT
    share = req // n_pool
    capacity = share + share // 2
    cr = -(-capacity * DRAFT // 16) * 16
    head_local = w_dt.shape[1]
    span = max(1, head_local // (HEADS // GROUPS))

    def row(v):
        return v.reshape(1, -1)

    def to_owner(parts):
        return [parts[0]] + [
            lax.ppermute(parts[s], "pool", [(i, (i + s) % n_pool) for i in range(n_pool)]) for s in range(1, n_pool)
        ]

    def to_requester(parts):
        return [parts[0]] + [
            lax.ppermute(parts[s], "pool", [((i + s) % n_pool, i) for i in range(n_pool)]) for s in range(1, n_pool)
        ]

    bc_sent, routes = project_bc([row(owners), row(slots), row(accepted)], hidden, w_bc, w_dt.T, ssm_pool.shape[0], n_pool, req, cr)
    hidden_kept, send, owner, pack, back, collect, accepts = routes
    bc_got = to_owner(bc_sent)
    x_sent = project_x(hidden_kept, w_x, send, n_pool, cr)
    x_got = to_owner(x_sent)
    bc_got, _ = lax.optimization_barrier((bc_got, x_sent))
    plan = exchange_plan(n_tensor, w_bc.shape[1], span)
    raw_bc, *pieces = bc_stage(owner, bc_got, conv_pool_bc, conv_bc, plan, span, n_pool, n_tensor)
    for i in range(1, len(plan)):
        pieces[i] = lax.ppermute(pieces[i], "tensor", completed(plan[i], n_tensor))
    fade_m, fade, w, d, states = pre_stage(accepts, raw_bc, row(dt_bias), row(a_log), ssm_pool)
    pieces, _ = lax.optimization_barrier((pieces, fade))
    y, m, b = mix_stage(fade_m, fade, states, pieces, plan, n_tensor)
    normed, x, raw_x = x_stage(owner, pack, x_got, conv_pool_x, conv_x, y, m, row(d_skip), row(norm_gain), n_pool)
    ahead = list(range(1, n_line))
    swap = [(i, i ^ 1) for i in range(n_tensor)]
    sends = out_stage(normed, w_out, ahead, n_line, True)
    core_got = [lax.ppermute(v, "tensor", swap) for v in sends]
    keeps = out_stage(normed, w_out, ahead, n_line, False)
    summed = [(k + g.astype(F32)).astype(BF16) for k, g in zip(keeps, core_got)]
    width = w_out.shape[1] // n_tensor
    parts = [slice(0, width // 2), slice(width // 2, width)]
    arrived = [
        [
            lax.ppermute(v[:, part], "tensor", [(r, ((r // 2 + i) % n_line) * 2 + r % 2) for r in range(n_tensor)])
            for i, v in zip(ahead, summed)
        ]
        for part in parts
    ]
    normed, _ = lax.optimization_barrier((normed, summed))
    (send_0,) = out_stage(normed, w_out, [0], n_line, True)
    core_0 = lax.ppermute(send_0, "tensor", swap)
    (keep_0,) = out_stage(normed, w_out, [0], n_line, False)
    half = states.shape[0] // 2
    x, _ = lax.optimization_barrier((x, keep_0))
    begun, _ = state_stage(range(half), d, x, w, b, states, accepts, [], [], None)
    keep_0, _ = lax.optimization_barrier((keep_0, begun))
    placed = [place_stage(part, keep_0, core_0, back, one, n_pool, cr) for part, one in zip(parts, arrived)]
    returned = [to_requester(one) for one in placed]
    x, _ = lax.optimization_barrier((x, placed[-1]))
    new_pool, (new_conv_x, new_conv_bc) = state_stage(
        range(half, states.shape[0]), d, x, w, b, states, accepts, [raw_x, raw_bc], [conv_pool_x, conv_pool_bc], begun
    )
    returned, _ = lax.optimization_barrier((returned, new_conv_x))
    mixed = collect_stage(collect, returned)
    return (mixed, new_pool, new_conv_x, new_conv_bc)


def solution(mesh):
    in_specs = (
        P(("groups", "pool"), None),
        P(None, "tensor"),
        P(None, "tensor"),
        P(None, "tensor"),
        P(None, "tensor"),
        P(None, "tensor"),
        P("tensor"),
        P("tensor"),
        P("tensor"),
        P("tensor"),
        P("tensor", None),
        P(("groups", "pool"), "tensor", None, None),
        P(("groups", "pool"), None, "tensor"),
        P(("groups", "pool"), None, "tensor"),
        P("groups"),
        P("groups"),
        P("groups"),
    )
    out_specs = (
        P(("groups", "pool"), "tensor"),
        P(("groups", "pool"), "tensor", None, None),
        P(("groups", "pool"), None, "tensor"),
        P(("groups", "pool"), None, "tensor"),
    )
    return jax.shard_map(body, mesh=mesh, in_specs=in_specs, out_specs=out_specs, check_vma=False)
```

```python
import functools

import jax
import jax.numpy as jnp
from jax import lax
from jax.experimental import pallas as pl
from jax.experimental.pallas import tpu as pltpu
from jax.sharding import PartitionSpec as P

HEADS = 64
HEAD_DIM = 64
STATE = 128
GROUPS = 8
DRAFT = 8
SHIFT = 3
EPS = 1e-05
FAR = 4096.0
HEAD_PART = 4

F32 = jnp.float32
BF16 = jnp.bfloat16
ANY = pl.BlockSpec(memory_space=pl.ANY)
HBM = pl.BlockSpec(memory_space=pltpu.HBM)
VMEM = pl.BlockSpec(memory_space=pltpu.VMEM)
SMEM = pl.BlockSpec(memory_space=pltpu.SMEM)


def params(mib, **more):
    return pltpu.CompilerParams(vmem_limit_bytes=mib * 2**20, **more)


def cost(flops, moved):
    return pl.CostEstimate(flops=int(flops), bytes_accessed=int(moved), transcendentals=0)


def iota(shape, dim):
    return lax.broadcasted_iota(jnp.int32, shape, dim)


def dot(a, b):
    return jnp.dot(a, b, preferred_element_type=F32)


def dot_t(a, b):
    return lax.dot_general(a, b, (((1,), (1,)), ((), ())), preferred_element_type=F32)


def as_col(row):
    n = row.shape[1]
    eye = iota((n, n), 0) == iota((n, n), 1)
    return jnp.sum(jnp.where(eye, jnp.broadcast_to(row, (n, n)), 0.0), axis=1, keepdims=True)


def partner_step(n, i, s):
    return (i + s) % n


def step_to(n, owner, requester):
    owner, requester = owner.astype(jnp.int32), requester.astype(jnp.int32)
    step = owner - requester
    return jnp.where(step < 0, step + n, step).astype(F32)


def block_shift(req):
    return req.bit_length() - 1


def ranks(orow, ocol, req):
    n = orow.shape[1]
    sub, lane = iota((n, n), 0), iota((n, n), 1)
    sh = block_shift(req)
    same = (ocol == orow) & ((sub >> sh) == (lane >> sh))
    row = jnp.sum(jnp.where(same & (sub < lane), 1.0, 0.0), axis=0, keepdims=True)
    col = jnp.sum(jnp.where(same & (lane < sub), 1.0, 0.0), axis=1, keepdims=True)
    return row, col


def hot(mask):
    return jnp.where(mask, 1.0, 0.0).astype(BF16)


def send_matrix(orow, me, n_pool, req, cr):
    ocol = as_col(orow)
    _, rank_col = ranks(orow, ocol, req)
    total, tokens = orow.shape[1], req * DRAFT
    place_col = step_to(n_pool, ocol, me) * cr + rank_col * DRAFT
    token = iota((total, tokens), 1)
    mine = (iota((total, tokens), 0) - me * req) == (token >> SHIFT)
    place = jnp.sum(jnp.where(mine, jnp.broadcast_to(place_col, (total, tokens)), 0.0), axis=0, keepdims=True)
    place = place + (iota((1, tokens), 1) & (DRAFT - 1)).astype(F32)
    return hot(iota((n_pool * cr, tokens), 0).astype(F32) == place)


def collect_matrix(orow, me, n_pool, req, cr):
    ocol = as_col(orow)
    rank_row, _ = ranks(orow, ocol, req)
    total, tokens = orow.shape[1], req * DRAFT
    place_row = step_to(n_pool, orow, me) * cr + rank_row * DRAFT
    token = iota((tokens, total), 0)
    mine = (iota((tokens, total), 1) - me * req) == (token >> SHIFT)
    place = jnp.sum(jnp.where(mine, jnp.broadcast_to(place_row, (tokens, total)), 0.0), axis=1, keepdims=True)
    place = place + (iota((tokens, 1), 0) & (DRAFT - 1)).astype(F32)
    return hot(iota((tokens, n_pool * cr), 1).astype(F32) == place)


def owner_matrix(orow, srow, me, n_pool, req, cr, slots):
    ocol = as_col(orow)
    rank_row, _ = ranks(orow, ocol, req)
    total, rows = orow.shape[1], slots * DRAFT
    block = (iota((1, total), 1) >> block_shift(req)).astype(F32)
    place_row = step_to(n_pool, me, block) * cr + rank_row * DRAFT + FAR
    slot = (iota((rows, total), 0) >> SHIFT).astype(F32)
    match = (orow == me.astype(F32)) & (srow == slot)
    place = jnp.sum(jnp.where(match, jnp.broadcast_to(place_row, (rows, total)), 0.0), axis=1, keepdims=True)
    place = place - FAR + (iota((rows, 1), 0) & (DRAFT - 1)).astype(F32)
    return hot(iota((rows, n_pool * cr), 1).astype(F32) == place)


def pack_matrices(orow, srow, me, n_pool, req, cr, slots):
    ocol, scol = as_col(orow), as_col(srow)
    _, rank_col = ranks(orow, ocol, req)
    total, rows, tokens = orow.shape[1], slots * DRAFT, req * DRAFT
    mine = me.astype(F32)
    sub, lane = iota((total, total), 0), iota((total, total), 1)
    index = jnp.sum(jnp.where((orow == mine) & (lane < sub), 1.0, 0.0), axis=1, keepdims=True)
    slot = (iota((total, rows), 1) >> SHIFT).astype(F32)
    match = (ocol == mine) & (scol == slot)
    value = jnp.broadcast_to(index * DRAFT + FAR, (total, rows))
    at = jnp.sum(jnp.where(match, value, 0.0), axis=0, keepdims=True) - FAR
    at = at + (iota((1, rows), 1) & (DRAFT - 1)).astype(F32)
    pack = hot(iota((tokens, rows), 0).astype(F32) == at)
    block = (iota((total, 1), 0) >> block_shift(req)).astype(F32)
    place_col = step_to(n_pool, me, block) * cr + rank_col * DRAFT + FAR
    match = (ocol == mine) & (index == (iota((total, tokens), 1) >> SHIFT).astype(F32))
    at = jnp.sum(jnp.where(match, jnp.broadcast_to(place_col, (total, tokens)), 0.0), axis=0, keepdims=True) - FAR
    at = at + (iota((1, tokens), 1) & (DRAFT - 1)).astype(F32)
    return pack, hot(iota((n_pool * cr, tokens), 0).astype(F32) == at)


def slot_accepts(orow, srow, arow, me, slots):
    total, rows = orow.shape[1], slots * DRAFT
    slot = (iota((rows, total), 0) >> SHIFT).astype(F32)
    match = (orow == me.astype(F32)) & (srow == slot)
    return jnp.sum(jnp.where(match, jnp.broadcast_to(arow, (rows, total)), 0.0), axis=1, keepdims=True)


def padded_pool(pool, width):
    slots, window, _ = pool.shape
    old = jnp.concatenate([pool.astype(F32), jnp.zeros((slots, DRAFT - window, width), F32)], axis=1)
    return old.reshape(slots * DRAFT, width)


def conv_slots(raw, pool, weight):
    rows, width = raw.shape
    window = pool.shape[1]
    old = padded_pool(pool, width)
    position = iota((rows, width), 0) & (DRAFT - 1)
    summed = weight[window] * raw
    for back in range(1, window + 1):
        new_part = pltpu.roll(raw, back, 0)
        old_part = pltpu.roll(old, (back - window) % rows, 0)
        summed = summed + weight[window - back] * jnp.where(position < back, old_part, new_part)
    return summed


def kept_rows(raw, pool, accepts):
    rows, width = raw.shape
    slots, window, _ = pool.shape
    old = padded_pool(pool, width)
    sub, lane = iota((rows, rows), 0), iota((rows, rows), 1)
    here = (sub >> SHIFT) == (lane >> SHIFT)
    at = (sub & (DRAFT - 1)).astype(F32) + accepts
    source = (lane & (DRAFT - 1)).astype(F32)
    from_old = hot(here & (source == at) & (source < window))
    from_new = hot(here & (source + window == at))
    kept = dot(from_old, old.astype(BF16)) + dot(from_new, raw.astype(BF16))
    return kept.astype(BF16).reshape(slots, DRAFT, width)[:, :window]


def silu(v):
    return v / (1.0 + jnp.exp(-v))


def spread_matrix(heads):
    shape = (heads, heads * HEAD_DIM)
    return hot(iota(shape, 0) == (iota(shape, 1) >> 6))


def spread(values, matrix):
    high = values.astype(BF16)
    low = (values - high.astype(F32)).astype(BF16)
    return dot(high, matrix) + dot(low, matrix)


def dma(pairs, sems, row):
    return [pltpu.make_async_copy(src, dst, sems.at[row, k]) for k, (src, dst) in enumerate(pairs)]


def project_bc_kernel(n_pool, req, cr, chunk, slots, owners, places, takes, hidden, w, w_dt, w_x, *refs):
    outs, refs = refs[:n_pool], refs[n_pool:]
    hbuf, head, send_ref, owner_ref, pack_ref, return_ref, collect_ref, accepts_ref = refs[:8]
    meta_buf, wbuf, dt_buf, sems = refs[8:]
    steps = hidden.shape[1] // chunk
    parts = [pl.ds(k * chunk, chunk) for k in range(steps)]
    copies = list(
        zip(
            dma([(hidden.at[:, p], hbuf.at[:, p]) for p in parts], sems, 0),
            dma([(w.at[p], wbuf.at[p]) for p in parts], sems, 1),
            dma([(w_dt.at[:, p], dt_buf.at[:, p]) for p in parts], sems, 2),
        )
    )
    tables = dma([(v, meta_buf.at[i]) for i, v in enumerate((owners, places, takes))], sems, 3)
    for copy in tables:
        copy.start()
    for group in copies:
        for copy in group:
            copy.start()
    ahead = pltpu.make_async_copy(w_x.at[pl.ds(0, head.shape[0])], head, sems.at[3, len(tables)])
    ahead.start()
    for copy in tables:
        copy.wait()
    me = lax.axis_index("pool").astype(jnp.int32)
    orow, srow, arow = (meta_buf[i].astype(F32) for i in range(3))
    order = send_matrix(orow, me, n_pool, req, cr)
    send_ref[...] = order
    owner_ref[...] = owner_matrix(orow, srow, me, n_pool, req, cr, slots)
    pack_ref[...], return_ref[...] = pack_matrices(orow, srow, me, n_pool, req, cr, slots)
    collect_ref[...] = collect_matrix(orow, me, n_pool, req, cr)
    accepts_ref[...] = slot_accepts(orow, srow, arow, me, slots)
    heads = w_dt.shape[0]
    total, total_dt = None, None
    for k in range(steps):
        for copy in copies[k]:
            copy.wait()
        here = slice(k * chunk, (k + 1) * chunk)
        added, added_dt = dot(hbuf[:, here], wbuf[here]), dot_t(hbuf[:, here], dt_buf[:, here])
        total = added if total is None else total + added
        total_dt = added_dt if total_dt is None else total_dt + added_dt
    width = w.shape[1]
    placed = dot(order, total.astype(BF16)).astype(BF16)
    high = total_dt.astype(BF16)
    low = (total_dt - high.astype(F32)).astype(BF16)
    shape = (heads, 128)
    to_high = hot(iota(shape, 0) == iota(shape, 1))
    to_low = hot(iota(shape, 0) + heads == iota(shape, 1))
    pair = (dot(high, to_high) + dot(low, to_low)).astype(BF16)
    placed_dt = dot(order, pair).astype(BF16)
    for s in range(n_pool):
        outs[s][:, :width] = placed[s * cr : (s + 1) * cr]
        outs[s][:, width:] = placed_dt[s * cr : (s + 1) * cr]
    ahead.wait()


def in_hbm(*arrays):
    return [pltpu.with_memory_space_constraint(v, pltpu.HBM) for v in arrays]


def project_bc(tables, hidden, w, w_dt, w_x, slots, n_pool, req, cr):
    tokens, depth = hidden.shape
    chunk = min(512, depth)
    width, rows = w.shape[1], slots * DRAFT
    outs = pl.pallas_call(
        functools.partial(project_bc_kernel, n_pool, req, cr, chunk, slots),
        out_shape=[jax.ShapeDtypeStruct((cr, width + 128), BF16)] * n_pool
        + [
            jax.ShapeDtypeStruct((tokens, depth), BF16),
            jax.ShapeDtypeStruct((depth // HEAD_PART, w_x.shape[1]), BF16),
            jax.ShapeDtypeStruct((n_pool * cr, tokens), BF16),
            jax.ShapeDtypeStruct((rows, n_pool * cr), BF16),
            jax.ShapeDtypeStruct((tokens, rows), BF16),
            jax.ShapeDtypeStruct((n_pool * cr, tokens), BF16),
            jax.ShapeDtypeStruct((tokens, n_pool * cr), BF16),
            jax.ShapeDtypeStruct((rows, 1), F32),
        ],
        in_specs=[HBM] * 7,
        out_specs=[VMEM] * (n_pool + 8),
        scratch_shapes=[
            pltpu.VMEM((3,) + tables[0].shape, jnp.int32),
            pltpu.VMEM((depth, width), BF16),
            pltpu.VMEM(w_dt.shape, BF16),
            pltpu.SemaphoreType.DMA((4, max(4, depth // chunk))),
        ],
        compiler_params=params(12),
        cost_estimate=cost(2 * tokens * depth * width, depth * (width + 128 + tokens) * 2),
    )(*in_hbm(*tables, hidden, w, w_dt, w_x))
    return outs[:n_pool], outs[n_pool:]


def project_x_kernel(n_pool, cr, chunk, hbuf, head, w, send_ref, *refs):
    outs, (wbuf, sems) = refs[:n_pool], refs[n_pool:]
    first = head.shape[0]
    steps = (w.shape[0] - first) // chunk
    copies = dma([(w.at[pl.ds(first + k * chunk, chunk)], wbuf.at[k]) for k in range(steps)], sems, 0)
    for copy in copies:
        copy.start()
    total = dot(hbuf[:, :first], head[...])
    for k in range(steps):
        copies[k].wait()
        here = slice(first + k * chunk, first + (k + 1) * chunk)
        total = total + dot(hbuf[:, here], wbuf[k])
    placed = dot(send_ref[...], total.astype(BF16)).astype(BF16)
    for s in range(n_pool):
        outs[s][...] = placed[s * cr : (s + 1) * cr]


def project_x(hidden, head, w, send, n_pool, cr):
    tokens, depth = hidden.shape
    chunk = min(512, depth)
    width = w.shape[1]
    steps = (depth - head.shape[0]) // chunk
    return pl.pallas_call(
        functools.partial(project_x_kernel, n_pool, cr, chunk),
        out_shape=[jax.ShapeDtypeStruct((cr, width), BF16)] * n_pool,
        in_specs=[VMEM, VMEM, HBM, VMEM],
        out_specs=[VMEM] * n_pool,
        scratch_shapes=[
            pltpu.VMEM((steps, chunk, width), BF16),
            pltpu.SemaphoreType.DMA((1, steps)),
        ],
        compiler_params=params(14),
        cost_estimate=cost(2 * tokens * depth * width, depth * (width + tokens) * 2),
    )(hidden, head, *in_hbm(w), send)


def pick(rank, table):
    value = jnp.int32(table[0])
    for i in range(1, len(table)):
        value = jnp.where(rank == i, jnp.int32(table[i]), value)
    return value


def exchange_plan(n_tensor, width, span):
    piece = span * STATE
    per_group = HEADS // GROUPS
    head_local = HEADS // n_tensor
    edges, own = [], []
    for target in range(n_tensor):
        first = target * head_local // per_group
        for kind in range(2):
            column = (kind * GROUPS + first) * STATE
            source, part = column // width, column % width // piece
            (own if source == target else edges).append((source, target, kind, part))
    rounds = []
    while edges:
        best = matching(edges, n_tensor)
        rounds.append(best)
        edges = [e for e in edges if e not in best]
    return [own] + rounds


def completed(edges, n):
    pairs = [(e[0], e[1]) for e in edges]
    sources = [i for i in range(n) if i not in [p[0] for p in pairs]]
    targets = [i for i in reversed(range(n)) if i not in [p[1] for p in pairs]]
    return pairs + list(zip(sources, targets))


def matching(edges, n):
    held = {}

    def place(source, seen):
        for edge in edges:
            if edge[0] == source and edge[1] not in seen:
                seen.add(edge[1])
                if edge[1] not in held or place(held[edge[1]][0], seen):
                    held[edge[1]] = edge
                    return True
        return False

    for source in range(n):
        place(source, set())
    return [held[target] for target in sorted(held)]


def bc_kernel(n_pool, parts, owner_ref, *refs):
    got, refs = refs[:n_pool], refs[n_pool:]
    pool_ref, weight_ref, raw_ref = refs[:3]
    outs, act_ref = refs[3:-1], refs[-1]
    width = pool_ref.shape[2]
    rank = lax.axis_index("tensor").astype(jnp.int32)
    raw = dot(owner_ref[...], jnp.concatenate([g[...] for g in got], axis=0))
    raw_ref[...] = raw
    act_ref[...] = silu(conv_slots(raw[:, :width], pool_ref[...], weight_ref[...])).astype(BF16)
    for table, out in zip(parts, outs):
        piece = out.shape[1]
        out[...] = act_ref[:, pl.ds(pl.multiple_of(pick(rank, table) * piece, 128), piece)]


def bc_stage(owner, got, pool, weight, plan, span, n_pool, n_tensor):
    slots, _, width = pool.shape
    rows = slots * DRAFT
    piece = span * STATE
    parts = []
    for one in plan:
        table = [0] * n_tensor
        for source, _, _, part in one:
            table[source] = part
        parts.append(table)
    return pl.pallas_call(
        functools.partial(bc_kernel, n_pool, parts),
        out_shape=[jax.ShapeDtypeStruct((rows, width + 128), F32)]
        + [jax.ShapeDtypeStruct((rows, piece), BF16)] * len(plan),
        in_specs=[VMEM] * (n_pool + 3),
        out_specs=[VMEM] * (1 + len(plan)),
        scratch_shapes=[pltpu.VMEM((rows, width), BF16)],
        compiler_params=params(8),
        cost_estimate=cost(2e6, 1e6),
    )(owner, *got, pool, weight)


def pre_kernel(slots, accepts_ref, raw_ref, conv_ref, bias_ref, alog_ref, kept_ref, m_ref, fade_ref, w_ref, d_ref):
    heads = w_ref.shape[1]
    rows = slots * DRAFT
    accepts = accepts_ref[...]
    width = raw_ref.shape[1] - 128
    shape = (128, heads)
    lane, head = iota(shape, 0), iota(shape, 1)
    both = hot((lane == head) | (lane == head + heads))
    x = dot(raw_ref[:, width:].astype(BF16), both) + bias_ref[...]
    step = jnp.maximum(x, 0.0) + jnp.log1p(jnp.exp(-jnp.abs(x)))
    logs = -step * jnp.exp(alog_ref[...])
    position = iota((rows, heads), 0) & (DRAFT - 1)
    for back in (1, 2, 4):
        logs = logs + jnp.where(position >= back, pltpu.roll(logs, back, 0), 0.0)
    last = jnp.where(position.astype(F32) + 1 == accepts, logs, 0.0).reshape(slots, DRAFT, heads)
    last = jnp.broadcast_to(jnp.sum(last, axis=1, keepdims=True), (slots, DRAFT, heads))
    d_ref[...] = jnp.exp(last[:, 0, :])
    last = last.reshape(rows, heads)
    w_ref[...] = jnp.where(position.astype(F32) < accepts, jnp.exp(jnp.minimum(last - logs, 0.0)) * step, 0.0)
    lanes = heads * DRAFT
    shape = (heads, lanes)
    repeat = jnp.where(iota(shape, 0) == (iota(shape, 1) >> SHIFT), 1.0, 0.0)

    def wide(v):
        return jnp.dot(v, repeat, preferred_element_type=F32, precision=lax.Precision.HIGHEST)

    t, u = iota((rows, lanes), 0) & (DRAFT - 1), iota((rows, lanes), 1) & (DRAFT - 1)

    def at_u(v):
        v = jnp.where(t == u, v, 0.0).reshape(slots, DRAFT, lanes)
        return jnp.broadcast_to(jnp.sum(v, axis=1, keepdims=True), (slots, DRAFT, lanes)).reshape(rows, lanes)

    wide_logs = wide(logs)
    fade = jnp.where(u <= t, jnp.exp(jnp.minimum(wide_logs - at_u(wide_logs), 0.0)) * at_u(wide(step)), 0.0)
    fade = fade.astype(BF16)
    shape = (lanes, rows)
    same = (iota(shape, 0) & (DRAFT - 1)) == (iota(shape, 1) & (DRAFT - 1))
    head = iota(shape, 0) >> SHIFT
    for h in range(heads):
        m_ref[h] = dot(fade, hot(same & (head == h))).astype(BF16)
    fade_ref[...] = spread(jnp.exp(logs), spread_matrix(heads))
    kept_ref[...] = kept_rows(raw_ref[:, :width], conv_ref[...], accepts)


def pre_stage(accepts, raw, conv_pool, bias, a_log, pool):
    slots, heads = pool.shape[:2]
    rows = slots * DRAFT
    return pl.pallas_call(
        functools.partial(pre_kernel, slots),
        out_shape=[
            jax.ShapeDtypeStruct(conv_pool.shape, BF16),
            jax.ShapeDtypeStruct((heads, rows, rows), BF16),
            jax.ShapeDtypeStruct((rows, heads * HEAD_DIM), F32),
            jax.ShapeDtypeStruct((rows, heads), F32),
            jax.ShapeDtypeStruct((slots, heads), F32),
        ],
        in_specs=[VMEM] * 5,
        out_specs=[VMEM] * 5,
        compiler_params=params(10),
        cost_estimate=cost(1e6, 1e6),
    )(accepts, raw, conv_pool, bias, a_log)


def mix_kernel(kinds, fade_m_ref, fade_ref, states, *refs):
    pieces, (y_ref, m_ref, b_ref, c_ref) = refs[: len(kinds)], refs[len(kinds) :]
    slots, heads = states.shape[:2]
    span = b_ref.shape[1] // STATE
    per = heads // span
    rank = lax.axis_index("tensor").astype(jnp.int32)
    for side, ref in enumerate((b_ref, c_ref)):
        ref[...] = pieces[0][...]
        for table, piece in zip(kinds, pieces):
            mine = [int(kind == side) for kind in table]
            if any(mine):

                @pl.when(pick(rank, mine) == 1)
                def _(ref=ref, piece=piece):
                    ref[...] = piece[...]

    rows = slots * DRAFT
    here = (iota((rows, rows), 0) >> SHIFT) == (iota((rows, rows), 1) >> SHIFT)
    for g in range(span):
        part = slice(g * STATE, (g + 1) * STATE)
        pair = jnp.where(here, dot_t(c_ref[:, part], b_ref[:, part]), 0.0)
        for h in range(g * per, (g + 1) * per):
            m_ref[h] = (pair * fade_m_ref[h].astype(F32)).astype(BF16)
    c = c_ref[...].astype(F32)
    for j in range(slots):
        here = slice(j * DRAFT, (j + 1) * DRAFT)
        for g in range(span):
            old = states[j, g * per : (g + 1) * per].reshape(per * HEAD_DIM, STATE)
            columns = slice(g * per * HEAD_DIM, (g + 1) * per * HEAD_DIM)
            read = dot_t(c[here, g * STATE : (g + 1) * STATE].astype(BF16), old)
            y_ref[here, columns] = read * fade_ref[here, columns]


def mix_stage(fade_m, fade, states, pieces, plan, n_tensor):
    slots, heads = states.shape[:2]
    rows = slots * DRAFT
    kinds = []
    for one in plan:
        table = [-1] * n_tensor
        for _, target, kind, _ in one:
            table[target] = kind
        kinds.append(table)
    return pl.pallas_call(
        functools.partial(mix_kernel, kinds),
        out_shape=[
            jax.ShapeDtypeStruct((rows, heads * HEAD_DIM), F32),
            jax.ShapeDtypeStruct((heads, rows, rows), BF16),
            jax.ShapeDtypeStruct(pieces[0].shape, BF16),
        ],
        in_specs=[VMEM] * (3 + len(plan)),
        out_specs=[VMEM] * 3,
        scratch_shapes=[pltpu.VMEM(pieces[0].shape, BF16)],
        compiler_params=params(8),
        cost_estimate=cost(2 * rows * heads * HEAD_DIM * STATE, 2 * states.size),
    )(fade_m, fade, states, *pieces)


def x_kernel(n_pool, owner_ref, pack_ref, *refs):
    got, refs = refs[:n_pool], refs[n_pool:]
    pool_ref, weight_ref, y_ref, m_ref, skip_ref, gain_ref = refs[:6]
    normed_ref, x_ref, raw_ref = refs[6:]
    heads = pool_ref.shape[2] // HEAD_DIM
    raw = dot(owner_ref[...], jnp.concatenate([g[...] for g in got], axis=0))
    raw_ref[...] = raw
    x = silu(conv_slots(raw, pool_ref[...], weight_ref[...]))
    x_ref[...] = x
    matrix = spread_matrix(heads)
    small = x.astype(BF16)
    parts = [dot(m_ref[h], small[:, h * HEAD_DIM : (h + 1) * HEAD_DIM]) for h in range(heads)]
    y = jnp.concatenate(parts, axis=1) + y_ref[...] + spread(skip_ref[...], matrix) * x
    square = (y * y).astype(BF16)
    scale = lax.rsqrt(dot_t(square, matrix) * (1.0 / HEAD_DIM) + EPS)
    normed = (y * spread(scale, matrix) * gain_ref[...]).astype(BF16)
    normed_ref[...] = dot(pack_ref[...], normed).astype(BF16)


def x_stage(owner, pack, got, pool, weight, y, m, skip, gain, n_pool):
    slots, _, width = pool.shape
    rows = slots * DRAFT
    return pl.pallas_call(
        functools.partial(x_kernel, n_pool),
        out_shape=[jax.ShapeDtypeStruct((pack.shape[0], width), BF16)] + [jax.ShapeDtypeStruct((rows, width), F32)] * 2,
        in_specs=[VMEM] * (n_pool + 8),
        out_specs=[VMEM] * 3,
        compiler_params=params(16),
        cost_estimate=cost(2 * rows * rows * width, 4e6),
    )(owner, pack, *got, pool, weight, y, m, skip, gain)


def fill_states(span_of, d_ref, turned, b_ref, pool, new_pool, buf, out_sems):
    slots, heads = pool.shape[:2]
    rows = slots * DRAFT
    span = b_ref.shape[1] // STATE
    per = heads // span
    backs = [pltpu.make_async_copy(buf.at[j], new_pool.at[j], out_sems.at[j]) for j in span_of]
    b = b_ref[...].astype(F32)
    slot = iota((rows, STATE), 0) >> SHIFT
    for at in range(0, len(span_of), 2):
        pair = span_of[at : at + 2]
        for g in range(span):
            part = b[:, g * STATE : (g + 1) * STATE]
            rhs = jnp.concatenate([jnp.where(slot == j, part, 0.0) for j in pair], axis=1).astype(BF16)
            added = dot(turned[g * per * HEAD_DIM : (g + 1) * per * HEAD_DIM], rhs)
            for n, j in enumerate(pair):
                for i in range(per):
                    h = g * per + i
                    more = added[i * HEAD_DIM : (i + 1) * HEAD_DIM, n * STATE : (n + 1) * STATE]
                    buf[j, h] = (pool[j, h].astype(F32) * d_ref[j, h] + more).astype(BF16)
        for back in backs[at : at + 2]:
            back.start()
    return backs


def first_state_kernel(span_of, d_ref, x_ref, w_ref, b_ref, pool, new_pool, turned_ref, buf, out_sems):
    weighted = x_ref[...] * spread(w_ref[...], spread_matrix(pool.shape[1]))
    turned_ref[...] = weighted.T.astype(BF16)
    for copy in fill_states(span_of, d_ref, turned_ref, b_ref, pool, new_pool, buf, out_sems):
        copy.wait()


def first_state_stage(span_of, d, x, w, b, pool):
    return pl.pallas_call(
        functools.partial(first_state_kernel, span_of),
        out_shape=[jax.ShapeDtypeStruct(pool.shape, BF16), jax.ShapeDtypeStruct(x.shape[::-1], BF16)],
        in_specs=[SMEM] + [VMEM] * 4,
        out_specs=[HBM, VMEM],
        scratch_shapes=[pltpu.VMEM(pool.shape, BF16), pltpu.SemaphoreType.DMA((pool.shape[0],))],
        compiler_params=params(16),
        cost_estimate=cost(2 * pool.size * DRAFT, 2 * pool.size),
    )(d, x, w, b, pool)


def last_state_kernel(span_of, d_ref, turned_ref, b_ref, pool, accepts_ref, raw_ref, conv_ref, begun, *refs):
    del begun
    new_pool, kept_ref, buf, out_sems = refs
    backs = fill_states(span_of, d_ref, turned_ref, b_ref, pool, new_pool, buf, out_sems)
    kept_ref[...] = kept_rows(raw_ref[...], conv_ref[...], accepts_ref[...])
    for copy in backs:
        copy.wait()


def last_state_stage(span_of, d, turned, b, pool, accepts, raw, conv, begun):
    return pl.pallas_call(
        functools.partial(last_state_kernel, span_of),
        out_shape=[jax.ShapeDtypeStruct(pool.shape, BF16), jax.ShapeDtypeStruct(conv.shape, BF16)],
        in_specs=[SMEM] + [VMEM] * 6 + [HBM],
        out_specs=[HBM, VMEM],
        scratch_shapes=[pltpu.VMEM(pool.shape, BF16), pltpu.SemaphoreType.DMA((pool.shape[0],))],
        input_output_aliases={7: 0},
        compiler_params=params(16),
        cost_estimate=cost(2 * pool.size * DRAFT, 2 * pool.size),
    )(d, turned, b, pool, accepts, raw, conv, begun)


def out_kernel(wants, n_line, rows, w, *outs):
    width = outs[0].shape[1]
    rank = lax.axis_index("tensor").astype(jnp.int32)
    core, line = rank & 1, rank >> 1
    for (i, other_core), out in zip(wants, outs):
        there = line + i
        there = jnp.where(there >= n_line, there - n_line, there)
        column = pl.multiple_of((2 * there + (1 - core if other_core else core)) * width, 128)
        out[...] = dot(rows[...], w[:, pl.ds(column, width)]).astype(out.dtype)


def out_stage(rows, w, wants, n_line):
    depth, total = w.shape
    width = total // (2 * n_line)
    tokens = rows.shape[0]
    return pl.pallas_call(
        functools.partial(out_kernel, wants, n_line),
        out_shape=[jax.ShapeDtypeStruct((tokens, width), BF16 if other else F32) for _, other in wants],
        in_specs=[VMEM] * 2,
        out_specs=[VMEM] * len(wants),
        compiler_params=params(8),
        cost_estimate=cost(2 * tokens * depth * width * len(wants), 2 * depth * width * len(wants)),
    )(rows, w)


def sum_kernel(n, parts, *refs):
    for i in range(n):
        for p, part in enumerate(parts):
            refs[2 * n + p * n + i][...] = (refs[i][:, part] + refs[n + i][:, part].astype(F32)).astype(BF16)


def sum_stage(keeps, gots, parts):
    n = len(keeps)
    shape = jax.ShapeDtypeStruct((keeps[0].shape[0], parts[0].stop), BF16)
    outs = pl.pallas_call(
        functools.partial(sum_kernel, n, parts),
        out_shape=[shape] * (n * len(parts)),
        in_specs=[VMEM] * (2 * n),
        out_specs=[VMEM] * (n * len(parts)),
        compiler_params=params(8),
        cost_estimate=cost(1e6, 1e6),
    )(*keeps, *gots)
    return [outs[p * n : (p + 1) * n] for p in range(len(parts))]


def place_kernel(part, n_pool, cr, keep, core, return_ref, *refs):
    arrived, outs = refs[:-n_pool], refs[-n_pool:]
    total = keep[:, part] + core[:, part].astype(F32)
    for one in arrived:
        total = total + one[...].astype(F32)
    placed = dot(return_ref[...], total.astype(BF16)).astype(BF16)
    for s in range(n_pool):
        outs[s][...] = placed[s * cr : (s + 1) * cr]


def place_stage(part, keep, core, back, arrived, n_pool, cr):
    width = part.stop - part.start
    return pl.pallas_call(
        functools.partial(place_kernel, part, n_pool, cr),
        out_shape=[jax.ShapeDtypeStruct((cr, width), BF16)] * n_pool,
        in_specs=[VMEM] * (3 + len(arrived)),
        out_specs=[VMEM] * n_pool,
        compiler_params=params(8),
        cost_estimate=cost(1e6, 1e6),
    )(keep, core, back, *arrived)


def collect_kernel(collect_ref, parts, out):
    at = 0
    for got in parts:
        width = got[0].shape[1]
        rows = jnp.concatenate([g[...] for g in got], axis=0)
        out[:, at : at + width] = dot(collect_ref[...], rows).astype(BF16)
        at += width


def collect_stage(collect, parts):
    width = sum(got[0].shape[1] for got in parts)
    return pl.pallas_call(
        collect_kernel,
        out_shape=jax.ShapeDtypeStruct((collect.shape[0], width), BF16),
        in_specs=[VMEM, [[VMEM] * len(got) for got in parts]],
        out_specs=VMEM,
        compiler_params=params(8),
        cost_estimate=cost(1e6, 1e6),
    )(collect, parts)


def body(
    hidden,
    w_x,
    w_bc,
    w_dt,
    conv_x,
    conv_bc,
    dt_bias,
    a_log,
    d_skip,
    norm_gain,
    w_out,
    ssm_pool,
    conv_pool_x,
    conv_pool_bc,
    owners,
    slots,
    accepted,
):
    n_pool = lax.axis_size("pool")
    n_tensor = lax.axis_size("tensor")
    n_line = n_tensor // 2
    req = hidden.shape[0] // DRAFT
    share = req // n_pool
    capacity = share + share // 2
    cr = -(-capacity * DRAFT // 16) * 16
    head_local = w_dt.shape[1]
    span = max(1, head_local // (HEADS // GROUPS))

    def row(v):
        return v.reshape(1, -1)

    def over_pool(parts, home):
        moved = list(parts)
        for step in range(1, n_pool):
            pairs = [(i, partner_step(n_pool, i, step)) for i in range(n_pool)]
            pairs = [(b, a) for a, b in pairs] if home else pairs
            moved[step] = lax.ppermute(parts[step], "pool", pairs)
        return moved

    bc_sent, routes = project_bc([row(owners), row(slots), row(accepted)], hidden, w_bc, w_dt.T, w_x, ssm_pool.shape[0], n_pool, req, cr)
    hidden_kept, head, send, owner, pack, back, collect, accepts = routes
    bc_got = over_pool(bc_sent, False)
    x_sent = project_x(hidden_kept, head, w_x, send, n_pool, cr)
    x_got = over_pool(x_sent, False)
    bc_got, _ = lax.optimization_barrier((bc_got, x_sent))
    plan = exchange_plan(n_tensor, w_bc.shape[1], span)
    raw_bc, *pieces = bc_stage(owner, bc_got, conv_pool_bc, conv_bc, plan, span, n_pool, n_tensor)
    for i in range(1, len(plan)):
        pieces[i] = lax.ppermute(pieces[i], "tensor", completed(plan[i], n_tensor))
    new_conv_bc, fade_m, fade, w, d = pre_stage(accepts, raw_bc, conv_pool_bc, row(dt_bias), row(a_log), ssm_pool)
    states, _ = lax.optimization_barrier((ssm_pool, x_sent))
    states = pltpu.with_memory_space_constraint(states, pltpu.VMEM)
    pieces, _ = lax.optimization_barrier((pieces, fade))
    y, m, b = mix_stage(fade_m, fade, states, pieces, plan, n_tensor)
    normed, x, raw_x = x_stage(owner, pack, x_got, conv_pool_x, conv_x, y, m, row(d_skip), row(norm_gain), n_pool)
    ahead = list(range(1, n_line))
    swap = [(i, i ^ 1) for i in range(n_tensor)]
    sends = out_stage(normed, w_out, [(i, True) for i in ahead], n_line)
    core_got = [lax.ppermute(v, "tensor", swap) for v in sends]
    *keeps, send_0, keep_0 = out_stage(normed, w_out, [(i, False) for i in ahead] + [(0, True), (0, False)], n_line)
    width = w_out.shape[1] // n_tensor
    parts = [slice(0, width // 2), slice(width // 2, width)]
    summed = sum_stage(keeps, core_got, parts)

    def over_line(values):
        return [
            lax.ppermute(v, "tensor", [(r, ((r // 2 + i) % n_line) * 2 + r % 2) for r in range(n_tensor)])
            for i, v in zip(ahead, values)
        ]

    arrived = [over_line(summed[0])]
    core_0 = lax.ppermute(send_0, "tensor", swap)
    half = states.shape[0] // 2
    x, _ = lax.optimization_barrier((x, summed))
    begun, turned = first_state_stage(range(half), d, x, w, b, states)
    second, _ = lax.optimization_barrier((summed[1], begun))
    arrived.append(over_line(second))
    keep_0, _ = lax.optimization_barrier((keep_0, begun))
    placed = [place_stage(part, keep_0, core_0, back, one, n_pool, cr) for part, one in zip(parts, arrived)]
    returned = [over_pool(one, True) for one in placed]
    turned, _ = lax.optimization_barrier((turned, placed[-1]))
    new_pool, new_conv_x = last_state_stage(
        range(half, states.shape[0]), d, turned, b, states, accepts, raw_x, conv_pool_x, begun
    )
    returned, _ = lax.optimization_barrier((returned, new_conv_x))
    mixed = collect_stage(collect, returned)
    return (mixed, new_pool, new_conv_x, new_conv_bc)


def solution(mesh):
    in_specs = (
        P(("groups", "pool"), None),
        P(None, "tensor"),
        P(None, "tensor"),
        P(None, "tensor"),
        P(None, "tensor"),
        P(None, "tensor"),
        P("tensor"),
        P("tensor"),
        P("tensor"),
        P("tensor"),
        P("tensor", None),
        P(("groups", "pool"), "tensor", None, None),
        P(("groups", "pool"), None, "tensor"),
        P(("groups", "pool"), None, "tensor"),
        P("groups"),
        P("groups"),
        P("groups"),
    )
    out_specs = (
        P(("groups", "pool"), "tensor"),
        P(("groups", "pool"), "tensor", None, None),
        P(("groups", "pool"), None, "tensor"),
        P(("groups", "pool"), None, "tensor"),
    )
    return jax.shard_map(body, mesh=mesh, in_specs=in_specs, out_specs=out_specs, check_vma=False)
```

```python
import functools

import jax
import jax.numpy as jnp
from jax import lax
from jax.experimental import pallas as pl
from jax.experimental.pallas import tpu as pltpu
from jax.sharding import PartitionSpec as P

HEADS = 64
HEAD_DIM = 64
STATE = 128
GROUPS = 8
DRAFT = 8
SHIFT = 3
EPS = 1e-05
FAR = 4096.0
HEAD_PART = 4

F32 = jnp.float32
BF16 = jnp.bfloat16
ANY = pl.BlockSpec(memory_space=pl.ANY)
HBM = pl.BlockSpec(memory_space=pltpu.HBM)
VMEM = pl.BlockSpec(memory_space=pltpu.VMEM)
SMEM = pl.BlockSpec(memory_space=pltpu.SMEM)


def params(mib, **more):
    return pltpu.CompilerParams(vmem_limit_bytes=mib * 2**20, **more)


def cost(flops, moved):
    return pl.CostEstimate(flops=int(flops), bytes_accessed=int(moved), transcendentals=0)


def iota(shape, dim):
    return lax.broadcasted_iota(jnp.int32, shape, dim)


def dot(a, b):
    return jnp.dot(a, b, preferred_element_type=F32)


def dot_t(a, b):
    return lax.dot_general(a, b, (((1,), (1,)), ((), ())), preferred_element_type=F32)


def as_col(row):
    n = row.shape[1]
    eye = iota((n, n), 0) == iota((n, n), 1)
    return jnp.sum(jnp.where(eye, jnp.broadcast_to(row, (n, n)), 0.0), axis=1, keepdims=True)


def partner_step(n, i, s):
    return (i + s) % n


def step_to(n, owner, requester):
    owner, requester = owner.astype(jnp.int32), requester.astype(jnp.int32)
    step = owner - requester
    return jnp.where(step < 0, step + n, step).astype(F32)


def block_shift(req):
    return req.bit_length() - 1


def ranks(orow, ocol, req):
    n = orow.shape[1]
    sub, lane = iota((n, n), 0), iota((n, n), 1)
    sh = block_shift(req)
    same = (ocol == orow) & ((sub >> sh) == (lane >> sh))
    row = jnp.sum(jnp.where(same & (sub < lane), 1.0, 0.0), axis=0, keepdims=True)
    col = jnp.sum(jnp.where(same & (lane < sub), 1.0, 0.0), axis=1, keepdims=True)
    return row, col


def hot(mask):
    return jnp.where(mask, 1.0, 0.0).astype(BF16)


def send_matrix(orow, me, n_pool, req, cr):
    ocol = as_col(orow)
    _, rank_col = ranks(orow, ocol, req)
    total, tokens = orow.shape[1], req * DRAFT
    place_col = step_to(n_pool, ocol, me) * cr + rank_col * DRAFT
    token = iota((total, tokens), 1)
    mine = (iota((total, tokens), 0) - me * req) == (token >> SHIFT)
    place = jnp.sum(jnp.where(mine, jnp.broadcast_to(place_col, (total, tokens)), 0.0), axis=0, keepdims=True)
    place = place + (iota((1, tokens), 1) & (DRAFT - 1)).astype(F32)
    return hot(iota((n_pool * cr, tokens), 0).astype(F32) == place)


def collect_matrix(orow, me, n_pool, req, cr):
    ocol = as_col(orow)
    rank_row, _ = ranks(orow, ocol, req)
    total, tokens = orow.shape[1], req * DRAFT
    place_row = step_to(n_pool, orow, me) * cr + rank_row * DRAFT
    token = iota((tokens, total), 0)
    mine = (iota((tokens, total), 1) - me * req) == (token >> SHIFT)
    place = jnp.sum(jnp.where(mine, jnp.broadcast_to(place_row, (tokens, total)), 0.0), axis=1, keepdims=True)
    place = place + (iota((tokens, 1), 0) & (DRAFT - 1)).astype(F32)
    return hot(iota((tokens, n_pool * cr), 1).astype(F32) == place)


def owner_matrix(orow, srow, me, n_pool, req, cr, slots):
    ocol = as_col(orow)
    rank_row, _ = ranks(orow, ocol, req)
    total, rows = orow.shape[1], slots * DRAFT
    block = (iota((1, total), 1) >> block_shift(req)).astype(F32)
    place_row = step_to(n_pool, me, block) * cr + rank_row * DRAFT + FAR
    slot = (iota((rows, total), 0) >> SHIFT).astype(F32)
    match = (orow == me.astype(F32)) & (srow == slot)
    place = jnp.sum(jnp.where(match, jnp.broadcast_to(place_row, (rows, total)), 0.0), axis=1, keepdims=True)
    place = place - FAR + (iota((rows, 1), 0) & (DRAFT - 1)).astype(F32)
    return hot(iota((rows, n_pool * cr), 1).astype(F32) == place)


def pack_matrices(orow, srow, me, n_pool, req, cr, slots):
    ocol, scol = as_col(orow), as_col(srow)
    _, rank_col = ranks(orow, ocol, req)
    total, rows, tokens = orow.shape[1], slots * DRAFT, req * DRAFT
    mine = me.astype(F32)
    sub, lane = iota((total, total), 0), iota((total, total), 1)
    index = jnp.sum(jnp.where((orow == mine) & (lane < sub), 1.0, 0.0), axis=1, keepdims=True)
    slot = (iota((total, rows), 1) >> SHIFT).astype(F32)
    match = (ocol == mine) & (scol == slot)
    value = jnp.broadcast_to(index * DRAFT + FAR, (total, rows))
    at = jnp.sum(jnp.where(match, value, 0.0), axis=0, keepdims=True) - FAR
    at = at + (iota((1, rows), 1) & (DRAFT - 1)).astype(F32)
    pack = hot(iota((tokens, rows), 0).astype(F32) == at)
    block = (iota((total, 1), 0) >> block_shift(req)).astype(F32)
    place_col = step_to(n_pool, me, block) * cr + rank_col * DRAFT + FAR
    match = (ocol == mine) & (index == (iota((total, tokens), 1) >> SHIFT).astype(F32))
    at = jnp.sum(jnp.where(match, jnp.broadcast_to(place_col, (total, tokens)), 0.0), axis=0, keepdims=True) - FAR
    at = at + (iota((1, tokens), 1) & (DRAFT - 1)).astype(F32)
    return pack, hot(iota((n_pool * cr, tokens), 0).astype(F32) == at)


def slot_accepts(orow, srow, arow, me, slots):
    total, rows = orow.shape[1], slots * DRAFT
    slot = (iota((rows, total), 0) >> SHIFT).astype(F32)
    match = (orow == me.astype(F32)) & (srow == slot)
    return jnp.sum(jnp.where(match, jnp.broadcast_to(arow, (rows, total)), 0.0), axis=1, keepdims=True)


def padded_pool(pool, width):
    slots, window, _ = pool.shape
    old = jnp.concatenate([pool.astype(F32), jnp.zeros((slots, DRAFT - window, width), F32)], axis=1)
    return old.reshape(slots * DRAFT, width)


def conv_old(pool, weight):
    slots, window, width = pool.shape
    rows = slots * DRAFT
    old = padded_pool(pool, width)
    position = iota((rows, width), 0) & (DRAFT - 1)
    summed = jnp.zeros((rows, width), F32)
    for back in range(1, window + 1):
        part = pltpu.roll(old, (back - window) % rows, 0)
        summed = summed + weight[window - back] * jnp.where(position < back, part, 0.0)
    return summed


def conv_new(raw, weight, window):
    position = iota(raw.shape, 0) & (DRAFT - 1)
    summed = weight[window] * raw
    for back in range(1, window + 1):
        part = pltpu.roll(raw, back, 0)
        summed = summed + weight[window - back] * jnp.where(position < back, 0.0, part)
    return summed


def kept_rows(raw, pool, accepts):
    rows, width = raw.shape
    slots, window, _ = pool.shape
    old = padded_pool(pool, width)
    sub, lane = iota((rows, rows), 0), iota((rows, rows), 1)
    here = (sub >> SHIFT) == (lane >> SHIFT)
    at = (sub & (DRAFT - 1)).astype(F32) + accepts
    source = (lane & (DRAFT - 1)).astype(F32)
    from_old = hot(here & (source == at) & (source < window))
    from_new = hot(here & (source + window == at))
    kept = dot(from_old, old.astype(BF16)) + dot(from_new, raw.astype(BF16))
    return kept.astype(BF16).reshape(slots, DRAFT, width)[:, :window]


def silu(v):
    return v / (1.0 + jnp.exp(-v))


def spread_matrix(heads):
    shape = (heads, heads * HEAD_DIM)
    return hot(iota(shape, 0) == (iota(shape, 1) >> 6))


def spread(values, matrix):
    high = values.astype(BF16)
    low = (values - high.astype(F32)).astype(BF16)
    return dot(high, matrix) + dot(low, matrix)


def dma(pairs, sems, row):
    return [pltpu.make_async_copy(src, dst, sems.at[row, k]) for k, (src, dst) in enumerate(pairs)]


def project_bc_kernel(n_pool, req, cr, chunk, slots, owners, places, takes, hidden, w, w_dt, w_x, *refs):
    outs, refs = refs[:n_pool], refs[n_pool:]
    hbuf, head, send_ref, owner_ref, pack_ref, return_ref, collect_ref, accepts_ref = refs[:8]
    meta_buf, wbuf, dt_buf, sems = refs[8:]
    steps = hidden.shape[1] // chunk
    parts = [pl.ds(k * chunk, chunk) for k in range(steps)]
    copies = list(
        zip(
            dma([(hidden.at[:, p], hbuf.at[:, p]) for p in parts], sems, 0),
            dma([(w.at[p], wbuf.at[p]) for p in parts], sems, 1),
            dma([(w_dt.at[:, p], dt_buf.at[:, p]) for p in parts], sems, 2),
        )
    )
    tables = dma([(v, meta_buf.at[i]) for i, v in enumerate((owners, places, takes))], sems, 3)
    for copy in tables:
        copy.start()
    for group in copies:
        for copy in group:
            copy.start()
    ahead = pltpu.make_async_copy(w_x.at[pl.ds(0, head.shape[0])], head, sems.at[3, len(tables)])
    ahead.start()
    for copy in tables:
        copy.wait()
    me = lax.axis_index("pool").astype(jnp.int32)
    orow, srow, arow = (meta_buf[i].astype(F32) for i in range(3))
    order = send_matrix(orow, me, n_pool, req, cr)
    send_ref[...] = order
    owner_ref[...] = owner_matrix(orow, srow, me, n_pool, req, cr, slots)
    pack_ref[...], return_ref[...] = pack_matrices(orow, srow, me, n_pool, req, cr, slots)
    collect_ref[...] = collect_matrix(orow, me, n_pool, req, cr)
    accepts_ref[...] = slot_accepts(orow, srow, arow, me, slots)
    heads = w_dt.shape[0]
    total, total_dt = None, None
    for k in range(steps):
        for copy in copies[k]:
            copy.wait()
        here = slice(k * chunk, (k + 1) * chunk)
        added, added_dt = dot(hbuf[:, here], wbuf[here]), dot_t(hbuf[:, here], dt_buf[:, here])
        total = added if total is None else total + added
        total_dt = added_dt if total_dt is None else total_dt + added_dt
    width = w.shape[1]
    placed = dot(order, total.astype(BF16)).astype(BF16)
    high = total_dt.astype(BF16)
    low = (total_dt - high.astype(F32)).astype(BF16)
    shape = (heads, 128)
    to_high = hot(iota(shape, 0) == iota(shape, 1))
    to_low = hot(iota(shape, 0) + heads == iota(shape, 1))
    pair = (dot(high, to_high) + dot(low, to_low)).astype(BF16)
    placed_dt = dot(order, pair).astype(BF16)
    for s in range(n_pool):
        outs[s][:, :width] = placed[s * cr : (s + 1) * cr]
        outs[s][:, width:] = placed_dt[s * cr : (s + 1) * cr]
    ahead.wait()


def in_hbm(*arrays):
    return [pltpu.with_memory_space_constraint(v, pltpu.HBM) for v in arrays]


def project_bc(tables, hidden, w, w_dt, w_x, slots, n_pool, req, cr):
    tokens, depth = hidden.shape
    chunk = min(1024, depth)
    width, rows = w.shape[1], slots * DRAFT
    outs = pl.pallas_call(
        functools.partial(project_bc_kernel, n_pool, req, cr, chunk, slots),
        out_shape=[jax.ShapeDtypeStruct((cr, width + 128), BF16)] * n_pool
        + [
            jax.ShapeDtypeStruct((tokens, depth), BF16),
            jax.ShapeDtypeStruct((depth // HEAD_PART, w_x.shape[1]), BF16),
            jax.ShapeDtypeStruct((n_pool * cr, tokens), BF16),
            jax.ShapeDtypeStruct((rows, n_pool * cr), BF16),
            jax.ShapeDtypeStruct((tokens, rows), BF16),
            jax.ShapeDtypeStruct((n_pool * cr, tokens), BF16),
            jax.ShapeDtypeStruct((tokens, n_pool * cr), BF16),
            jax.ShapeDtypeStruct((rows, 1), F32),
        ],
        in_specs=[HBM] * 7,
        out_specs=[VMEM] * (n_pool + 8),
        scratch_shapes=[
            pltpu.VMEM((3,) + tables[0].shape, jnp.int32),
            pltpu.VMEM((depth, width), BF16),
            pltpu.VMEM(w_dt.shape, BF16),
            pltpu.SemaphoreType.DMA((4, max(4, depth // chunk))),
        ],
        compiler_params=params(12),
        cost_estimate=cost(2 * tokens * depth * width, depth * (width + 128 + tokens) * 2),
    )(*in_hbm(*tables, hidden, w, w_dt, w_x))
    return outs[:n_pool], outs[n_pool:]


def project_x_kernel(n_pool, cr, chunk, hbuf, head, w, send_ref, *refs):
    outs, (wbuf, sems) = refs[:n_pool], refs[n_pool:]
    first = head.shape[0]
    steps = (w.shape[0] - first) // chunk
    copies = dma([(w.at[pl.ds(first + k * chunk, chunk)], wbuf.at[k]) for k in range(steps)], sems, 0)
    for copy in copies:
        copy.start()
    total = dot(hbuf[:, :first], head[...])
    for k in range(steps):
        copies[k].wait()
        here = slice(first + k * chunk, first + (k + 1) * chunk)
        total = total + dot(hbuf[:, here], wbuf[k])
    placed = dot(send_ref[...], total.astype(BF16)).astype(BF16)
    for s in range(n_pool):
        outs[s][...] = placed[s * cr : (s + 1) * cr]


def project_x(hidden, head, w, send, n_pool, cr):
    tokens, depth = hidden.shape
    chunk = min(512, depth)
    width = w.shape[1]
    steps = (depth - head.shape[0]) // chunk
    return pl.pallas_call(
        functools.partial(project_x_kernel, n_pool, cr, chunk),
        out_shape=[jax.ShapeDtypeStruct((cr, width), BF16)] * n_pool,
        in_specs=[VMEM, VMEM, HBM, VMEM],
        out_specs=[VMEM] * n_pool,
        scratch_shapes=[
            pltpu.VMEM((steps, chunk, width), BF16),
            pltpu.SemaphoreType.DMA((1, steps)),
        ],
        compiler_params=params(14),
        cost_estimate=cost(2 * tokens * depth * width, depth * (width + tokens) * 2),
    )(hidden, head, *in_hbm(w), send)


def pick(rank, table):
    value = jnp.int32(table[0])
    for i in range(1, len(table)):
        value = jnp.where(rank == i, jnp.int32(table[i]), value)
    return value


def exchange_plan(n_tensor, width, span):
    piece = span * STATE
    per_group = HEADS // GROUPS
    head_local = HEADS // n_tensor
    edges, own = [], []
    for target in range(n_tensor):
        first = target * head_local // per_group
        for kind in range(2):
            column = (kind * GROUPS + first) * STATE
            source, part = column // width, column % width // piece
            (own if source == target else edges).append((source, target, kind, part))
    rounds = []
    while edges:
        best = matching(edges, n_tensor)
        rounds.append(best)
        edges = [e for e in edges if e not in best]
    return [own] + rounds


def completed(edges, n):
    pairs = [(e[0], e[1]) for e in edges]
    sources = [i for i in range(n) if i not in [p[0] for p in pairs]]
    targets = [i for i in reversed(range(n)) if i not in [p[1] for p in pairs]]
    return pairs + list(zip(sources, targets))


def matching(edges, n):
    held = {}

    def place(source, seen):
        for edge in edges:
            if edge[0] == source and edge[1] not in seen:
                seen.add(edge[1])
                if edge[1] not in held or place(held[edge[1]][0], seen):
                    held[edge[1]] = edge
                    return True
        return False

    for source in range(n):
        place(source, set())
    return [held[target] for target in sorted(held)]


def bc_kernel(n_pool, parts, owner_ref, *refs):
    got, refs = refs[:n_pool], refs[n_pool:]
    pool_ref, weight_ref, raw_ref = refs[:3]
    outs, act_ref = refs[3:-1], refs[-1]
    width = pool_ref.shape[2]
    rank = lax.axis_index("tensor").astype(jnp.int32)
    raw = dot(owner_ref[...], jnp.concatenate([g[...] for g in got], axis=0))
    raw_ref[...] = raw
    window = pool_ref.shape[1]
    summed = conv_old(pool_ref[...], weight_ref[...]) + conv_new(raw[:, :width], weight_ref[...], window)
    act_ref[...] = silu(summed).astype(BF16)
    for table, out in zip(parts, outs):
        piece = out.shape[1]
        out[...] = act_ref[:, pl.ds(pl.multiple_of(pick(rank, table) * piece, 128), piece)]


def bc_stage(owner, got, pool, weight, plan, span, n_pool, n_tensor):
    slots, _, width = pool.shape
    rows = slots * DRAFT
    piece = span * STATE
    parts = []
    for one in plan:
        table = [0] * n_tensor
        for source, _, _, part in one:
            table[source] = part
        parts.append(table)
    return pl.pallas_call(
        functools.partial(bc_kernel, n_pool, parts),
        out_shape=[jax.ShapeDtypeStruct((rows, width + 128), F32)]
        + [jax.ShapeDtypeStruct((rows, piece), BF16)] * len(plan),
        in_specs=[VMEM] * (n_pool + 3),
        out_specs=[VMEM] * (1 + len(plan)),
        scratch_shapes=[pltpu.VMEM((rows, width), BF16)],
        compiler_params=params(8),
        cost_estimate=cost(2e6, 1e6),
    )(owner, *got, pool, weight)


def pre_kernel(slots, accepts_ref, raw_ref, conv_ref, bias_ref, alog_ref, x_pool_ref, x_weight_ref, old_ref, kept_ref, m_ref, fade_ref, w_ref, d_ref):
    heads = w_ref.shape[1]
    rows = slots * DRAFT
    accepts = accepts_ref[...]
    width = raw_ref.shape[1] - 128
    shape = (128, heads)
    lane, head = iota(shape, 0), iota(shape, 1)
    both = hot((lane == head) | (lane == head + heads))
    x = dot(raw_ref[:, width:].astype(BF16), both) + bias_ref[...]
    step = jnp.maximum(x, 0.0) + jnp.log1p(jnp.exp(-jnp.abs(x)))
    logs = -step * jnp.exp(alog_ref[...])
    position = iota((rows, heads), 0) & (DRAFT - 1)
    for back in (1, 2, 4):
        logs = logs + jnp.where(position >= back, pltpu.roll(logs, back, 0), 0.0)
    last = jnp.where(position.astype(F32) + 1 == accepts, logs, 0.0).reshape(slots, DRAFT, heads)
    last = jnp.broadcast_to(jnp.sum(last, axis=1, keepdims=True), (slots, DRAFT, heads))
    d_ref[...] = jnp.exp(last[:, 0, :])
    last = last.reshape(rows, heads)
    w_ref[...] = jnp.where(position.astype(F32) < accepts, jnp.exp(jnp.minimum(last - logs, 0.0)) * step, 0.0)
    lanes = heads * DRAFT
    shape = (heads, lanes)
    repeat = jnp.where(iota(shape, 0) == (iota(shape, 1) >> SHIFT), 1.0, 0.0)

    def wide(v):
        return jnp.dot(v, repeat, preferred_element_type=F32, precision=lax.Precision.HIGHEST)

    t, u = iota((rows, lanes), 0) & (DRAFT - 1), iota((rows, lanes), 1) & (DRAFT - 1)

    def at_u(v):
        v = jnp.where(t == u, v, 0.0).reshape(slots, DRAFT, lanes)
        return jnp.broadcast_to(jnp.sum(v, axis=1, keepdims=True), (slots, DRAFT, lanes)).reshape(rows, lanes)

    wide_logs = wide(logs)
    fade = jnp.where(u <= t, jnp.exp(jnp.minimum(wide_logs - at_u(wide_logs), 0.0)) * at_u(wide(step)), 0.0)
    fade = fade.astype(BF16)
    shape = (lanes, rows)
    same = (iota(shape, 0) & (DRAFT - 1)) == (iota(shape, 1) & (DRAFT - 1))
    head = iota(shape, 0) >> SHIFT
    for h in range(heads):
        m_ref[h] = dot(fade, hot(same & (head == h))).astype(BF16)
    fade_ref[...] = spread(jnp.exp(logs), spread_matrix(heads))
    old_ref[...] = conv_old(x_pool_ref[...], x_weight_ref[...])
    kept_ref[...] = kept_rows(raw_ref[:, :width], conv_ref[...], accepts)


def pre_stage(accepts, raw, conv_pool, bias, a_log, x_pool, x_weight, pool):
    slots, heads = pool.shape[:2]
    rows = slots * DRAFT
    return pl.pallas_call(
        functools.partial(pre_kernel, slots),
        out_shape=[
            jax.ShapeDtypeStruct((rows, heads * HEAD_DIM), F32),
            jax.ShapeDtypeStruct(conv_pool.shape, BF16),
            jax.ShapeDtypeStruct((heads, rows, rows), BF16),
            jax.ShapeDtypeStruct((rows, heads * HEAD_DIM), F32),
            jax.ShapeDtypeStruct((rows, heads), F32),
            jax.ShapeDtypeStruct((slots, heads), F32),
        ],
        in_specs=[VMEM] * 7,
        out_specs=[VMEM] * 6,
        compiler_params=params(10),
        cost_estimate=cost(1e6, 1e6),
    )(accepts, raw, conv_pool, bias, a_log, x_pool, x_weight)


def mix_kernel(kinds, fade_m_ref, fade_ref, states, *refs):
    pieces, (y_ref, m_ref, b_ref, c_ref) = refs[: len(kinds)], refs[len(kinds) :]
    slots, heads = states.shape[:2]
    span = b_ref.shape[1] // STATE
    per = heads // span
    rank = lax.axis_index("tensor").astype(jnp.int32)
    for side, ref in enumerate((b_ref, c_ref)):
        ref[...] = pieces[0][...]
        for table, piece in zip(kinds, pieces):
            mine = [int(kind == side) for kind in table]
            if any(mine):

                @pl.when(pick(rank, mine) == 1)
                def _(ref=ref, piece=piece):
                    ref[...] = piece[...]

    rows = slots * DRAFT
    here = (iota((rows, rows), 0) >> SHIFT) == (iota((rows, rows), 1) >> SHIFT)
    for g in range(span):
        part = slice(g * STATE, (g + 1) * STATE)
        pair = jnp.where(here, dot_t(c_ref[:, part], b_ref[:, part]), 0.0)
        for h in range(g * per, (g + 1) * per):
            m_ref[h] = (pair * fade_m_ref[h].astype(F32)).astype(BF16)
    c = c_ref[...].astype(F32)
    for j in range(slots):
        here = slice(j * DRAFT, (j + 1) * DRAFT)
        for g in range(span):
            old = states[j, g * per : (g + 1) * per].reshape(per * HEAD_DIM, STATE)
            columns = slice(g * per * HEAD_DIM, (g + 1) * per * HEAD_DIM)
            read = dot_t(c[here, g * STATE : (g + 1) * STATE].astype(BF16), old)
            y_ref[here, columns] = read * fade_ref[here, columns]


def mix_stage(fade_m, fade, states, pieces, plan, n_tensor):
    slots, heads = states.shape[:2]
    rows = slots * DRAFT
    kinds = []
    for one in plan:
        table = [-1] * n_tensor
        for _, target, kind, _ in one:
            table[target] = kind
        kinds.append(table)
    return pl.pallas_call(
        functools.partial(mix_kernel, kinds),
        out_shape=[
            jax.ShapeDtypeStruct((rows, heads * HEAD_DIM), F32),
            jax.ShapeDtypeStruct((heads, rows, rows), BF16),
            jax.ShapeDtypeStruct(pieces[0].shape, BF16),
        ],
        in_specs=[VMEM] * (3 + len(plan)),
        out_specs=[VMEM] * 3,
        scratch_shapes=[pltpu.VMEM(pieces[0].shape, BF16)],
        compiler_params=params(8),
        cost_estimate=cost(2 * rows * heads * HEAD_DIM * STATE, 2 * states.size),
    )(fade_m, fade, states, *pieces)


def x_kernel(n_pool, owner_ref, pack_ref, *refs):
    got, refs = refs[:n_pool], refs[n_pool:]
    old_ref, weight_ref, y_ref, m_ref, skip_ref, gain_ref = refs[:6]
    normed_ref, x_ref, raw_ref = refs[6:]
    heads = old_ref.shape[1] // HEAD_DIM
    raw = dot(owner_ref[...], jnp.concatenate([g[...] for g in got], axis=0))
    raw_ref[...] = raw
    x = silu(old_ref[...] + conv_new(raw, weight_ref[...], weight_ref.shape[0] - 1))
    x_ref[...] = x
    matrix = spread_matrix(heads)
    small = x.astype(BF16)
    rows = x.shape[0]
    left = iota((rows, 2 * HEAD_DIM), 1) < HEAD_DIM
    parts = []
    for h in range(0, heads, 2):
        both = m_ref[h : h + 2].reshape(2 * rows, rows)
        both = dot(both, small[:, h * HEAD_DIM : (h + 2) * HEAD_DIM])
        parts.append(jnp.where(left, both[:rows], both[rows:]))
    y = jnp.concatenate(parts, axis=1) + y_ref[...] + spread(skip_ref[...], matrix) * x
    square = (y * y).astype(BF16)
    scale = lax.rsqrt(dot_t(square, matrix) * (1.0 / HEAD_DIM) + EPS)
    normed = (y * spread(scale, matrix) * gain_ref[...]).astype(BF16)
    normed_ref[...] = dot(pack_ref[...], normed).astype(BF16)


def x_stage(owner, pack, got, old, weight, y, m, skip, gain, n_pool):
    rows, width = old.shape
    return pl.pallas_call(
        functools.partial(x_kernel, n_pool),
        out_shape=[jax.ShapeDtypeStruct((pack.shape[0], width), BF16)] + [jax.ShapeDtypeStruct((rows, width), F32)] * 2,
        in_specs=[VMEM] * (n_pool + 8),
        out_specs=[VMEM] * 3,
        compiler_params=params(16),
        cost_estimate=cost(2 * rows * rows * width, 4e6),
    )(owner, pack, *got, old, weight, y, m, skip, gain)


def fill_states(span_of, d_ref, turned, b_ref, pool, new_pool, buf, out_sems):
    slots, heads = pool.shape[:2]
    rows = slots * DRAFT
    span = b_ref.shape[1] // STATE
    per = heads // span
    backs = [pltpu.make_async_copy(buf.at[j], new_pool.at[j], out_sems.at[j]) for j in span_of]
    b = b_ref[...].astype(F32)
    slot = iota((rows, STATE), 0) >> SHIFT
    for at in range(0, len(span_of), 2):
        pair = span_of[at : at + 2]
        for g in range(span):
            part = b[:, g * STATE : (g + 1) * STATE]
            rhs = jnp.concatenate([jnp.where(slot == j, part, 0.0) for j in pair], axis=1).astype(BF16)
            added = dot(turned[g * per * HEAD_DIM : (g + 1) * per * HEAD_DIM], rhs)
            for n, j in enumerate(pair):
                for i in range(per):
                    h = g * per + i
                    more = added[i * HEAD_DIM : (i + 1) * HEAD_DIM, n * STATE : (n + 1) * STATE]
                    buf[j, h] = (pool[j, h].astype(F32) * d_ref[j, h] + more).astype(BF16)
        for back in backs[at : at + 2]:
            back.start()
    return backs


def first_state_kernel(span_of, d_ref, x_ref, w_ref, b_ref, pool, new_pool, turned_ref, buf, out_sems):
    weighted = x_ref[...] * spread(w_ref[...], spread_matrix(pool.shape[1]))
    turned_ref[...] = weighted.T.astype(BF16)
    for copy in fill_states(span_of, d_ref, turned_ref, b_ref, pool, new_pool, buf, out_sems):
        copy.wait()


def first_state_stage(span_of, d, x, w, b, pool):
    return pl.pallas_call(
        functools.partial(first_state_kernel, span_of),
        out_shape=[jax.ShapeDtypeStruct(pool.shape, BF16), jax.ShapeDtypeStruct(x.shape[::-1], BF16)],
        in_specs=[SMEM] + [VMEM] * 4,
        out_specs=[HBM, VMEM],
        scratch_shapes=[pltpu.VMEM(pool.shape, BF16), pltpu.SemaphoreType.DMA((pool.shape[0],))],
        compiler_params=params(16),
        cost_estimate=cost(2 * pool.size * DRAFT, 2 * pool.size),
    )(d, x, w, b, pool)


def last_state_kernel(span_of, d_ref, turned_ref, b_ref, pool, accepts_ref, raw_ref, conv_ref, begun, *refs):
    del begun
    new_pool, kept_ref, buf, out_sems = refs
    backs = fill_states(span_of, d_ref, turned_ref, b_ref, pool, new_pool, buf, out_sems)
    kept_ref[...] = kept_rows(raw_ref[...], conv_ref[...], accepts_ref[...])
    for copy in backs:
        copy.wait()


def last_state_stage(span_of, d, turned, b, pool, accepts, raw, conv, begun):
    return pl.pallas_call(
        functools.partial(last_state_kernel, span_of),
        out_shape=[jax.ShapeDtypeStruct(pool.shape, BF16), jax.ShapeDtypeStruct(conv.shape, BF16)],
        in_specs=[SMEM] + [VMEM] * 6 + [HBM],
        out_specs=[HBM, VMEM],
        scratch_shapes=[pltpu.VMEM(pool.shape, BF16), pltpu.SemaphoreType.DMA((pool.shape[0],))],
        input_output_aliases={7: 0},
        compiler_params=params(16),
        cost_estimate=cost(2 * pool.size * DRAFT, 2 * pool.size),
    )(d, turned, b, pool, accepts, raw, conv, begun)


def out_kernel(wants, n_line, rows, w, *outs):
    width = outs[0].shape[1]
    rank = lax.axis_index("tensor").astype(jnp.int32)
    core, line = rank & 1, rank >> 1
    for (i, other_core), out in zip(wants, outs):
        there = line + i
        there = jnp.where(there >= n_line, there - n_line, there)
        column = pl.multiple_of((2 * there + (1 - core if other_core else core)) * width, 128)
        out[...] = dot(rows[...], w[:, pl.ds(column, width)]).astype(out.dtype)


def out_stage(rows, w, wants, n_line):
    depth, total = w.shape
    width = total // (2 * n_line)
    tokens = rows.shape[0]
    return pl.pallas_call(
        functools.partial(out_kernel, wants, n_line),
        out_shape=[jax.ShapeDtypeStruct((tokens, width), BF16 if other else F32) for _, other in wants],
        in_specs=[VMEM] * 2,
        out_specs=[VMEM] * len(wants),
        compiler_params=params(8),
        cost_estimate=cost(2 * tokens * depth * width * len(wants), 2 * depth * width * len(wants)),
    )(rows, w)


def sum_kernel(n, parts, *refs):
    for i in range(n):
        for p, part in enumerate(parts):
            refs[2 * n + p * n + i][...] = (refs[i][:, part] + refs[n + i][:, part].astype(F32)).astype(BF16)


def sum_stage(keeps, gots, parts):
    n = len(keeps)
    shape = jax.ShapeDtypeStruct((keeps[0].shape[0], parts[0].stop), BF16)
    outs = pl.pallas_call(
        functools.partial(sum_kernel, n, parts),
        out_shape=[shape] * (n * len(parts)),
        in_specs=[VMEM] * (2 * n),
        out_specs=[VMEM] * (n * len(parts)),
        compiler_params=params(8),
        cost_estimate=cost(1e6, 1e6),
    )(*keeps, *gots)
    return [outs[p * n : (p + 1) * n] for p in range(len(parts))]


def place_kernel(part, n_pool, cr, keep, core, return_ref, *refs):
    arrived, outs = refs[:-n_pool], refs[-n_pool:]
    total = keep[:, part] + core[:, part].astype(F32)
    for one in arrived:
        total = total + one[...].astype(F32)
    placed = dot(return_ref[...], total.astype(BF16)).astype(BF16)
    for s in range(n_pool):
        outs[s][...] = placed[s * cr : (s + 1) * cr]


def place_stage(part, keep, core, back, arrived, n_pool, cr):
    width = part.stop - part.start
    return pl.pallas_call(
        functools.partial(place_kernel, part, n_pool, cr),
        out_shape=[jax.ShapeDtypeStruct((cr, width), BF16)] * n_pool,
        in_specs=[VMEM] * (3 + len(arrived)),
        out_specs=[VMEM] * n_pool,
        compiler_params=params(8),
        cost_estimate=cost(1e6, 1e6),
    )(keep, core, back, *arrived)


def collect_kernel(collect_ref, parts, out):
    at = 0
    for got in parts:
        width = got[0].shape[1]
        rows = jnp.concatenate([g[...] for g in got], axis=0)
        out[:, at : at + width] = dot(collect_ref[...], rows).astype(BF16)
        at += width


def collect_stage(collect, parts):
    width = sum(got[0].shape[1] for got in parts)
    return pl.pallas_call(
        collect_kernel,
        out_shape=jax.ShapeDtypeStruct((collect.shape[0], width), BF16),
        in_specs=[VMEM, [[VMEM] * len(got) for got in parts]],
        out_specs=VMEM,
        compiler_params=params(8),
        cost_estimate=cost(1e6, 1e6),
    )(collect, parts)


def body(
    hidden,
    w_x,
    w_bc,
    w_dt,
    conv_x,
    conv_bc,
    dt_bias,
    a_log,
    d_skip,
    norm_gain,
    w_out,
    ssm_pool,
    conv_pool_x,
    conv_pool_bc,
    owners,
    slots,
    accepted,
):
    n_pool = lax.axis_size("pool")
    n_tensor = lax.axis_size("tensor")
    n_line = n_tensor // 2
    req = hidden.shape[0] // DRAFT
    share = req // n_pool
    capacity = share + share // 2
    cr = -(-capacity * DRAFT // 16) * 16
    head_local = w_dt.shape[1]
    span = max(1, head_local // (HEADS // GROUPS))

    def row(v):
        return v.reshape(1, -1)

    def over_pool(parts, home):
        moved = list(parts)
        for step in range(1, n_pool):
            pairs = [(i, partner_step(n_pool, i, step)) for i in range(n_pool)]
            pairs = [(b, a) for a, b in pairs] if home else pairs
            moved[step] = lax.ppermute(parts[step], "pool", pairs)
        return moved

    bc_sent, routes = project_bc([row(owners), row(slots), row(accepted)], hidden, w_bc, w_dt.T, w_x, ssm_pool.shape[0], n_pool, req, cr)
    hidden_kept, head, send, owner, pack, back, collect, accepts = routes
    bc_got = over_pool(bc_sent, False)
    x_sent = project_x(hidden_kept, head, w_x, send, n_pool, cr)
    x_got = over_pool(x_sent, False)
    bc_got, _ = lax.optimization_barrier((bc_got, x_sent))
    plan = exchange_plan(n_tensor, w_bc.shape[1], span)
    raw_bc, *pieces = bc_stage(owner, bc_got, conv_pool_bc, conv_bc, plan, span, n_pool, n_tensor)
    for i in range(1, len(plan)):
        pieces[i] = lax.ppermute(pieces[i], "tensor", completed(plan[i], n_tensor))
    old_x, new_conv_bc, fade_m, fade, w, d = pre_stage(
        accepts, raw_bc, conv_pool_bc, row(dt_bias), row(a_log), conv_pool_x, conv_x, ssm_pool
    )
    states, _ = lax.optimization_barrier((ssm_pool, x_sent))
    states = pltpu.with_memory_space_constraint(states, pltpu.VMEM)
    pieces, _ = lax.optimization_barrier((pieces, fade))
    y, m, b = mix_stage(fade_m, fade, states, pieces, plan, n_tensor)
    normed, x, raw_x = x_stage(owner, pack, x_got, old_x, conv_x, y, m, row(d_skip), row(norm_gain), n_pool)
    ahead = list(range(1, n_line))
    swap = [(i, i ^ 1) for i in range(n_tensor)]
    sends = out_stage(normed, w_out, [(i, True) for i in ahead], n_line)
    core_got = [lax.ppermute(v, "tensor", swap) for v in sends]
    *keeps, send_0, keep_0 = out_stage(normed, w_out, [(i, False) for i in ahead] + [(0, True), (0, False)], n_line)
    width = w_out.shape[1] // n_tensor
    parts = [slice(0, width // 2), slice(width // 2, width)]
    summed = sum_stage(keeps, core_got, parts)

    def over_line(values):
        return [
            lax.ppermute(v, "tensor", [(r, ((r // 2 + i) % n_line) * 2 + r % 2) for r in range(n_tensor)])
            for i, v in zip(ahead, values)
        ]

    arrived = [over_line(summed[0])]
    core_0 = lax.ppermute(send_0, "tensor", swap)
    half = states.shape[0] // 2
    x, _ = lax.optimization_barrier((x, summed))
    begun, turned = first_state_stage(range(half), d, x, w, b, states)
    second, _ = lax.optimization_barrier((summed[1], begun))
    arrived.append(over_line(second))
    keep_0, _ = lax.optimization_barrier((keep_0, begun))
    placed = [place_stage(part, keep_0, core_0, back, one, n_pool, cr) for part, one in zip(parts, arrived)]
    returned = [over_pool(one, True) for one in placed]
    turned, _ = lax.optimization_barrier((turned, placed[-1]))
    new_pool, new_conv_x = last_state_stage(
        range(half, states.shape[0]), d, turned, b, states, accepts, raw_x, conv_pool_x, begun
    )
    returned, _ = lax.optimization_barrier((returned, new_conv_x))
    mixed = collect_stage(collect, returned)
    return (mixed, new_pool, new_conv_x, new_conv_bc)


def solution(mesh):
    in_specs = (
        P(("groups", "pool"), None),
        P(None, "tensor"),
        P(None, "tensor"),
        P(None, "tensor"),
        P(None, "tensor"),
        P(None, "tensor"),
        P("tensor"),
        P("tensor"),
        P("tensor"),
        P("tensor"),
        P("tensor", None),
        P(("groups", "pool"), "tensor", None, None),
        P(("groups", "pool"), None, "tensor"),
        P(("groups", "pool"), None, "tensor"),
        P("groups"),
        P("groups"),
        P("groups"),
    )
    out_specs = (
        P(("groups", "pool"), "tensor"),
        P(("groups", "pool"), "tensor", None, None),
        P(("groups", "pool"), None, "tensor"),
        P(("groups", "pool"), None, "tensor"),
    )
    return jax.shard_map(body, mesh=mesh, in_specs=in_specs, out_specs=out_specs, check_vma=False)
```

```python
import functools

import jax
import jax.numpy as jnp
from jax import lax
from jax.experimental import pallas as pl
from jax.experimental.pallas import tpu as pltpu
from jax.sharding import PartitionSpec as P

HEADS = 64
HEAD_DIM = 64
STATE = 128
GROUPS = 8
DRAFT = 8
SHIFT = 3
EPS = 1e-05
FAR = 4096.0
HEAD_PART = 4

F32 = jnp.float32
BF16 = jnp.bfloat16
ANY = pl.BlockSpec(memory_space=pl.ANY)
HBM = pl.BlockSpec(memory_space=pltpu.HBM)
VMEM = pl.BlockSpec(memory_space=pltpu.VMEM)
SMEM = pl.BlockSpec(memory_space=pltpu.SMEM)


def params(mib, **more):
    return pltpu.CompilerParams(vmem_limit_bytes=mib * 2**20, **more)


def cost(flops, moved):
    return pl.CostEstimate(flops=int(flops), bytes_accessed=int(moved), transcendentals=0)


def iota(shape, dim):
    return lax.broadcasted_iota(jnp.int32, shape, dim)


def dot(a, b):
    return jnp.dot(a, b, preferred_element_type=F32)


def dot_t(a, b):
    return lax.dot_general(a, b, (((1,), (1,)), ((), ())), preferred_element_type=F32)


def as_col(row):
    n = row.shape[1]
    eye = iota((n, n), 0) == iota((n, n), 1)
    return jnp.sum(jnp.where(eye, jnp.broadcast_to(row, (n, n)), 0.0), axis=1, keepdims=True)


def partner_step(n, i, s):
    return (i + s) % n


def step_to(n, owner, requester):
    owner, requester = owner.astype(jnp.int32), requester.astype(jnp.int32)
    step = owner - requester
    return jnp.where(step < 0, step + n, step).astype(F32)


def block_shift(req):
    return req.bit_length() - 1


def ranks(orow, ocol, req):
    n = orow.shape[1]
    sub, lane = iota((n, n), 0), iota((n, n), 1)
    sh = block_shift(req)
    same = (ocol == orow) & ((sub >> sh) == (lane >> sh))
    row = jnp.sum(jnp.where(same & (sub < lane), 1.0, 0.0), axis=0, keepdims=True)
    col = jnp.sum(jnp.where(same & (lane < sub), 1.0, 0.0), axis=1, keepdims=True)
    return row, col


def hot(mask):
    return jnp.where(mask, 1.0, 0.0).astype(BF16)


def send_matrix(orow, me, n_pool, req, cr):
    ocol = as_col(orow)
    _, rank_col = ranks(orow, ocol, req)
    total, tokens = orow.shape[1], req * DRAFT
    place_col = step_to(n_pool, ocol, me) * cr + rank_col * DRAFT
    token = iota((total, tokens), 1)
    mine = (iota((total, tokens), 0) - me * req) == (token >> SHIFT)
    place = jnp.sum(jnp.where(mine, jnp.broadcast_to(place_col, (total, tokens)), 0.0), axis=0, keepdims=True)
    place = place + (iota((1, tokens), 1) & (DRAFT - 1)).astype(F32)
    return hot(iota((n_pool * cr, tokens), 0).astype(F32) == place)


def collect_matrix(orow, me, n_pool, req, cr):
    ocol = as_col(orow)
    rank_row, _ = ranks(orow, ocol, req)
    total, tokens = orow.shape[1], req * DRAFT
    place_row = step_to(n_pool, orow, me) * cr + rank_row * DRAFT
    token = iota((tokens, total), 0)
    mine = (iota((tokens, total), 1) - me * req) == (token >> SHIFT)
    place = jnp.sum(jnp.where(mine, jnp.broadcast_to(place_row, (tokens, total)), 0.0), axis=1, keepdims=True)
    place = place + (iota((tokens, 1), 0) & (DRAFT - 1)).astype(F32)
    return hot(iota((tokens, n_pool * cr), 1).astype(F32) == place)


def owner_matrix(orow, srow, me, n_pool, req, cr, slots):
    ocol = as_col(orow)
    rank_row, _ = ranks(orow, ocol, req)
    total, rows = orow.shape[1], slots * DRAFT
    block = (iota((1, total), 1) >> block_shift(req)).astype(F32)
    place_row = step_to(n_pool, me, block) * cr + rank_row * DRAFT + FAR
    slot = (iota((rows, total), 0) >> SHIFT).astype(F32)
    match = (orow == me.astype(F32)) & (srow == slot)
    place = jnp.sum(jnp.where(match, jnp.broadcast_to(place_row, (rows, total)), 0.0), axis=1, keepdims=True)
    place = place - FAR + (iota((rows, 1), 0) & (DRAFT - 1)).astype(F32)
    return hot(iota((rows, n_pool * cr), 1).astype(F32) == place)


def pack_matrices(orow, srow, me, n_pool, req, cr, slots):
    ocol, scol = as_col(orow), as_col(srow)
    _, rank_col = ranks(orow, ocol, req)
    total, rows, tokens = orow.shape[1], slots * DRAFT, req * DRAFT
    mine = me.astype(F32)
    sub, lane = iota((total, total), 0), iota((total, total), 1)
    index = jnp.sum(jnp.where((orow == mine) & (lane < sub), 1.0, 0.0), axis=1, keepdims=True)
    slot = (iota((total, rows), 1) >> SHIFT).astype(F32)
    match = (ocol == mine) & (scol == slot)
    value = jnp.broadcast_to(index * DRAFT + FAR, (total, rows))
    at = jnp.sum(jnp.where(match, value, 0.0), axis=0, keepdims=True) - FAR
    at = at + (iota((1, rows), 1) & (DRAFT - 1)).astype(F32)
    pack = hot(iota((tokens, rows), 0).astype(F32) == at)
    block = (iota((total, 1), 0) >> block_shift(req)).astype(F32)
    place_col = step_to(n_pool, me, block) * cr + rank_col * DRAFT + FAR
    match = (ocol == mine) & (index == (iota((total, tokens), 1) >> SHIFT).astype(F32))
    at = jnp.sum(jnp.where(match, jnp.broadcast_to(place_col, (total, tokens)), 0.0), axis=0, keepdims=True) - FAR
    at = at + (iota((1, tokens), 1) & (DRAFT - 1)).astype(F32)
    return pack, hot(iota((n_pool * cr, tokens), 0).astype(F32) == at)


def slot_accepts(orow, srow, arow, me, slots):
    total, rows = orow.shape[1], slots * DRAFT
    slot = (iota((rows, total), 0) >> SHIFT).astype(F32)
    match = (orow == me.astype(F32)) & (srow == slot)
    return jnp.sum(jnp.where(match, jnp.broadcast_to(arow, (rows, total)), 0.0), axis=1, keepdims=True)


def padded_pool(pool, width):
    slots, window, _ = pool.shape
    old = jnp.concatenate([pool.astype(F32), jnp.zeros((slots, DRAFT - window, width), F32)], axis=1)
    return old.reshape(slots * DRAFT, width)


def conv_old(pool, weight):
    slots, window, width = pool.shape
    rows = slots * DRAFT
    old = padded_pool(pool, width)
    position = iota((rows, width), 0) & (DRAFT - 1)
    summed = jnp.zeros((rows, width), F32)
    for back in range(1, window + 1):
        part = pltpu.roll(old, (back - window) % rows, 0)
        summed = summed + weight[window - back] * jnp.where(position < back, part, 0.0)
    return summed


def conv_new(raw, weight, window):
    position = iota(raw.shape, 0) & (DRAFT - 1)
    summed = weight[window] * raw
    for back in range(1, window + 1):
        part = pltpu.roll(raw, back, 0)
        summed = summed + weight[window - back] * jnp.where(position < back, 0.0, part)
    return summed


def kept_rows(raw, pool, accepts):
    rows, width = raw.shape
    slots, window, _ = pool.shape
    old = padded_pool(pool, width)
    sub, lane = iota((rows, rows), 0), iota((rows, rows), 1)
    here = (sub >> SHIFT) == (lane >> SHIFT)
    at = (sub & (DRAFT - 1)).astype(F32) + accepts
    source = (lane & (DRAFT - 1)).astype(F32)
    from_old = hot(here & (source == at) & (source < window))
    from_new = hot(here & (source + window == at))
    kept = dot(from_old, old.astype(BF16)) + dot(from_new, raw.astype(BF16))
    return kept.astype(BF16).reshape(slots, DRAFT, width)[:, :window]


def silu(v):
    return v / (1.0 + jnp.exp(-v))


def spread_matrix(heads):
    shape = (heads, heads * HEAD_DIM)
    return hot(iota(shape, 0) == (iota(shape, 1) >> 6))


def spread(values, matrix):
    high = values.astype(BF16)
    low = (values - high.astype(F32)).astype(BF16)
    return dot(high, matrix) + dot(low, matrix)


def dma(pairs, sems, row):
    return [pltpu.make_async_copy(src, dst, sems.at[row, k]) for k, (src, dst) in enumerate(pairs)]


def project_bc_kernel(n_pool, req, cr, chunk, slots, owners, places, takes, hidden, w, w_dt, w_x, *refs):
    outs, refs = refs[:n_pool], refs[n_pool:]
    hbuf, head, send_ref, owner_ref, pack_ref, return_ref, collect_ref, accepts_ref = refs[:8]
    meta_buf, wbuf, dt_buf, sems = refs[8:]
    steps = hidden.shape[1] // chunk
    parts = [pl.ds(k * chunk, chunk) for k in range(steps)]
    copies = list(
        zip(
            dma([(hidden.at[:, p], hbuf.at[:, p]) for p in parts], sems, 0),
            dma([(w.at[p], wbuf.at[p]) for p in parts], sems, 1),
            dma([(w_dt.at[:, p], dt_buf.at[:, p]) for p in parts], sems, 2),
        )
    )
    tables = dma([(v, meta_buf.at[i]) for i, v in enumerate((owners, places, takes))], sems, 3)
    for copy in tables:
        copy.start()
    for group in copies:
        for copy in group:
            copy.start()
    ahead = pltpu.make_async_copy(w_x.at[pl.ds(0, head.shape[0])], head, sems.at[3, len(tables)])
    ahead.start()
    for copy in tables:
        copy.wait()
    me = lax.axis_index("pool").astype(jnp.int32)
    orow, srow, arow = (meta_buf[i].astype(F32) for i in range(3))
    order = send_matrix(orow, me, n_pool, req, cr)
    send_ref[...] = order
    owner_ref[...] = owner_matrix(orow, srow, me, n_pool, req, cr, slots)
    pack_ref[...], return_ref[...] = pack_matrices(orow, srow, me, n_pool, req, cr, slots)
    collect_ref[...] = collect_matrix(orow, me, n_pool, req, cr)
    accepts_ref[...] = slot_accepts(orow, srow, arow, me, slots)
    heads = w_dt.shape[0]
    total, total_dt = None, None
    for k in range(steps):
        for copy in copies[k]:
            copy.wait()
        here = slice(k * chunk, (k + 1) * chunk)
        added, added_dt = dot(hbuf[:, here], wbuf[here]), dot_t(hbuf[:, here], dt_buf[:, here])
        total = added if total is None else total + added
        total_dt = added_dt if total_dt is None else total_dt + added_dt
    width = w.shape[1]
    placed = dot(order, total.astype(BF16)).astype(BF16)
    high = total_dt.astype(BF16)
    low = (total_dt - high.astype(F32)).astype(BF16)
    shape = (heads, 128)
    to_high = hot(iota(shape, 0) == iota(shape, 1))
    to_low = hot(iota(shape, 0) + heads == iota(shape, 1))
    pair = (dot(high, to_high) + dot(low, to_low)).astype(BF16)
    placed_dt = dot(order, pair).astype(BF16)
    for s in range(n_pool):
        outs[s][:, :width] = placed[s * cr : (s + 1) * cr]
        outs[s][:, width:] = placed_dt[s * cr : (s + 1) * cr]
    ahead.wait()


def in_hbm(*arrays):
    return [pltpu.with_memory_space_constraint(v, pltpu.HBM) for v in arrays]


def project_bc(tables, hidden, w, w_dt, w_x, slots, n_pool, req, cr):
    tokens, depth = hidden.shape
    chunk = min(1024, depth)
    width, rows = w.shape[1], slots * DRAFT
    outs = pl.pallas_call(
        functools.partial(project_bc_kernel, n_pool, req, cr, chunk, slots),
        out_shape=[jax.ShapeDtypeStruct((cr, width + 128), BF16)] * n_pool
        + [
            jax.ShapeDtypeStruct((tokens, depth), BF16),
            jax.ShapeDtypeStruct((depth // HEAD_PART, w_x.shape[1]), BF16),
            jax.ShapeDtypeStruct((n_pool * cr, tokens), BF16),
            jax.ShapeDtypeStruct((rows, n_pool * cr), BF16),
            jax.ShapeDtypeStruct((tokens, rows), BF16),
            jax.ShapeDtypeStruct((n_pool * cr, tokens), BF16),
            jax.ShapeDtypeStruct((tokens, n_pool * cr), BF16),
            jax.ShapeDtypeStruct((rows, 1), F32),
        ],
        in_specs=[HBM] * 7,
        out_specs=[VMEM] * (n_pool + 8),
        scratch_shapes=[
            pltpu.VMEM((3,) + tables[0].shape, jnp.int32),
            pltpu.VMEM((depth, width), BF16),
            pltpu.VMEM(w_dt.shape, BF16),
            pltpu.SemaphoreType.DMA((4, max(4, depth // chunk))),
        ],
        compiler_params=params(12),
        cost_estimate=cost(2 * tokens * depth * width, depth * (width + 128 + tokens) * 2),
    )(*in_hbm(*tables, hidden, w, w_dt, w_x))
    return outs[:n_pool], outs[n_pool:]


def project_x_kernel(n_pool, cr, chunk, hbuf, head, w, send_ref, *refs):
    outs, (wbuf, sems) = refs[:n_pool], refs[n_pool:]
    first = head.shape[0]
    steps = (w.shape[0] - first) // chunk
    copies = dma([(w.at[pl.ds(first + k * chunk, chunk)], wbuf.at[k]) for k in range(steps)], sems, 0)
    for copy in copies:
        copy.start()
    total = dot(hbuf[:, :first], head[...])
    for k in range(steps):
        copies[k].wait()
        here = slice(first + k * chunk, first + (k + 1) * chunk)
        total = total + dot(hbuf[:, here], wbuf[k])
    placed = dot(send_ref[...], total.astype(BF16)).astype(BF16)
    for s in range(n_pool):
        outs[s][...] = placed[s * cr : (s + 1) * cr]


def project_x(hidden, head, w, send, n_pool, cr):
    tokens, depth = hidden.shape
    chunk = min(512, depth)
    width = w.shape[1]
    steps = (depth - head.shape[0]) // chunk
    return pl.pallas_call(
        functools.partial(project_x_kernel, n_pool, cr, chunk),
        out_shape=[jax.ShapeDtypeStruct((cr, width), BF16)] * n_pool,
        in_specs=[VMEM, VMEM, HBM, VMEM],
        out_specs=[VMEM] * n_pool,
        scratch_shapes=[
            pltpu.VMEM((steps, chunk, width), BF16),
            pltpu.SemaphoreType.DMA((1, steps)),
        ],
        compiler_params=params(14),
        cost_estimate=cost(2 * tokens * depth * width, depth * (width + tokens) * 2),
    )(hidden, head, *in_hbm(w), send)


def pick(rank, table):
    value = jnp.int32(table[0])
    for i in range(1, len(table)):
        value = jnp.where(rank == i, jnp.int32(table[i]), value)
    return value


def exchange_plan(n_tensor, width, span):
    piece = span * STATE
    per_group = HEADS // GROUPS
    head_local = HEADS // n_tensor
    edges, own = [], []
    for target in range(n_tensor):
        first = target * head_local // per_group
        for kind in range(2):
            column = (kind * GROUPS + first) * STATE
            source, part = column // width, column % width // piece
            (own if source == target else edges).append((source, target, kind, part))
    rounds = []
    while edges:
        best = matching(edges, n_tensor)
        rounds.append(best)
        edges = [e for e in edges if e not in best]
    return [own] + rounds


def completed(edges, n):
    pairs = [(e[0], e[1]) for e in edges]
    sources = [i for i in range(n) if i not in [p[0] for p in pairs]]
    targets = [i for i in reversed(range(n)) if i not in [p[1] for p in pairs]]
    return pairs + list(zip(sources, targets))


def matching(edges, n):
    held = {}

    def place(source, seen):
        for edge in edges:
            if edge[0] == source and edge[1] not in seen:
                seen.add(edge[1])
                if edge[1] not in held or place(held[edge[1]][0], seen):
                    held[edge[1]] = edge
                    return True
        return False

    for source in range(n):
        place(source, set())
    return [held[target] for target in sorted(held)]


def bc_kernel(n_pool, parts, owner_ref, *refs):
    got, refs = refs[:n_pool], refs[n_pool:]
    pool_ref, weight_ref, raw_ref = refs[:3]
    outs, act_ref = refs[3:-1], refs[-1]
    width = pool_ref.shape[2]
    rank = lax.axis_index("tensor").astype(jnp.int32)
    raw = dot(owner_ref[...], jnp.concatenate([g[...] for g in got], axis=0))
    raw_ref[...] = raw
    window = pool_ref.shape[1]
    summed = conv_old(pool_ref[...], weight_ref[...]) + conv_new(raw[:, :width], weight_ref[...], window)
    act_ref[...] = silu(summed).astype(BF16)
    for table, out in zip(parts, outs):
        piece = out.shape[1]
        out[...] = act_ref[:, pl.ds(pl.multiple_of(pick(rank, table) * piece, 128), piece)]


def bc_stage(owner, got, pool, weight, plan, span, n_pool, n_tensor):
    slots, _, width = pool.shape
    rows = slots * DRAFT
    piece = span * STATE
    parts = []
    for one in plan:
        table = [0] * n_tensor
        for source, _, _, part in one:
            table[source] = part
        parts.append(table)
    return pl.pallas_call(
        functools.partial(bc_kernel, n_pool, parts),
        out_shape=[jax.ShapeDtypeStruct((rows, width + 128), F32)]
        + [jax.ShapeDtypeStruct((rows, piece), BF16)] * len(plan),
        in_specs=[VMEM] * (n_pool + 3),
        out_specs=[VMEM] * (1 + len(plan)),
        scratch_shapes=[pltpu.VMEM((rows, width), BF16)],
        compiler_params=params(8),
        cost_estimate=cost(2e6, 1e6),
    )(owner, *got, pool, weight)


def pre_kernel(slots, accepts_ref, raw_ref, conv_ref, bias_ref, alog_ref, x_pool_ref, x_weight_ref, old_ref, kept_ref, m_ref, fade_ref, w_ref, d_ref):
    heads = w_ref.shape[1]
    rows = slots * DRAFT
    accepts = accepts_ref[...]
    width = raw_ref.shape[1] - 128
    shape = (128, heads)
    lane, head = iota(shape, 0), iota(shape, 1)
    both = hot((lane == head) | (lane == head + heads))
    x = dot(raw_ref[:, width:].astype(BF16), both) + bias_ref[...]
    step = jnp.maximum(x, 0.0) + jnp.log1p(jnp.exp(-jnp.abs(x)))
    logs = -step * jnp.exp(alog_ref[...])
    position = iota((rows, heads), 0) & (DRAFT - 1)
    for back in (1, 2, 4):
        logs = logs + jnp.where(position >= back, pltpu.roll(logs, back, 0), 0.0)
    last = jnp.where(position.astype(F32) + 1 == accepts, logs, 0.0).reshape(slots, DRAFT, heads)
    last = jnp.broadcast_to(jnp.sum(last, axis=1, keepdims=True), (slots, DRAFT, heads))
    d_ref[...] = jnp.exp(last[:, 0, :])
    last = last.reshape(rows, heads)
    w_ref[...] = jnp.where(position.astype(F32) < accepts, jnp.exp(jnp.minimum(last - logs, 0.0)) * step, 0.0)
    lanes = heads * DRAFT
    shape = (heads, lanes)
    repeat = jnp.where(iota(shape, 0) == (iota(shape, 1) >> SHIFT), 1.0, 0.0)

    def wide(v):
        return jnp.dot(v, repeat, preferred_element_type=F32, precision=lax.Precision.HIGHEST)

    t, u = iota((rows, lanes), 0) & (DRAFT - 1), iota((rows, lanes), 1) & (DRAFT - 1)

    def at_u(v):
        v = jnp.where(t == u, v, 0.0).reshape(slots, DRAFT, lanes)
        return jnp.broadcast_to(jnp.sum(v, axis=1, keepdims=True), (slots, DRAFT, lanes)).reshape(rows, lanes)

    wide_logs = wide(logs)
    fade = jnp.where(u <= t, jnp.exp(jnp.minimum(wide_logs - at_u(wide_logs), 0.0)) * at_u(wide(step)), 0.0)
    fade = fade.astype(BF16)
    shape = (lanes, rows)
    same = (iota(shape, 0) & (DRAFT - 1)) == (iota(shape, 1) & (DRAFT - 1))
    head = iota(shape, 0) >> SHIFT
    for h in range(heads):
        m_ref[h] = dot(fade, hot(same & (head == h))).astype(BF16)
    fade_ref[...] = spread(jnp.exp(logs), spread_matrix(heads))
    old_ref[...] = conv_old(x_pool_ref[...], x_weight_ref[...])
    kept_ref[...] = kept_rows(raw_ref[:, :width], conv_ref[...], accepts)


def pre_stage(accepts, raw, conv_pool, bias, a_log, x_pool, x_weight, pool):
    slots, heads = pool.shape[:2]
    rows = slots * DRAFT
    return pl.pallas_call(
        functools.partial(pre_kernel, slots),
        out_shape=[
            jax.ShapeDtypeStruct((rows, heads * HEAD_DIM), F32),
            jax.ShapeDtypeStruct(conv_pool.shape, BF16),
            jax.ShapeDtypeStruct((heads, rows, rows), BF16),
            jax.ShapeDtypeStruct((rows, heads * HEAD_DIM), F32),
            jax.ShapeDtypeStruct((rows, heads), F32),
            jax.ShapeDtypeStruct((slots, heads), F32),
        ],
        in_specs=[VMEM] * 7,
        out_specs=[VMEM] * 6,
        compiler_params=params(10),
        cost_estimate=cost(1e6, 1e6),
    )(accepts, raw, conv_pool, bias, a_log, x_pool, x_weight)


def mix_kernel(kinds, fade_m_ref, fade_ref, states, *refs):
    pieces, (y_ref, m_ref, b_ref, c_ref) = refs[: len(kinds)], refs[len(kinds) :]
    slots, heads = states.shape[:2]
    span = b_ref.shape[1] // STATE
    per = heads // span
    rank = lax.axis_index("tensor").astype(jnp.int32)
    for side, ref in enumerate((b_ref, c_ref)):
        ref[...] = pieces[0][...]
        for table, piece in zip(kinds, pieces):
            mine = [int(kind == side) for kind in table]
            if any(mine):

                @pl.when(pick(rank, mine) == 1)
                def _(ref=ref, piece=piece):
                    ref[...] = piece[...]

    rows = slots * DRAFT
    here = (iota((rows, rows), 0) >> SHIFT) == (iota((rows, rows), 1) >> SHIFT)
    for g in range(span):
        part = slice(g * STATE, (g + 1) * STATE)
        pair = jnp.where(here, dot_t(c_ref[:, part], b_ref[:, part]), 0.0)
        for h in range(g * per, (g + 1) * per):
            m_ref[h] = (pair * fade_m_ref[h].astype(F32)).astype(BF16)
    c = c_ref[...].astype(F32)
    for j in range(slots):
        here = slice(j * DRAFT, (j + 1) * DRAFT)
        for g in range(span):
            old = states[j, g * per : (g + 1) * per].reshape(per * HEAD_DIM, STATE)
            columns = slice(g * per * HEAD_DIM, (g + 1) * per * HEAD_DIM)
            read = dot_t(c[here, g * STATE : (g + 1) * STATE].astype(BF16), old)
            y_ref[here, columns] = read * fade_ref[here, columns]


def mix_stage(fade_m, fade, states, pieces, plan, n_tensor):
    slots, heads = states.shape[:2]
    rows = slots * DRAFT
    kinds = []
    for one in plan:
        table = [-1] * n_tensor
        for _, target, kind, _ in one:
            table[target] = kind
        kinds.append(table)
    return pl.pallas_call(
        functools.partial(mix_kernel, kinds),
        out_shape=[
            jax.ShapeDtypeStruct((rows, heads * HEAD_DIM), F32),
            jax.ShapeDtypeStruct((heads, rows, rows), BF16),
            jax.ShapeDtypeStruct(pieces[0].shape, BF16),
        ],
        in_specs=[VMEM] * (3 + len(plan)),
        out_specs=[VMEM] * 3,
        scratch_shapes=[pltpu.VMEM(pieces[0].shape, BF16)],
        compiler_params=params(8),
        cost_estimate=cost(2 * rows * heads * HEAD_DIM * STATE, 2 * states.size),
    )(fade_m, fade, states, *pieces)


def x_kernel(n_pool, owner_ref, pack_ref, *refs):
    got, refs = refs[:n_pool], refs[n_pool:]
    old_ref, weight_ref, y_ref, m_ref, skip_ref, gain_ref = refs[:6]
    normed_ref, x_ref, raw_ref = refs[6:]
    heads = old_ref.shape[1] // HEAD_DIM
    raw = dot(owner_ref[...], jnp.concatenate([g[...] for g in got], axis=0))
    raw_ref[...] = raw
    x = silu(old_ref[...] + conv_new(raw, weight_ref[...], weight_ref.shape[0] - 1))
    x_ref[...] = x
    matrix = spread_matrix(heads)
    small = x.astype(BF16)
    rows = x.shape[0]
    left = iota((rows, 2 * HEAD_DIM), 1) < HEAD_DIM
    parts = []
    for h in range(0, heads, 2):
        both = m_ref[h : h + 2].reshape(2 * rows, rows)
        both = dot(both, small[:, h * HEAD_DIM : (h + 2) * HEAD_DIM])
        parts.append(jnp.where(left, both[:rows], both[rows:]))
    y = jnp.concatenate(parts, axis=1) + y_ref[...] + spread(skip_ref[...], matrix) * x
    square = (y * y).astype(BF16)
    scale = lax.rsqrt(dot_t(square, matrix) * (1.0 / HEAD_DIM) + EPS)
    normed = (y * spread(scale, matrix) * gain_ref[...]).astype(BF16)
    normed_ref[...] = dot(pack_ref[...], normed).astype(BF16)


def x_stage(owner, pack, got, old, weight, y, m, skip, gain, n_pool):
    rows, width = old.shape
    return pl.pallas_call(
        functools.partial(x_kernel, n_pool),
        out_shape=[jax.ShapeDtypeStruct((pack.shape[0], width), BF16)] + [jax.ShapeDtypeStruct((rows, width), F32)] * 2,
        in_specs=[VMEM] * (n_pool + 8),
        out_specs=[VMEM] * 3,
        compiler_params=params(16),
        cost_estimate=cost(2 * rows * rows * width, 4e6),
    )(owner, pack, *got, old, weight, y, m, skip, gain)


def fill_states(span_of, d_ref, turned, b_ref, pool, new_pool, buf, out_sems):
    slots, heads = pool.shape[:2]
    rows = slots * DRAFT
    span = b_ref.shape[1] // STATE
    per = heads // span
    backs = [pltpu.make_async_copy(buf.at[j], new_pool.at[j], out_sems.at[j]) for j in span_of]
    b = b_ref[...].astype(F32)
    slot = iota((rows, STATE), 0) >> SHIFT
    for at in range(0, len(span_of), 2):
        pair = span_of[at : at + 2]
        for g in range(span):
            part = b[:, g * STATE : (g + 1) * STATE]
            rhs = jnp.concatenate([jnp.where(slot == j, part, 0.0) for j in pair], axis=1).astype(BF16)
            added = dot(turned[g * per * HEAD_DIM : (g + 1) * per * HEAD_DIM], rhs)
            for n, j in enumerate(pair):
                for i in range(per):
                    h = g * per + i
                    more = added[i * HEAD_DIM : (i + 1) * HEAD_DIM, n * STATE : (n + 1) * STATE]
                    buf[j, h] = (pool[j, h].astype(F32) * d_ref[j, h] + more).astype(BF16)
        for back in backs[at : at + 2]:
            back.start()
    return backs


def first_state_kernel(span_of, d_ref, x_ref, w_ref, b_ref, pool, new_pool, turned_ref, buf, out_sems):
    weighted = x_ref[...] * spread(w_ref[...], spread_matrix(pool.shape[1]))
    turned_ref[...] = weighted.T.astype(BF16)
    for copy in fill_states(span_of, d_ref, turned_ref, b_ref, pool, new_pool, buf, out_sems):
        copy.wait()


def first_state_stage(span_of, d, x, w, b, pool):
    return pl.pallas_call(
        functools.partial(first_state_kernel, span_of),
        out_shape=[jax.ShapeDtypeStruct(pool.shape, BF16), jax.ShapeDtypeStruct(x.shape[::-1], BF16)],
        in_specs=[SMEM] + [VMEM] * 4,
        out_specs=[HBM, VMEM],
        scratch_shapes=[pltpu.VMEM(pool.shape, BF16), pltpu.SemaphoreType.DMA((pool.shape[0],))],
        compiler_params=params(16),
        cost_estimate=cost(2 * pool.size * DRAFT, 2 * pool.size),
    )(d, x, w, b, pool)


def last_state_kernel(span_of, d_ref, turned_ref, b_ref, pool, accepts_ref, raw_ref, conv_ref, begun, *refs):
    del begun
    new_pool, kept_ref, buf, out_sems = refs
    backs = fill_states(span_of, d_ref, turned_ref, b_ref, pool, new_pool, buf, out_sems)
    kept_ref[...] = kept_rows(raw_ref[...], conv_ref[...], accepts_ref[...])
    for copy in backs:
        copy.wait()


def last_state_stage(span_of, d, turned, b, pool, accepts, raw, conv, begun):
    return pl.pallas_call(
        functools.partial(last_state_kernel, span_of),
        out_shape=[jax.ShapeDtypeStruct(pool.shape, BF16), jax.ShapeDtypeStruct(conv.shape, BF16)],
        in_specs=[SMEM] + [VMEM] * 6 + [HBM],
        out_specs=[HBM, VMEM],
        scratch_shapes=[pltpu.VMEM(pool.shape, BF16), pltpu.SemaphoreType.DMA((pool.shape[0],))],
        input_output_aliases={7: 0},
        compiler_params=params(16),
        cost_estimate=cost(2 * pool.size * DRAFT, 2 * pool.size),
    )(d, turned, b, pool, accepts, raw, conv, begun)


def out_kernel(wants, n_line, rows, w, *outs):
    width = outs[0].shape[1]
    rank = lax.axis_index("tensor").astype(jnp.int32)
    core, line = rank & 1, rank >> 1
    for (i, other_core), out in zip(wants, outs):
        there = line + i
        there = jnp.where(there >= n_line, there - n_line, there)
        column = pl.multiple_of((2 * there + (1 - core if other_core else core)) * width, 128)
        out[...] = dot(rows[...], w[:, pl.ds(column, width)]).astype(out.dtype)


def out_stage(rows, w, wants, n_line):
    depth, total = w.shape
    width = total // (2 * n_line)
    tokens = rows.shape[0]
    return pl.pallas_call(
        functools.partial(out_kernel, wants, n_line),
        out_shape=[jax.ShapeDtypeStruct((tokens, width), BF16 if other else F32) for _, other in wants],
        in_specs=[VMEM] * 2,
        out_specs=[VMEM] * len(wants),
        compiler_params=params(8),
        cost_estimate=cost(2 * tokens * depth * width * len(wants), 2 * depth * width * len(wants)),
    )(rows, w)


def sum_kernel(n, parts, *refs):
    for i in range(n):
        for p, part in enumerate(parts):
            refs[2 * n + p * n + i][...] = (refs[i][:, part] + refs[n + i][:, part].astype(F32)).astype(BF16)


def sum_stage(keeps, gots, parts):
    n = len(keeps)
    shape = jax.ShapeDtypeStruct((keeps[0].shape[0], parts[0].stop), BF16)
    outs = pl.pallas_call(
        functools.partial(sum_kernel, n, parts),
        out_shape=[shape] * (n * len(parts)),
        in_specs=[VMEM] * (2 * n),
        out_specs=[VMEM] * (n * len(parts)),
        compiler_params=params(8),
        cost_estimate=cost(1e6, 1e6),
    )(*keeps, *gots)
    return [outs[p * n : (p + 1) * n] for p in range(len(parts))]


def place_kernel(part, n_pool, cr, keep, core, return_ref, *refs):
    arrived, outs = refs[:-n_pool], refs[-n_pool:]
    total = keep[:, part] + core[:, part].astype(F32)
    for one in arrived:
        total = total + one[...].astype(F32)
    placed = dot(return_ref[...], total.astype(BF16)).astype(BF16)
    for s in range(n_pool):
        outs[s][...] = placed[s * cr : (s + 1) * cr]


def place_stage(part, keep, core, back, arrived, n_pool, cr):
    width = part.stop - part.start
    return pl.pallas_call(
        functools.partial(place_kernel, part, n_pool, cr),
        out_shape=[jax.ShapeDtypeStruct((cr, width), BF16)] * n_pool,
        in_specs=[VMEM] * (3 + len(arrived)),
        out_specs=[VMEM] * n_pool,
        compiler_params=params(8),
        cost_estimate=cost(1e6, 1e6),
    )(keep, core, back, *arrived)


def collect_kernel(collect_ref, parts, out, buf, sems):
    at, copies = 0, []
    for k, got in enumerate(parts):
        width = got[0].shape[1]
        rows = jnp.concatenate([g[...] for g in got], axis=0)
        buf[:, at : at + width] = dot(collect_ref[...], rows).astype(BF16)
        here = pl.ds(at, width)
        copies.append(pltpu.make_async_copy(buf.at[:, here], out.at[:, here], sems.at[k]))
        copies[-1].start()
        at += width
    for copy in copies:
        copy.wait()


def collect_stage(collect, parts):
    width = sum(got[0].shape[1] for got in parts)
    shape = (collect.shape[0], width)
    return pl.pallas_call(
        collect_kernel,
        out_shape=jax.ShapeDtypeStruct(shape, BF16),
        in_specs=[VMEM, [[VMEM] * len(got) for got in parts]],
        out_specs=HBM,
        scratch_shapes=[pltpu.VMEM(shape, BF16), pltpu.SemaphoreType.DMA((len(parts),))],
        compiler_params=params(8),
        cost_estimate=cost(1e6, 1e6),
    )(collect, parts)


def body(
    hidden,
    w_x,
    w_bc,
    w_dt,
    conv_x,
    conv_bc,
    dt_bias,
    a_log,
    d_skip,
    norm_gain,
    w_out,
    ssm_pool,
    conv_pool_x,
    conv_pool_bc,
    owners,
    slots,
    accepted,
):
    n_pool = lax.axis_size("pool")
    n_tensor = lax.axis_size("tensor")
    n_line = n_tensor // 2
    req = hidden.shape[0] // DRAFT
    share = req // n_pool
    capacity = share + share // 2
    cr = -(-capacity * DRAFT // 16) * 16
    head_local = w_dt.shape[1]
    span = max(1, head_local // (HEADS // GROUPS))

    def row(v):
        return v.reshape(1, -1)

    def over_pool(parts, home):
        moved = list(parts)
        for step in range(1, n_pool):
            pairs = [(i, partner_step(n_pool, i, step)) for i in range(n_pool)]
            pairs = [(b, a) for a, b in pairs] if home else pairs
            moved[step] = lax.ppermute(parts[step], "pool", pairs)
        return moved

    bc_sent, routes = project_bc([row(owners), row(slots), row(accepted)], hidden, w_bc, w_dt.T, w_x, ssm_pool.shape[0], n_pool, req, cr)
    hidden_kept, head, send, owner, pack, back, collect, accepts = routes
    bc_got = over_pool(bc_sent, False)
    x_sent = project_x(hidden_kept, head, w_x, send, n_pool, cr)
    x_got = over_pool(x_sent, False)
    bc_got, _ = lax.optimization_barrier((bc_got, x_sent))
    plan = exchange_plan(n_tensor, w_bc.shape[1], span)
    raw_bc, *pieces = bc_stage(owner, bc_got, conv_pool_bc, conv_bc, plan, span, n_pool, n_tensor)
    for i in range(1, len(plan)):
        pieces[i] = lax.ppermute(pieces[i], "tensor", completed(plan[i], n_tensor))
    old_x, new_conv_bc, fade_m, fade, w, d = pre_stage(
        accepts, raw_bc, conv_pool_bc, row(dt_bias), row(a_log), conv_pool_x, conv_x, ssm_pool
    )
    states, _ = lax.optimization_barrier((ssm_pool, x_sent))
    states = pltpu.with_memory_space_constraint(states, pltpu.VMEM)
    pieces, _ = lax.optimization_barrier((pieces, fade))
    y, m, b = mix_stage(fade_m, fade, states, pieces, plan, n_tensor)
    normed, x, raw_x = x_stage(owner, pack, x_got, old_x, conv_x, y, m, row(d_skip), row(norm_gain), n_pool)
    ahead = list(range(1, n_line))
    swap = [(i, i ^ 1) for i in range(n_tensor)]
    sends = out_stage(normed, w_out, [(i, True) for i in ahead], n_line)
    core_got = [lax.ppermute(v, "tensor", swap) for v in sends]
    *keeps, send_0, keep_0 = out_stage(normed, w_out, [(i, False) for i in ahead] + [(0, True), (0, False)], n_line)
    width = w_out.shape[1] // n_tensor
    parts = [slice(0, width // 2), slice(width // 2, width)]
    summed = sum_stage(keeps, core_got, parts)

    def over_line(values):
        return [
            lax.ppermute(v, "tensor", [(r, ((r // 2 + i) % n_line) * 2 + r % 2) for r in range(n_tensor)])
            for i, v in zip(ahead, values)
        ]

    arrived = [over_line(summed[0])]
    core_0 = lax.ppermute(send_0, "tensor", swap)
    half = states.shape[0] // 2
    x, _ = lax.optimization_barrier((x, summed))
    begun, turned = first_state_stage(range(half), d, x, w, b, states)
    second, _ = lax.optimization_barrier((summed[1], begun))
    arrived.append(over_line(second))
    keep_0, _ = lax.optimization_barrier((keep_0, begun))
    placed = [place_stage(part, keep_0, core_0, back, one, n_pool, cr) for part, one in zip(parts, arrived)]
    returned = [over_pool(one, True) for one in placed]
    turned, _ = lax.optimization_barrier((turned, placed[-1]))
    new_pool, new_conv_x = last_state_stage(
        range(half, states.shape[0]), d, turned, b, states, accepts, raw_x, conv_pool_x, begun
    )
    returned, _ = lax.optimization_barrier((returned, new_conv_x))
    mixed = collect_stage(collect, returned)
    return (mixed, new_pool, new_conv_x, new_conv_bc)


def solution(mesh):
    in_specs = (
        P(("groups", "pool"), None),
        P(None, "tensor"),
        P(None, "tensor"),
        P(None, "tensor"),
        P(None, "tensor"),
        P(None, "tensor"),
        P("tensor"),
        P("tensor"),
        P("tensor"),
        P("tensor"),
        P("tensor", None),
        P(("groups", "pool"), "tensor", None, None),
        P(("groups", "pool"), None, "tensor"),
        P(("groups", "pool"), None, "tensor"),
        P("groups"),
        P("groups"),
        P("groups"),
    )
    out_specs = (
        P(("groups", "pool"), "tensor"),
        P(("groups", "pool"), "tensor", None, None),
        P(("groups", "pool"), None, "tensor"),
        P(("groups", "pool"), None, "tensor"),
    )
    return jax.shard_map(body, mesh=mesh, in_specs=in_specs, out_specs=out_specs, check_vma=False)
```
